32 devices in a mesh: group: 4 (over x, core), fsdp: 4 (over z), tp: 2 (over y).
Axes of the slice: x: 2, y: 2, z: 4, core: 2. Of those that a mesh axis runs over, the one named last changes fastest.
Arguments:
- tokens: bfloat16 [128, 4, 5120], P(('group', 'fsdp')), may hold values from -6 to 6
- queries: bfloat16 [128, 4, 5120], P(('group', 'fsdp'), None, 'tp'), may hold values from -6 to 6
- cache_keys: bfloat16 [128, 512, 1024], P(('group', 'fsdp'), None, 'tp'), may hold values from -6 to 6
- cache_values: bfloat16 [128, 512, 1024], P(('group', 'fsdp'), None, 'tp'), may hold values from -6 to 6
- lengths: int32 [128], P(('group', 'fsdp')), may hold values from 16 to 512, as said below
- weights: float32 [5120, 2048], P(('fsdp', 'tp')), may hold values from -0.078125 to 0.078125
- moment1: float32 [5120, 2048], P(('fsdp', 'tp')), may hold values from -3 to 3
- moment2: float32 [5120, 2048], P(('fsdp', 'tp')), may hold values from 0.25 to 4
- grad_parts: float32 [4, 5120, 2048], P('group', ('fsdp', 'tp')), may hold values from -2 to 2
Outputs:
- new_weights: float32 [5120, 2048], P(('fsdp', 'tp'))
- new_moment1: float32 [5120, 2048], P(('fsdp', 'tp'))
- new_moment2: float32 [5120, 2048], P(('fsdp', 'tp'))
- new_kv: bfloat16 [128, 4, 2048], P(('group', 'fsdp'), None, 'tp')
- context: bfloat16 [128, 4, 5120], P(('group', 'fsdp'), None, 'tp')
The draws below stay inside these ranges and needn't reach their ends.
Inputs may be any that keep to these rules, and one draw needn't show every extreme that they name: Row r's cache holds lengths[r] valid slots; some row holds 512.
All inputs are finite; a program needn't handle non-finite values.
Results may differ from the reference program's by a relative error of at most 0.0065.
Values may be sent and summed in bfloat16 or wider, within the bound.
No kernel may reach another device: no remote copies, remote signals or barrier semaphores. Data moves between devices by JAX's collectives and lax.ppermute only.
A program may use at most 128 MiB of HBM per device.

```python
import math
import jax
import jax.numpy as jnp
from jax import lax

D = 5120
QH = 40
KVH = 8
HD = 128
STEPS = 4
R_DEV = 8
LMAX = 512
ROWS = 128
KVW = 2048
N_GROUP = 4


def draw_queries(key, part):
    sample = jax.random.truncated_normal(jax.random.fold_in(key, 11), -6.0, 6.0, (ROWS, STEPS, QH, HD), jnp.float32)
    return sample.reshape(ROWS, STEPS, QH * HD).astype(jnp.bfloat16)


def draw_cache_keys(key, part):
    sample = jax.random.truncated_normal(jax.random.fold_in(key, 13), -6.0, 6.0, (ROWS, LMAX, KVH, HD), jnp.float32)
    return sample.reshape(ROWS, LMAX, KVH * HD).astype(jnp.bfloat16)


def draw_lengths(key, part):
    blocks = ROWS // R_DEV
    device_caps = jax.random.randint(jax.random.fold_in(key, 21), (blocks,), LMAX // 4, LMAX + 1)
    cap_rows = jnp.repeat(device_caps, R_DEV)
    raw_draw = jax.random.randint(jax.random.fold_in(key, 22), (ROWS,), 0, 1 << 20)
    row_lengths = raw_draw % (cap_rows - 15) + 16
    return row_lengths.at[0].set(LMAX).astype(jnp.int32)


def level_of(stream_key, dims, cuts, low, largest):
    def one(axis_at, parts):
        draws = jax.random.uniform(jax.random.fold_in(jax.random.fold_in(stream_key, 6), axis_at), (parts,), jnp.float32, low / len(cuts), largest / len(cuts))
        return jnp.repeat(jnp.exp(draws), dims[axis_at] // parts).reshape((-1,) + (1,) * (len(dims) - axis_at - 1))

    loudness = one(*cuts[0])
    for cut in cuts[1:]:
        loudness = loudness * one(*cut)
    return loudness


def gaussian(own_key, dims, spread, bound, shards=(), kind=jnp.bfloat16):
    entries = jax.random.normal(own_key, dims, jnp.float32) * spread
    if len(shards) > 0:
        entries = level_of(own_key, dims, shards, -0.22, 0.18) * entries
    return jnp.clip(entries, min=-bound, max=bound).astype(kind)


def setup_inputs(seed: int = 0) -> dict:
    key_of = jax.random.split(jax.random.key(seed), 10)
    tokens = gaussian(key_of[0], (ROWS, STEPS, D), 1.0, 6.0, ((0, 16),))
    queries = draw_queries(jax.random.fold_in(key_of[9], 71), 0)
    cache_keys = draw_cache_keys(jax.random.fold_in(key_of[9], 71), 0)
    cache_values = gaussian(key_of[3], (ROWS, LMAX, KVH * HD), 1.0, 6.0, ((0, 16), (2, 2)))
    lengths = draw_lengths(jax.random.fold_in(key_of[9], 71), 0)
    weights = gaussian(key_of[5], (D, KVW), D ** -0.5, 0.078125, ((0, 8),), jnp.float32)
    moment1 = gaussian(key_of[6], (D, KVW), 0.5, 3.0, ((0, 8),), jnp.float32)
    moment2 = jnp.clip(jnp.exp(math.log(4.0) - 2.7725887 * jax.random.uniform(key_of[7], (D, KVW), jnp.float32) ** level_of(key_of[7], (D, KVW), ((0, 8),), -0.2, 0.2)), 0.25, 4.0)
    grad_parts = gaussian(key_of[8], (N_GROUP, D, KVW), 0.3, 2.0, ((0, 4), (1, 8)), jnp.float32)
    return {"tokens": tokens, "queries": queries, "cache_keys": cache_keys, "cache_values": cache_values, "lengths": lengths, "weights": weights, "moment1": moment1, "moment2": moment2, "grad_parts": grad_parts}


beta_one = 0.9
beta_two = 0.95
learning_rate = 0.004
decay_rate = 0.1
epsilon = 1e-08
correct_one = 1.0 - 0.9 ** 10
correct_two = 1.0 - 0.95 ** 10
masked_score = -1e+30

def adam_update(weights, moment1, moment2, gradient):
    new_moment1 = beta_one * moment1 + (1.0 - beta_one) * gradient
    new_moment2 = beta_two * moment2 + (1.0 - beta_two) * gradient * gradient
    direction = new_moment1 / correct_one / (jnp.sqrt(new_moment2 / correct_two) + epsilon)
    new_weights = weights - learning_rate * (direction + decay_rate * weights)
    return (new_weights, new_moment1, new_moment2)

def rotate_keys(keys, positions):
    half_width = keys.shape[-1] // 2
    frequency = jnp.power(jnp.float32(1000000.0), -2.0 * jnp.arange(half_width, dtype=jnp.float32) / keys.shape[-1])
    angles = positions[..., None] * frequency
    leading = keys[..., :half_width]
    trailing = keys[..., half_width:]
    cosine = jnp.cos(angles)
    sine_part = jnp.sin(angles)
    return jnp.concatenate([leading * cosine - trailing * sine_part, trailing * cosine + leading * sine_part], axis=-1)

def attend(block_args):
    query_rows, key_rows, value_rows, fresh_rows, row_lengths = block_args
    row_count = query_rows.shape[0]
    per_group = QH // KVH
    score_scale = 1.0 / math.sqrt(HD)
    grouped = query_rows.reshape(row_count, STEPS, KVH, per_group, HD).astype(jnp.float32)
    cached_keys = key_rows.reshape(row_count, LMAX, KVH, HD).astype(jnp.float32)
    cached_values = value_rows.reshape(row_count, LMAX, KVH, HD).astype(jnp.float32)
    fresh = fresh_rows.reshape(row_count, STEPS, KVH, 2, HD).astype(jnp.float32)
    cached_scores = jnp.einsum('risgd,rpsd->risgp', grouped, cached_keys) * score_scale
    in_range = jnp.arange(LMAX, dtype=jnp.int32)[None, :] < row_lengths[:, None]
    cached_scores = jnp.where(in_range[:, None, None, None, :], cached_scores, masked_score)
    new_scores = jnp.einsum('risgd,rjsd->risgj', grouped, fresh[:, :, :, 0]) * score_scale
    causal = jnp.arange(STEPS)[:, None] >= jnp.arange(STEPS)[None, :]
    new_scores = jnp.where(causal[None, :, None, None, :], new_scores, masked_score)
    all_scores = jnp.concatenate([cached_scores, new_scores], axis=-1)
    highest = lax.optimization_barrier(jnp.max(all_scores, axis=-1, keepdims=True))
    exponent = jnp.exp(all_scores - highest)
    probs = (exponent / lax.optimization_barrier(jnp.sum(exponent, axis=-1, keepdims=True))).astype(jnp.bfloat16)
    probs_wide = probs.astype(jnp.float32)
    context = jnp.einsum('risgp,rpsd->risgd', probs_wide[..., :LMAX], cached_values)
    context = context + jnp.einsum('risgj,rjsd->risgd', probs_wide[..., LMAX:], fresh[:, :, :, 1])
    return context.reshape(row_count, STEPS, QH * HD).astype(jnp.bfloat16)

def reference(tokens, queries, cache_keys, cache_values, lengths, weights, moment1, moment2, grad_parts):
    gradient = lax.optimization_barrier(jnp.sum(grad_parts, axis=0))
    new_weights, new_moment1, new_moment2 = adam_update(weights, moment1, moment2, gradient)
    rollout = new_weights.astype(jnp.bfloat16)
    projected = jnp.dot(tokens.reshape(ROWS * STEPS, D), rollout, preferred_element_type=jnp.float32)
    projected = projected.reshape(ROWS, STEPS, KVH, 2, HD)
    positions = (lengths[:, None] + jnp.arange(STEPS, dtype=jnp.int32)[None, :]).astype(jnp.float32)
    new_keys = rotate_keys(projected[:, :, :, 0], positions[:, :, None])
    new_kv = jnp.stack([new_keys, projected[:, :, :, 1]], axis=3).reshape(ROWS, STEPS, 2 * KVH * HD).astype(jnp.bfloat16)
    blocks = ROWS // R_DEV
    pieces = (queries.reshape(blocks, R_DEV, STEPS, QH * HD), cache_keys.reshape(blocks, R_DEV, LMAX, KVH * HD), cache_values.reshape(blocks, R_DEV, LMAX, KVH * HD), new_kv.reshape(blocks, R_DEV, STEPS, 2 * KVH * HD), lengths.reshape(blocks, R_DEV))
    context = lax.map(attend, pieces).reshape(ROWS, STEPS, QH * HD)
    return (new_weights, new_moment1, new_moment2, new_kv, context)
```

```python
import functools
import math

import jax
import jax.numpy as jnp
from jax import lax
from jax.experimental import pallas as pl
from jax.experimental.pallas import tpu as pltpu
from jax.sharding import PartitionSpec as P

QH = 40
KVH = 8
HD = 128
STEPS = 4
PER_GROUP = QH // KVH
HEAD_COLS = 2 * HD


beta_one = 0.9
beta_two = 0.95
learning_rate = 0.004
decay_rate = 0.1
epsilon = 1e-08
correct_one = 1.0 - 0.9**10
correct_two = 1.0 - 0.95**10
masked_score = -1e30
score_scale = 1.0 / math.sqrt(HD)
VMEM_LIMIT = 40 * 1024 * 1024


def adam_update(weights, moment1, moment2, gradient):
    new_moment1 = beta_one * moment1 + (1.0 - beta_one) * gradient
    new_moment2 = beta_two * moment2 + (1.0 - beta_two) * gradient * gradient
    direction = new_moment1 / correct_one / (jnp.sqrt(new_moment2 / correct_two) + epsilon)
    new_weights = weights - learning_rate * (direction + decay_rate * weights)
    return (new_weights, new_moment1, new_moment2)


def rotation_tables(lengths):
    half_width = HD // 2
    frequency = jnp.power(
        jnp.float32(1000000.0), -2.0 * jnp.arange(half_width, dtype=jnp.float32) / HD
    )
    positions = (lengths[:, None] + jnp.arange(STEPS, dtype=jnp.int32)[None, :]).astype(jnp.float32)
    angles = positions.reshape(-1)[:, None] * frequency
    cosine = jnp.cos(angles)
    sine = jnp.sin(angles)
    return (
        jnp.concatenate([cosine, cosine], axis=-1),
        jnp.concatenate([-sine, sine], axis=-1),
    )


def adam_kernel(n_parts, n_tok, place, *refs):
    totals = refs[:n_parts]
    w, m1, m2 = refs[n_parts : n_parts + 3]
    toks = refs[n_parts + 3 : n_parts + 3 + n_tok]
    new_w, new_m1, new_m2 = refs[-3 - n_parts : -n_parts]
    sums = refs[-n_parts:]
    part = pl.program_id(0)
    cols = pl.program_id(1)
    for j in range(n_parts):

        @pl.when(part == j)
        def _():
            gradient = totals[j][...].astype(jnp.float32)
            weights, moment1, moment2 = adam_update(w[...], m1[...], m2[...], gradient)
            new_w[...] = weights
            new_m1[...] = moment1
            new_m2[...] = moment2
            rollout = weights.astype(jnp.bfloat16)
            tok = jnp.concatenate([t[...] for t in toks], axis=0)
            terms = jnp.dot(tok, rollout, preferred_element_type=jnp.float32)
            sums[j][:, pl.ds(pl.multiple_of(cols * HD, HD), HD)] = terms.astype(jnp.bfloat16)


def adam_and_project(place, parts, totals, weights, moment1, moment2, toks, previous, chunk, n_chunks):
    rows, width = weights.shape
    per_head = HEAD_COLS // HD
    n = len(parts)

    def column(j, b, place):
        half = jnp.int32(0)
        for i, p in enumerate(parts):
            half = jnp.where(j == i, place[0] if p == 0 else 1 - place[0], half)
        return (0, (half * n_chunks + chunk) * per_head + b)

    def total_map(i):
        return lambda j, b, place: (0, jnp.where(j == i, b, jnp.where(j < i, 0, per_head - 1)))

    block = pl.BlockSpec((rows, HD), column)
    n_tokens = sum(t.shape[0] for t in toks)
    whole = lambda shape: pl.BlockSpec(shape, lambda j, b, place: (0,) * len(shape))
    in_specs = (
        [pl.BlockSpec((rows, HD), total_map(i)) for i in range(n)]
        + [block] * 3
        + [whole(t.shape) for t in toks]
    )
    operands = [*totals, weights, moment1, moment2, *toks]
    aliases = {}
    if previous is not None:
        for i, p in enumerate(previous):
            aliases[1 + len(operands)] = i
            operands.append(p)
            in_specs.append(pl.BlockSpec(memory_space=pl.ANY))
    full = jax.ShapeDtypeStruct((rows, width), jnp.float32)
    out = pl.pallas_call(
        functools.partial(adam_kernel, n, len(toks)),
        grid_spec=pltpu.PrefetchScalarGridSpec(
            num_scalar_prefetch=1,
            grid=(n, per_head),
            in_specs=in_specs,
            out_specs=[block] * 3 + [whole((n_tokens, HEAD_COLS))] * n,
        ),
        out_shape=[full] * 3 + [jax.ShapeDtypeStruct((n_tokens, HEAD_COLS), jnp.bfloat16)] * n,
        input_output_aliases=aliases,
        compiler_params=pltpu.CompilerParams(vmem_limit_bytes=VMEM_LIMIT),
        cost_estimate=pl.CostEstimate(
            flops=2 * n_tokens * rows * HEAD_COLS * n,
            bytes_accessed=26 * rows * HEAD_COLS * n,
            transcendentals=0,
        ),
        name="adam_project",
    )(place, *operands)
    return tuple(out[:3]), tuple(out[3:])


SLOT = 32


def cache_kernel(heads, lens, q, k, v, stacked, acc, stats):
    row = pl.program_id(0)
    length = lens[row]
    query = q[0].astype(jnp.float32)
    used = PER_GROUP * STEPS
    blocks = []
    for h in range(heads):
        pieces = [
            query[:, (h * PER_GROUP + g) * HD : (h * PER_GROUP + g + 1) * HD] for g in range(PER_GROUP)
        ]
        pieces.append(jnp.zeros((SLOT - used, HD), jnp.float32))
        one = jnp.concatenate(pieces, axis=0).astype(jnp.bfloat16)
        stacked[h, 0] = one
        blocks.append(one)
    keys = k[0]
    values = v[0]
    span = keys.shape[0]
    in_range = lax.broadcasted_iota(jnp.int32, (1, span), 1) < length
    for h in range(heads):
        cols = slice(h * HD, (h + 1) * HD)
        scores = (
            lax.dot_general(
                blocks[h], keys[:, cols], (((1,), (1,)), ((), ())), preferred_element_type=jnp.float32
            )
            * score_scale
        )
        scores = jnp.where(in_range, scores, masked_score)
        highest = jnp.max(scores, axis=-1, keepdims=True)
        weight = jnp.exp(scores - highest)
        total = jnp.sum(weight, axis=-1, keepdims=True)
        acc[h, 0] = jnp.dot(
            weight.astype(jnp.bfloat16), values[:, cols], preferred_element_type=jnp.float32
        )
        lane = lax.broadcasted_iota(jnp.int32, (SLOT, HD), 1)
        stats[h, 0] = jnp.where(lane < HD // 2, highest, total)


def cache_attention(queries, cache_keys, cache_values, lengths):
    row_count, span, kv_cols = cache_keys.shape
    heads = kv_cols // HD
    shape = (heads, row_count, SLOT, HD)
    out_block = pl.BlockSpec((heads, 1, SLOT, HD), lambda r, lens: (0, r, 0, 0))
    return pl.pallas_call(
        functools.partial(cache_kernel, heads),
        grid_spec=pltpu.PrefetchScalarGridSpec(
            num_scalar_prefetch=1,
            grid=(row_count,),
            in_specs=[
                pl.BlockSpec((1, STEPS, queries.shape[2]), lambda r, lens: (r, 0, 0)),
                pl.BlockSpec((1, span, kv_cols), lambda r, lens: (r, 0, 0)),
                pl.BlockSpec((1, span, kv_cols), lambda r, lens: (r, 0, 0)),
            ],
            out_specs=[out_block] * 3,
        ),
        out_shape=[
            jax.ShapeDtypeStruct(shape, jnp.bfloat16),
            jax.ShapeDtypeStruct(shape, jnp.float32),
            jax.ShapeDtypeStruct(shape, jnp.float32),
        ],
        compiler_params=pltpu.CompilerParams(vmem_limit_bytes=VMEM_LIMIT),
        cost_estimate=pl.CostEstimate(
            flops=8 * row_count * SLOT * span * kv_cols,
            bytes_accessed=4 * row_count * span * kv_cols,
            transcendentals=row_count * heads * SLOT * span,
        ),
        name="cache_attention",
    )(lengths, queries, cache_keys, cache_values)


def fold_kernel(n, arrived, kept, *outs):
    total = arrived[...].astype(jnp.float32) + kept[...].astype(jnp.float32)
    step = total.shape[0] // n
    for d in range(n):
        outs[d][...] = total[d * step : (d + 1) * step].astype(outs[d].dtype)


def fold(arrived, kept, n):
    rows, width = kept.shape
    step = rows // n
    return pl.pallas_call(
        functools.partial(fold_kernel, n),
        out_shape=[
            jax.ShapeDtypeStruct((step, width), jnp.float32 if d == 0 else jnp.bfloat16) for d in range(n)
        ],
        name="fold_halves",
    )(arrived, kept)


def merge_kernel(n, row_count, *refs):
    pieces = refs[:n]
    cosine, sine, stacked, acc, stats = refs[n : n + 5]
    new_kv, context = refs[-2:]
    total = pieces[0][...].astype(jnp.float32)
    for piece in pieces[1:]:
        total = total + piece[...].astype(jnp.float32)
    keys = total[:, :HD]
    keys = keys * cosine[...] + pltpu.roll(keys, HD // 2, 1) * sine[...]
    keys = keys.astype(jnp.bfloat16)
    values = total[:, HD:].astype(jnp.bfloat16)
    both = jnp.concatenate([keys, values], axis=1).astype(jnp.float32)
    for r in range(row_count):
        new_kv[r] = both[r * STEPS : (r + 1) * STEPS].astype(jnp.bfloat16)
    query = stacked[0].reshape(row_count * SLOT, HD)
    scores = (
        lax.dot_general(query, keys, (((1,), (1,)), ((), ())), preferred_element_type=jnp.float32)
        * score_scale
    )
    at = lax.broadcasted_iota(jnp.int32, scores.shape, 0)
    to = lax.broadcasted_iota(jnp.int32, scores.shape, 1)
    seen = (at // SLOT == to // STEPS) & (at % STEPS >= to % STEPS)
    scores = jnp.where(seen, scores, masked_score)
    stat = stats[0].reshape(row_count * SLOT, HD)
    old_highest = stat[:, :1]
    old_total = stat[:, HD // 2 : HD // 2 + 1]
    highest = jnp.maximum(jnp.max(scores, axis=-1, keepdims=True), old_highest)
    weight = jnp.exp(scores - highest)
    scale = jnp.exp(old_highest - highest)
    denominator = jnp.sum(weight, axis=-1, keepdims=True) + scale * old_total
    out = jnp.dot(weight.astype(jnp.bfloat16), values, preferred_element_type=jnp.float32)
    out = (out + scale * acc[0].reshape(row_count * SLOT, HD)) / denominator
    for r in range(row_count):
        for g in range(PER_GROUP):
            first = r * SLOT + g * STEPS
            context[r, :, g * HD : (g + 1) * HD] = out[first : first + STEPS].astype(jnp.bfloat16)


def merge(pieces, cosine, sine, stacked, acc, stats, previous, head):
    heads, row_count = stacked.shape[:2]
    whole = lambda a: pl.BlockSpec(a.shape, lambda i: (0,) * a.ndim)
    one_head = pl.BlockSpec((1, row_count, SLOT, HD), lambda i: (head, 0, 0, 0))
    operands = [*pieces, cosine, sine, stacked, acc, stats]
    in_specs = [whole(p) for p in pieces] + [whole(cosine), whole(sine)] + [one_head] * 3
    aliases = {}
    if previous is not None:
        for i, p in enumerate(previous):
            aliases[len(operands)] = i
            operands.append(p)
            in_specs.append(pl.BlockSpec(memory_space=pl.ANY))
    return pl.pallas_call(
        functools.partial(merge_kernel, len(pieces), row_count),
        grid=(1,),
        in_specs=in_specs,
        out_specs=[
            pl.BlockSpec((row_count, STEPS, HEAD_COLS), lambda i: (0, 0, head)),
            pl.BlockSpec((row_count, STEPS, PER_GROUP * HD), lambda i: (0, 0, head)),
        ],
        out_shape=[
            jax.ShapeDtypeStruct((row_count, STEPS, heads * HEAD_COLS), jnp.bfloat16),
            jax.ShapeDtypeStruct((row_count, STEPS, heads * PER_GROUP * HD), jnp.bfloat16),
        ],
        input_output_aliases=aliases,
        compiler_params=pltpu.CompilerParams(vmem_limit_bytes=VMEM_LIMIT),
        name="merge_new",
    )(*operands)


def swap(array, axis, bit):
    size = lax.axis_size(axis)
    return lax.ppermute(array, axis, [(i, i ^ bit) for i in range(size)])


def add_rounded(a, b):
    return (a.astype(jnp.float32) + b.astype(jnp.float32)).astype(jnp.bfloat16)


def butterfly_shards(
    tokens, queries, cache_keys, cache_values, lengths, weights, moment1, moment2, grad_parts
):
    group_count = lax.axis_size("group")
    fsdp_count = lax.axis_size("fsdp")
    tp_count = lax.axis_size("tp")
    core = lax.axis_index("group") % 2
    fsdp = lax.axis_index("fsdp")
    tp = lax.axis_index("tp")
    place = jnp.stack([core, tp]).astype(jnp.int32)
    rows, width = weights.shape
    row_count = tokens.shape[0]
    n_chunks = width // (tp_count * HEAD_COLS)
    local = grad_parts[0]

    def columns(half, chunk):
        return lax.dynamic_slice(local, (0, (half * n_chunks + chunk) * HEAD_COLS), (rows, HEAD_COLS))

    arrived = [swap(columns(1 - core, k).astype(jnp.bfloat16), "group", 1) for k in range(n_chunks)]
    own = [add_rounded(columns(core, k), arrived[k]) for k in range(n_chunks)]
    bit = 2
    while bit < group_count:
        own = [add_rounded(o, swap(o, "group", bit)) for o in own]
        bit *= 2
    partner = [swap(o, "group", 1) for o in own]

    toks = []
    for d in range(fsdp_count):
        first = ((fsdp ^ d) * tp_count + tp) * rows
        piece = lax.dynamic_slice(tokens, (0, 0, first), (row_count, STEPS, rows))
        piece = piece.reshape(row_count * STEPS, rows)
        toks.append(piece if d == 0 else swap(piece, "fsdp", d))

    cosine, sine = rotation_tables(lengths)
    stacked, acc, stats = cache_attention(queries, cache_keys, cache_values, lengths)

    updated = None
    outs = None
    same = core == tp
    for k in range(n_chunks):
        updated, (own_sums, partner_sums) = adam_and_project(
            place, (0, 1), (own[k], partner[k]), weights, moment1, moment2, toks, updated, k, n_chunks
        )
        kept = jnp.where(same, own_sums, partner_sums)
        sent = jnp.where(same, partner_sums, own_sums)
        pieces = fold(swap(sent, "tp", 1), kept, fsdp_count)
        pieces = [pieces[0]] + [swap(pieces[d], "fsdp", d) for d in range(1, fsdp_count)]
        outs = merge(pieces, cosine, sine, stacked, acc, stats, outs, k)
    return (*updated, *outs)


def rotate_keys(keys, positions):
    half_width = keys.shape[-1] // 2
    frequency = jnp.power(
        jnp.float32(1000000.0), -2.0 * jnp.arange(half_width, dtype=jnp.float32) / keys.shape[-1]
    )
    angles = positions[..., None] * frequency
    leading = keys[..., :half_width]
    trailing = keys[..., half_width:]
    cosine = jnp.cos(angles)
    sine_part = jnp.sin(angles)
    return jnp.concatenate(
        [leading * cosine - trailing * sine_part, trailing * cosine + leading * sine_part], axis=-1
    )


def plain_shards(
    tokens, queries, cache_keys, cache_values, lengths, weights, moment1, moment2, grad_parts
):
    gradient = lax.psum(grad_parts[0], "group")
    new_weights, new_moment1, new_moment2 = adam_update(weights, moment1, moment2, gradient)
    weight_shard = new_weights.astype(jnp.bfloat16)
    tp_count = lax.axis_size("tp")
    fsdp_count = lax.axis_size("fsdp")
    head_cols = weight_shard.shape[1] // tp_count
    row_count = tokens.shape[0]
    block_rows = weight_shard.shape[0]
    split_tokens = tokens.reshape(row_count, STEPS, fsdp_count, tp_count, block_rows)
    own_columns = lax.dynamic_index_in_dim(split_tokens, lax.axis_index("tp"), 3, keepdims=False)
    arrived = lax.all_to_all(own_columns, "fsdp", split_axis=2, concat_axis=0, tiled=True)
    arrived = arrived.reshape(fsdp_count * row_count * STEPS, block_rows)
    partial_terms = jnp.dot(arrived, weight_shard, preferred_element_type=jnp.float32)
    partial_terms = partial_terms.reshape(fsdp_count, row_count * STEPS, tp_count, head_cols)
    partial_terms = partial_terms.transpose(0, 2, 1, 3).reshape(
        fsdp_count * tp_count * row_count * STEPS, head_cols
    )
    projected = lax.psum_scatter(partial_terms, ("fsdp", "tp"), scatter_dimension=0, tiled=True)
    kv_heads = head_cols // (2 * HD)
    projected = projected.reshape(row_count, STEPS, kv_heads, 2, HD)
    positions = (lengths[:, None] + jnp.arange(STEPS, dtype=jnp.int32)[None, :]).astype(jnp.float32)
    new_keys = rotate_keys(projected[:, :, :, 0], positions[:, :, None])
    fresh = jnp.stack([new_keys, projected[:, :, :, 1]], axis=3).astype(jnp.bfloat16)
    new_kv = fresh.reshape(row_count, STEPS, head_cols)
    span_length = cache_keys.shape[1]
    grouped = queries.reshape(row_count, STEPS, kv_heads, PER_GROUP, HD)
    cached_keys = cache_keys.reshape(row_count, span_length, kv_heads, HD)
    cached_values = cache_values.reshape(row_count, span_length, kv_heads, HD)
    new_scores = (
        jnp.einsum(
            "risgd,rjsd->risgj", grouped, fresh[:, :, :, 0], preferred_element_type=jnp.float32
        )
        * score_scale
    )
    causal = jnp.arange(STEPS)[:, None] >= jnp.arange(STEPS)[None, :]
    new_scores = jnp.where(causal[None, :, None, None, :], new_scores, masked_score)
    scores = (
        jnp.einsum("risgd,rpsd->risgp", grouped, cached_keys, preferred_element_type=jnp.float32)
        * score_scale
    )
    in_range = jnp.arange(span_length, dtype=jnp.int32)[None, :] < lengths[:, None]
    all_scores = jnp.concatenate(
        [jnp.where(in_range[:, None, None, None, :], scores, masked_score), new_scores], axis=-1
    )
    highest = jnp.max(all_scores, axis=-1, keepdims=True)
    exponent = jnp.exp(all_scores - highest)
    probs = (exponent / jnp.sum(exponent, axis=-1, keepdims=True)).astype(jnp.bfloat16)
    context = jnp.einsum(
        "risgp,rpsd->risgd",
        probs[..., :span_length],
        cached_values,
        preferred_element_type=jnp.float32,
    )
    context = context + jnp.einsum(
        "risgj,rjsd->risgd",
        probs[..., span_length:],
        fresh[:, :, :, 1],
        preferred_element_type=jnp.float32,
    )
    context = context.reshape(row_count, STEPS, kv_heads * PER_GROUP * HD).astype(jnp.bfloat16)
    return (new_weights, new_moment1, new_moment2, new_kv, context)


def power_of_two(n):
    return n > 1 and n & (n - 1) == 0


def solution(mesh):
    in_specs = (
        P(("group", "fsdp"), None, None),
        P(("group", "fsdp"), None, "tp"),
        P(("group", "fsdp"), None, "tp"),
        P(("group", "fsdp"), None, "tp"),
        P(("group", "fsdp")),
        P(("fsdp", "tp"), None),
        P(("fsdp", "tp"), None),
        P(("fsdp", "tp"), None),
        P("group", ("fsdp", "tp"), None),
    )
    out_specs = (
        P(("fsdp", "tp"), None),
        P(("fsdp", "tp"), None),
        P(("fsdp", "tp"), None),
        P(("group", "fsdp"), None, "tp"),
        P(("group", "fsdp"), None, "tp"),
    )
    sizes = mesh.shape
    pairwise = power_of_two(sizes["group"]) and power_of_two(sizes["fsdp"]) and sizes["tp"] == 2
    shards = butterfly_shards if pairwise else plain_shards
    return jax.shard_map(shards, mesh=mesh, in_specs=in_specs, out_specs=out_specs, check_vma=False)
```

```python
import functools
import math

import jax
import jax.numpy as jnp
from jax import lax
from jax.experimental import pallas as pl
from jax.experimental.pallas import tpu as pltpu
from jax.sharding import PartitionSpec as P

QH = 40
KVH = 8
HD = 128
STEPS = 4
PER_GROUP = QH // KVH
HEAD_COLS = 2 * HD


beta_one = 0.9
beta_two = 0.95
learning_rate = 0.004
decay_rate = 0.1
epsilon = 1e-08
correct_one = 1.0 - 0.9**10
correct_two = 1.0 - 0.95**10
masked_score = -1e30
score_scale = 1.0 / math.sqrt(HD)
VMEM_LIMIT = 60 * 1024 * 1024


def adam_update(weights, moment1, moment2, gradient):
    new_moment1 = beta_one * moment1 + (1.0 - beta_one) * gradient
    new_moment2 = beta_two * moment2 + (1.0 - beta_two) * gradient * gradient
    direction = new_moment1 / correct_one / (jnp.sqrt(new_moment2 / correct_two) + epsilon)
    new_weights = weights - learning_rate * (direction + decay_rate * weights)
    return (new_weights, new_moment1, new_moment2)


def rotation_tables(lengths):
    half_width = HD // 2
    frequency = jnp.power(
        jnp.float32(1000000.0), -2.0 * jnp.arange(half_width, dtype=jnp.float32) / HD
    )
    positions = (lengths[:, None] + jnp.arange(STEPS, dtype=jnp.int32)[None, :]).astype(jnp.float32)
    angles = positions.reshape(-1)[:, None] * frequency
    cosine = jnp.cos(angles)
    sine = jnp.sin(angles)
    return (
        jnp.concatenate([cosine, cosine], axis=-1),
        jnp.concatenate([-sine, sine], axis=-1),
    )


def whole(a):
    return pl.BlockSpec(a.shape, lambda *_: (0,) * len(a.shape))


def adam_kernel(n_parts, n_tok, update, project, place, *refs):
    totals = refs[:n_parts]
    w, m1, m2 = refs[n_parts : n_parts + 3]
    toks = refs[n_parts + 3 : n_parts + 3 + n_tok]
    outs = refs[len(refs) - 3 * update - 2 * project :]
    part = pl.program_id(0)
    cols = pl.program_id(1)
    gradient = totals[0][...]
    for j in range(1, n_parts):
        gradient = jnp.where(part == j, totals[j][...], gradient)
    results = adam_update(w[...], m1[...], m2[...], gradient.astype(jnp.float32))
    if update:
        for ref, value in zip(outs, results):
            ref[...] = value
    if project:
        sent, kept = outs[-2:]
        tok = jnp.concatenate([t[...] for t in toks], axis=0)
        terms = jnp.dot(tok, results[0].astype(jnp.bfloat16), preferred_element_type=jnp.float32)
        width = terms.shape[1]
        at = pl.ds(pl.multiple_of(cols * width, width), width)
        half = half_of(place, part)
        stays = half == place[1]

        @pl.when(stays)
        def _():
            kept[:, at] = terms

        @pl.when(jnp.logical_not(stays))
        def _():
            sent[:, at] = terms.astype(jnp.bfloat16)


def half_of(place, part):
    return jnp.where(part + place[2] == 1, 1 - place[0], place[0])


def adam_call(place, totals, state, toks, first, n_units, n_chunks, update, project, previous=None, sums=None):
    weights = state[0]
    rows, width = weights.shape
    n = len(totals)

    def column(j, b, place):
        return (0, half_of(place, j) * n_chunks + first + b)

    def total_map(i):
        return lambda j, b, place: (0, jnp.where(j == i, b, jnp.where(j < i, 0, n_units - 1)))

    block = pl.BlockSpec((rows, HEAD_COLS), column)
    in_specs = [pl.BlockSpec((rows, HEAD_COLS), total_map(i)) for i in range(n)] + [block] * 3
    operands = [*totals, *state]
    if project:
        operands += toks
        in_specs += [whole(t) for t in toks]
    out_specs, out_shape, aliases = [], [], {}
    if update:
        out_specs += [block] * 3
        out_shape += [jax.ShapeDtypeStruct((rows, width), jnp.float32)] * 3
        if previous is not None:
            for i, p in enumerate(previous):
                aliases[1 + len(operands)] = i
                operands.append(p)
                in_specs.append(pl.BlockSpec(memory_space=pl.ANY))
    n_tokens = sum(t.shape[0] for t in toks)
    if project:
        for dtype in (jnp.bfloat16, jnp.float32):
            out_shape.append(jax.ShapeDtypeStruct((n_tokens, n_units * HEAD_COLS), dtype))
            out_specs.append(whole(out_shape[-1]))
    out = pl.pallas_call(
        functools.partial(adam_kernel, n, len(toks) if project else 0, update, project),
        grid_spec=pltpu.PrefetchScalarGridSpec(
            num_scalar_prefetch=1,
            grid=(n, n_units),
            in_specs=in_specs,
            out_specs=out_specs,
        ),
        out_shape=out_shape,
        input_output_aliases=aliases,
        compiler_params=pltpu.CompilerParams(vmem_limit_bytes=VMEM_LIMIT),
        cost_estimate=pl.CostEstimate(
            flops=2 * n_tokens * rows * HEAD_COLS * n * n_units,
            bytes_accessed=(14 + 12 * update) * rows * HEAD_COLS * n * n_units,
            transcendentals=0,
        ),
        name="adam_project" if project else "adam_update",
    )(place, *operands)
    return (tuple(out[:3]) if update else None), (tuple(out[-2:]) if project else None)


SLOT = 32


def cache_kernel(heads, lens, q, k, v, stacked, acc, stats):
    rows = q.shape[0]
    span = k.shape[1]
    used = PER_GROUP * STEPS
    for i in range(rows):
        length = lens[pl.program_id(0) * rows + i]
        query = q[i].astype(jnp.float32)
        scores = []
        for h in range(heads):
            pieces = [
                query[:, (h * PER_GROUP + g) * HD : (h * PER_GROUP + g + 1) * HD] for g in range(PER_GROUP)
            ]
            pieces.append(jnp.zeros((SLOT - used, HD), jnp.float32))
            one = jnp.concatenate(pieces, axis=0).astype(jnp.bfloat16)
            stacked[h, i] = one
            scores.append(
                lax.dot_general(
                    one,
                    k[i, :, h * HD : (h + 1) * HD],
                    (((1,), (1,)), ((), ())),
                    preferred_element_type=jnp.float32,
                )
            )
        scores = jnp.concatenate(scores, axis=0) * score_scale
        in_range = lax.broadcasted_iota(jnp.int32, (1, span), 1) < length
        scores = jnp.where(in_range, scores, masked_score)
        highest = jnp.max(scores, axis=-1, keepdims=True)
        weight = jnp.exp(scores - highest)
        total = jnp.sum(weight, axis=-1, keepdims=True)
        weight = weight.astype(jnp.bfloat16)
        lane = lax.broadcasted_iota(jnp.int32, (heads * SLOT, HD), 1)
        stat = jnp.where(lane < HD // 2, highest, total)
        for h in range(heads):
            at = slice(h * SLOT, (h + 1) * SLOT)
            acc[h, i] = jnp.dot(
                weight[at], v[i, :, h * HD : (h + 1) * HD], preferred_element_type=jnp.float32
            )
            stats[h, i] = stat[at]


def cache_attention(queries, cache_keys, cache_values, lengths):
    row_count, span, kv_cols = cache_keys.shape
    heads = kv_cols // HD
    rows = 2 if row_count % 2 == 0 else 1
    shape = (heads, row_count, SLOT, HD)
    out_block = pl.BlockSpec((heads, rows, SLOT, HD), lambda r, lens: (0, r, 0, 0))
    in_block = lambda a: pl.BlockSpec((rows, *a.shape[1:]), lambda r, lens: (r, 0, 0))
    return pl.pallas_call(
        functools.partial(cache_kernel, heads),
        grid_spec=pltpu.PrefetchScalarGridSpec(
            num_scalar_prefetch=1,
            grid=(row_count // rows,),
            in_specs=[in_block(queries), in_block(cache_keys), in_block(cache_values)],
            out_specs=[out_block] * 3,
        ),
        out_shape=[
            jax.ShapeDtypeStruct(shape, jnp.bfloat16),
            jax.ShapeDtypeStruct(shape, jnp.float32),
            jax.ShapeDtypeStruct(shape, jnp.float32),
        ],
        compiler_params=pltpu.CompilerParams(vmem_limit_bytes=VMEM_LIMIT),
        cost_estimate=pl.CostEstimate(
            flops=8 * row_count * SLOT * span * kv_cols,
            bytes_accessed=4 * row_count * span * kv_cols,
            transcendentals=row_count * heads * SLOT * span,
        ),
        name="cache_attention",
    )(lengths, queries, cache_keys, cache_values)


def merge_kernel(n_units, row_count, *refs):
    arrived, kept, cosine, sine, stacked, acc, stats = refs[:7]
    new_kv, context = refs[-2:]
    every = arrived[...].astype(jnp.float32) + kept[...]
    for u in range(n_units):
        total = every[:, u * HEAD_COLS : (u + 1) * HEAD_COLS]
        keys = total[:, :HD]
        keys = keys * cosine[...] + pltpu.roll(keys, HD // 2, 1) * sine[...]
        keys = keys.astype(jnp.bfloat16)
        values = total[:, HD:].astype(jnp.bfloat16)
        both = jnp.concatenate([keys, values], axis=1).astype(jnp.float32)
        for r in range(row_count):
            new_kv[r, :, u * HEAD_COLS : (u + 1) * HEAD_COLS] = both[
                r * STEPS : (r + 1) * STEPS
            ].astype(jnp.bfloat16)
        query = stacked[u].reshape(row_count * SLOT, HD)
        scores = (
            lax.dot_general(query, keys, (((1,), (1,)), ((), ())), preferred_element_type=jnp.float32)
            * score_scale
        )
        at = lax.broadcasted_iota(jnp.int32, scores.shape, 0)
        to = lax.broadcasted_iota(jnp.int32, scores.shape, 1)
        seen = (at // SLOT == to // STEPS) & (at % STEPS >= to % STEPS)
        scores = jnp.where(seen, scores, masked_score)
        stat = stats[u].reshape(row_count * SLOT, HD)
        old_highest = stat[:, :1]
        old_total = stat[:, HD // 2 : HD // 2 + 1]
        highest = jnp.maximum(jnp.max(scores, axis=-1, keepdims=True), old_highest)
        weight = jnp.exp(scores - highest)
        scale = jnp.exp(old_highest - highest)
        denominator = jnp.sum(weight, axis=-1, keepdims=True) + scale * old_total
        out = jnp.dot(weight.astype(jnp.bfloat16), values, preferred_element_type=jnp.float32)
        out = (out + scale * acc[u].reshape(row_count * SLOT, HD)) / denominator
        for r in range(row_count):
            for g in range(PER_GROUP):
                at_row = r * SLOT + g * STEPS
                at_col = (u * PER_GROUP + g) * HD
                context[r, :, at_col : at_col + HD] = out[at_row : at_row + STEPS].astype(jnp.bfloat16)


def merge(arrived, kept, cosine, sine, attended, previous, first, n_units):
    heads, row_count = attended[0].shape[:2]
    at = first // n_units
    some = pl.BlockSpec((n_units, row_count, SLOT, HD), lambda i: (at, 0, 0, 0))
    operands = [arrived, kept, cosine, sine]
    in_specs = [whole(a) for a in operands] + [some] * 3
    operands += attended
    aliases = {}
    if previous is not None:
        for i, p in enumerate(previous):
            aliases[len(operands)] = i
            operands.append(p)
            in_specs.append(pl.BlockSpec(memory_space=pl.ANY))
    widths = (HEAD_COLS, PER_GROUP * HD)
    return pl.pallas_call(
        functools.partial(merge_kernel, n_units, row_count),
        grid=(1,),
        in_specs=in_specs,
        out_specs=[pl.BlockSpec((row_count, STEPS, n_units * w), lambda i: (0, 0, at)) for w in widths],
        out_shape=[jax.ShapeDtypeStruct((row_count, STEPS, heads * w), jnp.bfloat16) for w in widths],
        input_output_aliases=aliases,
        compiler_params=pltpu.CompilerParams(vmem_limit_bytes=VMEM_LIMIT),
        name="merge_new",
    )(*operands)


def swap(array, axis, bit):
    size = lax.axis_size(axis)
    return lax.ppermute(array, axis, [(i, i ^ bit) for i in range(size)])


def add_rounded(a, b):
    return (a.astype(jnp.float32) + b.astype(jnp.float32)).astype(jnp.bfloat16)


def after(value, *earlier):
    return lax.optimization_barrier((value, *earlier))[0]


def fold_rows(arrived, kept, n):
    total = arrived.astype(jnp.float32) + kept
    half = total.shape[0] // 2
    return total[half:].astype(jnp.bfloat16), total[:half]


def butterfly_shards(
    tokens, queries, cache_keys, cache_values, lengths, weights, moment1, moment2, grad_parts
):
    group_count = lax.axis_size("group")
    fsdp_count = lax.axis_size("fsdp")
    tp_count = lax.axis_size("tp")
    core = lax.axis_index("group") % 2
    fsdp = lax.axis_index("fsdp")
    tp = lax.axis_index("tp")
    rows, width = weights.shape
    row_count = tokens.shape[0]
    n_chunks = width // (tp_count * HEAD_COLS)
    local = grad_parts[0]
    state = (weights, moment1, moment2)
    zero = jnp.zeros_like(core)
    both_parts = jnp.stack([core, tp, zero]).astype(jnp.int32)

    cut = n_chunks // 2
    chunks = [(0, cut), (cut, n_chunks - cut)]

    def columns(source, half, first, n):
        return lax.dynamic_slice(
            source, (0, (half * n_chunks + first) * HEAD_COLS), (rows, n * HEAD_COLS)
        )

    cast, arrived, own, crossed = [], [], [], []
    source = local
    for first, n in chunks:
        cast.append(columns(source, 1 - core, first, n).astype(jnp.bfloat16))
        arrived.append(swap(cast[-1], "group", 1))
        source = after(local, cast[-1])
    source = local
    for (first, n), got in zip(chunks, arrived):
        own.append(add_rounded(columns(source, core, first, n), got))
        crossed.append(swap(own[-1], "group", 2))
        source = after(local, own[-1])

    toks = []
    early = after(tokens, own[-1])
    for d in range(fsdp_count):
        at = ((fsdp ^ d) * tp_count + tp) * rows
        piece = lax.dynamic_slice(early, (0, 0, at), (row_count, STEPS, rows))
        piece = piece.reshape(row_count * STEPS, rows)
        toks.append(piece if d == 0 else swap(piece, "fsdp", d))

    cosine, sine = rotation_tables(lengths)
    attended = cache_attention(after(queries, own[-1]), cache_keys, cache_values, lengths)

    updated = None
    outs = None
    done = (attended[1],)
    for (first, n), mine, other in zip(chunks, own, crossed):
        bit = 2
        while True:
            mine = add_rounded(mine, after(other, *done))
            bit *= 2
            if bit >= group_count:
                break
            other = swap(mine, "group", bit)
        totals = (mine, swap(mine, "group", 1))
        updated, (sent, kept) = adam_call(
            both_parts, totals, state, toks, first, n, n_chunks, True, True, updated
        )
        done = (kept,)
        got = swap(sent, "tp", 1)
        distance = fsdp_count // 2
        while distance:
            sent, kept = fold_rows(got, kept, fsdp_count)
            got = swap(sent, "fsdp", distance)
            distance //= 2
        outs = merge(got, kept, cosine, sine, attended, outs, first, n)
    return (*updated, *outs)


def rotate_keys(keys, positions):
    half_width = keys.shape[-1] // 2
    frequency = jnp.power(
        jnp.float32(1000000.0), -2.0 * jnp.arange(half_width, dtype=jnp.float32) / keys.shape[-1]
    )
    angles = positions[..., None] * frequency
    leading = keys[..., :half_width]
    trailing = keys[..., half_width:]
    cosine = jnp.cos(angles)
    sine_part = jnp.sin(angles)
    return jnp.concatenate(
        [leading * cosine - trailing * sine_part, trailing * cosine + leading * sine_part], axis=-1
    )


def plain_shards(
    tokens, queries, cache_keys, cache_values, lengths, weights, moment1, moment2, grad_parts
):
    gradient = lax.psum(grad_parts[0], "group")
    new_weights, new_moment1, new_moment2 = adam_update(weights, moment1, moment2, gradient)
    weight_shard = new_weights.astype(jnp.bfloat16)
    tp_count = lax.axis_size("tp")
    fsdp_count = lax.axis_size("fsdp")
    head_cols = weight_shard.shape[1] // tp_count
    row_count = tokens.shape[0]
    block_rows = weight_shard.shape[0]
    split_tokens = tokens.reshape(row_count, STEPS, fsdp_count, tp_count, block_rows)
    own_columns = lax.dynamic_index_in_dim(split_tokens, lax.axis_index("tp"), 3, keepdims=False)
    arrived = lax.all_to_all(own_columns, "fsdp", split_axis=2, concat_axis=0, tiled=True)
    arrived = arrived.reshape(fsdp_count * row_count * STEPS, block_rows)
    partial_terms = jnp.dot(arrived, weight_shard, preferred_element_type=jnp.float32)
    partial_terms = partial_terms.reshape(fsdp_count, row_count * STEPS, tp_count, head_cols)
    partial_terms = partial_terms.transpose(0, 2, 1, 3).reshape(
        fsdp_count * tp_count * row_count * STEPS, head_cols
    )
    projected = lax.psum_scatter(partial_terms, ("fsdp", "tp"), scatter_dimension=0, tiled=True)
    kv_heads = head_cols // (2 * HD)
    projected = projected.reshape(row_count, STEPS, kv_heads, 2, HD)
    positions = (lengths[:, None] + jnp.arange(STEPS, dtype=jnp.int32)[None, :]).astype(jnp.float32)
    new_keys = rotate_keys(projected[:, :, :, 0], positions[:, :, None])
    fresh = jnp.stack([new_keys, projected[:, :, :, 1]], axis=3).astype(jnp.bfloat16)
    new_kv = fresh.reshape(row_count, STEPS, head_cols)
    span_length = cache_keys.shape[1]
    grouped = queries.reshape(row_count, STEPS, kv_heads, PER_GROUP, HD)
    cached_keys = cache_keys.reshape(row_count, span_length, kv_heads, HD)
    cached_values = cache_values.reshape(row_count, span_length, kv_heads, HD)
    new_scores = (
        jnp.einsum(
            "risgd,rjsd->risgj", grouped, fresh[:, :, :, 0], preferred_element_type=jnp.float32
        )
        * score_scale
    )
    causal = jnp.arange(STEPS)[:, None] >= jnp.arange(STEPS)[None, :]
    new_scores = jnp.where(causal[None, :, None, None, :], new_scores, masked_score)
    scores = (
        jnp.einsum("risgd,rpsd->risgp", grouped, cached_keys, preferred_element_type=jnp.float32)
        * score_scale
    )
    in_range = jnp.arange(span_length, dtype=jnp.int32)[None, :] < lengths[:, None]
    all_scores = jnp.concatenate(
        [jnp.where(in_range[:, None, None, None, :], scores, masked_score), new_scores], axis=-1
    )
    highest = jnp.max(all_scores, axis=-1, keepdims=True)
    exponent = jnp.exp(all_scores - highest)
    probs = (exponent / jnp.sum(exponent, axis=-1, keepdims=True)).astype(jnp.bfloat16)
    context = jnp.einsum(
        "risgp,rpsd->risgd",
        probs[..., :span_length],
        cached_values,
        preferred_element_type=jnp.float32,
    )
    context = context + jnp.einsum(
        "risgj,rjsd->risgd",
        probs[..., span_length:],
        fresh[:, :, :, 1],
        preferred_element_type=jnp.float32,
    )
    context = context.reshape(row_count, STEPS, kv_heads * PER_GROUP * HD).astype(jnp.bfloat16)
    return (new_weights, new_moment1, new_moment2, new_kv, context)


def power_of_two(n):
    return n > 1 and n & (n - 1) == 0


def solution(mesh):
    in_specs = (
        P(("group", "fsdp"), None, None),
        P(("group", "fsdp"), None, "tp"),
        P(("group", "fsdp"), None, "tp"),
        P(("group", "fsdp"), None, "tp"),
        P(("group", "fsdp")),
        P(("fsdp", "tp"), None),
        P(("fsdp", "tp"), None),
        P(("fsdp", "tp"), None),
        P("group", ("fsdp", "tp"), None),
    )
    out_specs = (
        P(("fsdp", "tp"), None),
        P(("fsdp", "tp"), None),
        P(("fsdp", "tp"), None),
        P(("group", "fsdp"), None, "tp"),
        P(("group", "fsdp"), None, "tp"),
    )
    sizes = mesh.shape
    pairwise = power_of_two(sizes["group"]) and power_of_two(sizes["fsdp"]) and sizes["tp"] == 2
    shards = butterfly_shards if pairwise else plain_shards
    return jax.shard_map(shards, mesh=mesh, in_specs=in_specs, out_specs=out_specs, check_vma=False)
```

```python
import functools
import math

import jax
import jax.numpy as jnp
from jax import lax
from jax.experimental import pallas as pl
from jax.experimental.pallas import tpu as pltpu
from jax.sharding import PartitionSpec as P

QH = 40
KVH = 8
HD = 128
STEPS = 4
PER_GROUP = QH // KVH
HEAD_COLS = 2 * HD


beta_one = 0.9
beta_two = 0.95
learning_rate = 0.004
decay_rate = 0.1
epsilon = 1e-08
correct_one = 1.0 - 0.9**10
correct_two = 1.0 - 0.95**10
masked_score = -1e30
score_scale = 1.0 / math.sqrt(HD)
VMEM_LIMIT = 12 * 1024 * 1024


def adam_update(weights, moment1, moment2, gradient):
    new_moment1 = beta_one * moment1 + (1.0 - beta_one) * gradient
    new_moment2 = beta_two * moment2 + (1.0 - beta_two) * gradient * gradient
    direction = new_moment1 / correct_one / (jnp.sqrt(new_moment2 / correct_two) + epsilon)
    new_weights = weights - learning_rate * (direction + decay_rate * weights)
    return (new_weights, new_moment1, new_moment2)


def rotation_tables(lengths):
    half_width = HD // 2
    frequency = jnp.power(
        jnp.float32(1000000.0), -2.0 * jnp.arange(half_width, dtype=jnp.float32) / HD
    )
    positions = (lengths[:, None] + jnp.arange(STEPS, dtype=jnp.int32)[None, :]).astype(jnp.float32)
    angles = positions.reshape(-1)[:, None] * frequency
    cosine = jnp.cos(angles)
    sine = jnp.sin(angles)
    return (
        jnp.concatenate([cosine, cosine], axis=-1),
        jnp.concatenate([-sine, sine], axis=-1),
    )


def whole(a):
    return pl.BlockSpec(a.shape, lambda *_: (0,) * len(a.shape))


def after(value, *earlier):
    return lax.optimization_barrier((value, *earlier))[0] if earlier else value


def cost(busy_us):
    return pl.CostEstimate(flops=1, bytes_accessed=max(1, int(busy_us * 2.5e6)), transcendentals=0)


def in_hbm(a):
    return pltpu.with_memory_space_constraint(a, pltpu.HBM)


VMEM = pl.BlockSpec(memory_space=pltpu.VMEM)
ANYWHERE = pl.BlockSpec(memory_space=pl.ANY)


def block_columns(place, part, unit):
    half = place[0] if part == 0 else 1 - place[0]
    return pl.ds(pl.multiple_of((half * place[2] + unit) * HEAD_COLS, HEAD_COLS), HEAD_COLS)


def cast_kernel(wanted, place, source, *refs):
    outs, (buffer, sems) = refs[:-2], refs[-2:]
    blocks = [(o, k, part, unit) for o, (part, units, _) in enumerate(wanted) for k, unit in enumerate(units)]
    copies = [
        pltpu.make_async_copy(source.at[:, block_columns(place, part, unit)], buffer.at[i], sems.at[i])
        for i, (_, _, part, unit) in enumerate(blocks)
    ]
    for copy in copies:
        copy.start()
    first = [sum(w[2] for w in wanted[:o]) for o in range(len(wanted))]
    for i, (o, k, _, _) in enumerate(blocks):
        copies[i].wait()
        n_pieces = wanted[o][2]
        rows = buffer.shape[1] // n_pieces
        for p in range(n_pieces):
            piece = buffer[i, p * rows : (p + 1) * rows].astype(jnp.bfloat16)
            outs[first[o] + p][:, k * HEAD_COLS : (k + 1) * HEAD_COLS] = piece


def cast_units(place, local, wanted):
    rows = local.shape[0]
    n = sum(len(units) for _, units, _ in wanted)
    shapes = [(rows // p, len(units) * HEAD_COLS) for _, units, p in wanted for _ in range(p)]
    out = pl.pallas_call(
        functools.partial(cast_kernel, wanted),
        grid_spec=pltpu.PrefetchScalarGridSpec(
            num_scalar_prefetch=1,
            grid=(),
            in_specs=[ANYWHERE],
            out_specs=[VMEM] * len(shapes),
            scratch_shapes=[pltpu.VMEM((n, rows, HEAD_COLS), jnp.float32), pltpu.SemaphoreType.DMA((n,))],
        ),
        out_shape=[jax.ShapeDtypeStruct(shape, jnp.bfloat16) for shape in shapes],
        compiler_params=pltpu.CompilerParams(vmem_limit_bytes=VMEM_LIMIT),
        cost_estimate=cost(0),
        name="cast_units",
    )(place, in_hbm(local))
    results = []
    for _, _, p in wanted:
        results.append(out[:p])
        out = out[p:]
    return results


def join(halves):
    return jnp.concatenate([h[...] for h in halves], axis=0)


def adam_kernel(units, n_pieces, n_tok, held, projects, updates, place, *refs):
    refs = list(refs)
    take = lambda n: [refs.pop(0) for _ in range(n)]
    mine = take(1)[0]
    partner = take(n_pieces)
    state = take(1 if held else 3)
    toks = take(n_tok)
    if updates:
        take(0 if updates == 1 else 3)
        updated = take(3)
    sums = take(2) if projects else None
    in_sems = None if held else take(1)[0]
    out_sems = take(1)[0] if updates else None
    buffer = refs.pop(0) if refs else None

    n = len(units)
    columns = [block_columns(place, i // n, units[i % n]) for i in range(2 * n)]
    incoming = []
    if not held:
        for i in range(2 * n):
            incoming.append(
                [
                    pltpu.make_async_copy(state[q].at[:, columns[i]], buffer.at[q, i], in_sems.at[q, i])
                    for q in range(3)
                ]
            )
            for copy in incoming[i]:
                copy.start()
    if projects:
        tok = join(toks)
    source = state[0] if held else buffer
    totals = [mine[...], join(partner)]
    outgoing, products = [], []
    for i in range(2 * n):
        for copy in incoming[i] if incoming else ():
            copy.wait()
        at = slice((i % n) * HEAD_COLS, (i % n + 1) * HEAD_COLS)
        gradient = totals[i // n][:, at].astype(jnp.float32)
        results = adam_update(source[0, i], source[1, i], source[2, i], gradient)
        if updates:
            for q in range(3):
                buffer[q, i] = results[q]
                outgoing.append(
                    pltpu.make_async_copy(buffer.at[q, i], updated[q].at[:, columns[i]], out_sems.at[q, i])
                )
                outgoing[-1].start()
        if projects:
            products.append(
                jnp.dot(tok, results[0].astype(jnp.bfloat16), preferred_element_type=jnp.float32)
            )
    if projects:
        sent, kept = sums
        stays = place[0] == place[1]
        for k in range(n):
            at = slice(k * HEAD_COLS, (k + 1) * HEAD_COLS)
            kept[:, at] = jnp.where(stays, products[k], products[n + k])
            sent[:, at] = jnp.where(stays, products[n + k], products[k]).astype(jnp.bfloat16)
    for copy in outgoing:
        copy.wait()


def adam_units(place, total, state, toks, units, width, projects=True, updates=True, previous=None):
    mine, partner = total
    held = not isinstance(state, tuple)
    n = 2 * len(units)
    rows = mine.shape[0]
    toks = toks if projects else []
    operands = [mine, *partner]
    in_specs = [VMEM] * len(operands)
    operands += [state] if held else [in_hbm(a) for a in state]
    in_specs += [VMEM] if held else [ANYWHERE] * 3
    operands += toks
    in_specs += [VMEM] * len(toks)
    out_specs, out_shape, scratch, aliases = [], [], [], {}
    if updates:
        if previous is not None:
            aliases = {1 + len(operands) + i: i for i in range(3)}
            operands += previous
            in_specs += [ANYWHERE] * 3
        out_specs += [ANYWHERE] * 3
        out_shape += [jax.ShapeDtypeStruct((rows, width), jnp.float32)] * 3
    if projects:
        shape = (sum(t.shape[0] for t in toks), len(units) * HEAD_COLS)
        out_specs += [VMEM] * 2
        out_shape += [jax.ShapeDtypeStruct(shape, jnp.bfloat16), jax.ShapeDtypeStruct(shape, jnp.float32)]
    scratch += [pltpu.SemaphoreType.DMA((3, n))] * (int(not held) + int(updates))
    if updates or not held:
        scratch.append(pltpu.VMEM((3, n, rows, HEAD_COLS), jnp.float32))
    out = pl.pallas_call(
        functools.partial(
            adam_kernel,
            units,
            len(partner),
            len(toks),
            held,
            projects,
            0 if not updates else 1 if previous is None else 2,
        ),
        grid_spec=pltpu.PrefetchScalarGridSpec(
            num_scalar_prefetch=1, grid=(), in_specs=in_specs, out_specs=out_specs, scratch_shapes=scratch
        ),
        out_shape=out_shape,
        input_output_aliases=aliases,
        compiler_params=pltpu.CompilerParams(vmem_limit_bytes=VMEM_LIMIT),
        cost_estimate=cost(0),
        name="adam_project" if projects else "adam_update",
    )(place, *operands)
    return (out[:3] if updates else None), (out[-2:] if projects else None)


SLOT = 32


def cache_kernel(heads, lens, q, k, v, stacked, acc, stats):
    step = pl.program_id(0)
    rows = q.shape[0]
    span = k.shape[1]
    used = PER_GROUP * STEPS
    for i in range(rows):
        length = lens[step * rows + i]
        query = q[i].astype(jnp.float32)
        scores = []
        for h in range(heads):
            pieces = [
                query[:, (h * PER_GROUP + g) * HD : (h * PER_GROUP + g + 1) * HD] for g in range(PER_GROUP)
            ]
            pieces.append(jnp.zeros((SLOT - used, HD), jnp.float32))
            one = jnp.concatenate(pieces, axis=0).astype(jnp.bfloat16)
            stacked[h, i] = one
            scores.append(
                lax.dot_general(
                    one,
                    k[i, :, h * HD : (h + 1) * HD],
                    (((1,), (1,)), ((), ())),
                    preferred_element_type=jnp.float32,
                )
            )
        scores = jnp.concatenate(scores, axis=0) * score_scale
        in_range = lax.broadcasted_iota(jnp.int32, (1, span), 1) < length
        scores = jnp.where(in_range, scores, masked_score)
        highest = jnp.max(scores, axis=-1, keepdims=True)
        weight = jnp.exp(scores - highest)
        total = jnp.sum(weight, axis=-1, keepdims=True)
        weight = weight.astype(jnp.bfloat16)
        lane = lax.broadcasted_iota(jnp.int32, (heads * SLOT, HD), 1)
        stat = jnp.where(lane < HD // 2, highest, total)
        for h in range(heads):
            at = slice(h * SLOT, (h + 1) * SLOT)
            acc[h, i] = jnp.dot(
                weight[at], v[i, :, h * HD : (h + 1) * HD], preferred_element_type=jnp.float32
            )
            stats[h, i] = stat[at]


def cache_attention(queries, cache_keys, cache_values, lengths):
    row_count, span, kv_cols = cache_keys.shape
    heads = kv_cols // HD
    rows = 2 if row_count % 2 == 0 else 1
    shape = (heads, row_count, SLOT, HD)
    out_block = pl.BlockSpec((heads, rows, SLOT, HD), lambda r, lens: (0, r, 0, 0))
    in_block = lambda a: pl.BlockSpec((rows, *a.shape[1:]), lambda r, lens: (r, 0, 0))
    return pl.pallas_call(
        functools.partial(cache_kernel, heads),
        grid_spec=pltpu.PrefetchScalarGridSpec(
            num_scalar_prefetch=1,
            grid=(row_count // rows,),
            in_specs=[in_block(queries), in_block(cache_keys), in_block(cache_values)],
            out_specs=[out_block] * 3,
        ),
        out_shape=[
            jax.ShapeDtypeStruct(shape, jnp.bfloat16),
            jax.ShapeDtypeStruct(shape, jnp.float32),
            jax.ShapeDtypeStruct(shape, jnp.float32),
        ],
        compiler_params=pltpu.CompilerParams(vmem_limit_bytes=VMEM_LIMIT),
        cost_estimate=cost(0),
        name="cache_attention",
    )(lengths, in_hbm(queries), in_hbm(cache_keys), in_hbm(cache_values))


def merge_kernel(n_folds, row_count, *refs):
    folds, refs = refs[: 2 * n_folds], refs[2 * n_folds :]
    cosine, sine, stacked, acc, stats, new_kv, context = refs
    every = jnp.concatenate(
        [folds[2 * f][...].astype(jnp.float32) + folds[2 * f + 1][...] for f in range(n_folds)], axis=1
    )
    heads = stacked.shape[0]
    at = lax.broadcasted_iota(jnp.int32, (row_count * SLOT, row_count * STEPS), 0)
    to = lax.broadcasted_iota(jnp.int32, (row_count * SLOT, row_count * STEPS), 1)
    seen = (at // SLOT == to // STEPS) & (at % STEPS >= to % STEPS)
    for u in range(heads):
        total = every[:, u * HEAD_COLS : (u + 1) * HEAD_COLS]
        keys = total[:, :HD]
        keys = keys * cosine[...] + pltpu.roll(keys, HD // 2, 1) * sine[...]
        keys = keys.astype(jnp.bfloat16)
        values = total[:, HD:].astype(jnp.bfloat16)
        both = jnp.concatenate([keys, values], axis=1).astype(jnp.float32)
        for r in range(row_count):
            new_kv[r, :, u * HEAD_COLS : (u + 1) * HEAD_COLS] = both[
                r * STEPS : (r + 1) * STEPS
            ].astype(jnp.bfloat16)
        query = stacked[u].reshape(row_count * SLOT, HD)
        scores = (
            lax.dot_general(query, keys, (((1,), (1,)), ((), ())), preferred_element_type=jnp.float32)
            * score_scale
        )
        scores = jnp.where(seen, scores, masked_score)
        stat = stats[u].reshape(row_count * SLOT, HD)
        old_highest = stat[:, :1]
        old_total = stat[:, HD // 2 : HD // 2 + 1]
        highest = jnp.maximum(jnp.max(scores, axis=-1, keepdims=True), old_highest)
        weight = jnp.exp(scores - highest)
        scale = jnp.exp(old_highest - highest)
        denominator = jnp.sum(weight, axis=-1, keepdims=True) + scale * old_total
        out = jnp.dot(weight.astype(jnp.bfloat16), values, preferred_element_type=jnp.float32)
        out = (out + scale * acc[u].reshape(row_count * SLOT, HD)) / denominator
        for r in range(row_count):
            for g in range(PER_GROUP):
                at_row = r * SLOT + g * STEPS
                at_col = (u * PER_GROUP + g) * HD
                context[r, :, at_col : at_col + HD] = out[at_row : at_row + STEPS].astype(jnp.bfloat16)


def merge(folds, cosine, sine, attended):
    heads, row_count = attended[0].shape[:2]
    operands = [a for fold in folds for a in fold] + [cosine, sine, *attended]
    widths = (HEAD_COLS, PER_GROUP * HD)
    return pl.pallas_call(
        functools.partial(merge_kernel, len(folds), row_count),
        in_specs=[VMEM] * len(operands),
        out_specs=[VMEM] * 2,
        out_shape=[jax.ShapeDtypeStruct((row_count, STEPS, heads * w), jnp.bfloat16) for w in widths],
        compiler_params=pltpu.CompilerParams(vmem_limit_bytes=VMEM_LIMIT),
        cost_estimate=cost(0),
        name="merge_new",
    )(*operands)


def swap(array, axis, bit):
    size = lax.axis_size(axis)
    return lax.ppermute(array, axis, [(i, i ^ bit) for i in range(size)])


def add_rounded(a, b):
    return (a.astype(jnp.float32) + b.astype(jnp.float32)).astype(jnp.bfloat16)


def fold_rows(arrived, kept, n):
    total = arrived.astype(jnp.float32) + kept
    half = total.shape[0] // 2
    return total[half:].astype(jnp.bfloat16), total[:half]


def butterfly_shards(
    tokens, queries, cache_keys, cache_values, lengths, weights, moment1, moment2, grad_parts
):
    group_count = lax.axis_size("group")
    fsdp_count = lax.axis_size("fsdp")
    tp_count = lax.axis_size("tp")
    core = lax.axis_index("group") % 2
    fsdp = lax.axis_index("fsdp")
    tp = lax.axis_index("tp")
    rows, width = weights.shape
    row_count = tokens.shape[0]
    n_units = width // (tp_count * HEAD_COLS)
    local = grad_parts[0]
    place = jnp.stack([core, tp, jnp.full_like(core, n_units)]).astype(jnp.int32)

    crossings = [[*range(n_units // 2)], [*range(n_units // 2, n_units)]]
    crossings = [c for c in crossings if c]
    cut = 1
    folds = [range(cut), range(cut, len(crossings))]
    folds = [f for f in folds if len(f)]

    def chip_sum(away, home):
        return add_rounded(home, jnp.concatenate([swap(a, "group", 1) for a in away], axis=0))

    (away,) = cast_units(place, local, [(1, crossings[0], 1)])
    later = [u for units in crossings[1:] for u in units]
    (home,), away_later, (home_later,) = cast_units(
        place, after(local, *away), [(0, crossings[0], 1), (1, later, 4), (0, later, 1)]
    )
    first = chip_sum(away, home)
    mine, crossed = [first], [swap(first, "group", 2)]
    rest = chip_sum(away_later, home_later)
    at = 0
    for units in crossings[1:]:
        mine.append(rest[:, at * HEAD_COLS : (at + len(units)) * HEAD_COLS])
        at += len(units)
        crossed.append(swap(mine[-1], "group", 2))
    started = mine[-1]

    cosine, sine = rotation_tables(lengths)
    attended = cache_attention(after(queries, *mine), cache_keys, cache_values, lengths)

    source = after(tokens, started)
    toks = []
    for d in range(fsdp_count):
        at = ((fsdp ^ d) * tp_count + tp) * rows
        piece = lax.dynamic_slice(source, (0, 0, at), (row_count, STEPS, rows))
        toks.append(piece.reshape(1, row_count * STEPS, rows))
    distance = 1
    while distance < fsdp_count:
        stay = toks[::2]
        away = toks[1::2]
        away_all = jnp.concatenate(away, axis=0) if len(away) > 1 else away[0]
        if distance > 1:
            away_all = after(away_all, attended[1])
        got = swap(away_all, "fsdp", distance)
        got = jnp.split(got, len(away), axis=0) if len(away) > 1 else [got]
        toks = [jnp.concatenate([s, g], axis=0) for s, g in zip(stay, got)]
        distance *= 2
    toks = [toks[0].reshape(fsdp_count * row_count * STEPS, rows)]

    state = (weights, moment1, moment2)
    last = crossings[-1]

    totals, sums = [], []
    updated = None
    step = (attended[1],)
    for c, units in enumerate(crossings):
        one, other = mine[c], after(crossed[c], *step)
        bit = 2
        while True:
            one = add_rounded(one, other)
            bit *= 2
            if bit >= group_count:
                break
            other = swap(one, "group", bit)
        totals.append((one, [swap(p, "group", 1) for p in jnp.split(one, 4, axis=0)]))
        updated, both = adam_units(place, totals[c], state, toks, units, width, previous=updated)
        sums.append(both)
        step = (sums[c][0],)

    moving = []
    for members in folds:
        sent = jnp.concatenate([sums[c][0] for c in members], axis=1)
        kept = jnp.concatenate([sums[c][1] for c in members], axis=1)
        moving.append((swap(sent, "tp", 1), kept))
    distance = fsdp_count // 2
    while distance:
        for f, (got, kept) in enumerate(moving):
            sent, kept = fold_rows(got, kept, fsdp_count)
            moving[f] = (swap(sent, "fsdp", distance), kept)
        distance //= 2

    outs = merge(moving, cosine, sine, attended)
    return (*updated, *outs)


def rotate_keys(keys, positions):
    half_width = keys.shape[-1] // 2
    frequency = jnp.power(
        jnp.float32(1000000.0), -2.0 * jnp.arange(half_width, dtype=jnp.float32) / keys.shape[-1]
    )
    angles = positions[..., None] * frequency
    leading = keys[..., :half_width]
    trailing = keys[..., half_width:]
    cosine = jnp.cos(angles)
    sine_part = jnp.sin(angles)
    return jnp.concatenate(
        [leading * cosine - trailing * sine_part, trailing * cosine + leading * sine_part], axis=-1
    )


def plain_shards(
    tokens, queries, cache_keys, cache_values, lengths, weights, moment1, moment2, grad_parts
):
    gradient = lax.psum(grad_parts[0], "group")
    new_weights, new_moment1, new_moment2 = adam_update(weights, moment1, moment2, gradient)
    weight_shard = new_weights.astype(jnp.bfloat16)
    tp_count = lax.axis_size("tp")
    fsdp_count = lax.axis_size("fsdp")
    head_cols = weight_shard.shape[1] // tp_count
    row_count = tokens.shape[0]
    block_rows = weight_shard.shape[0]
    split_tokens = tokens.reshape(row_count, STEPS, fsdp_count, tp_count, block_rows)
    own_columns = lax.dynamic_index_in_dim(split_tokens, lax.axis_index("tp"), 3, keepdims=False)
    arrived = lax.all_to_all(own_columns, "fsdp", split_axis=2, concat_axis=0, tiled=True)
    arrived = arrived.reshape(fsdp_count * row_count * STEPS, block_rows)
    partial_terms = jnp.dot(arrived, weight_shard, preferred_element_type=jnp.float32)
    partial_terms = partial_terms.reshape(fsdp_count, row_count * STEPS, tp_count, head_cols)
    partial_terms = partial_terms.transpose(0, 2, 1, 3).reshape(
        fsdp_count * tp_count * row_count * STEPS, head_cols
    )
    projected = lax.psum_scatter(partial_terms, ("fsdp", "tp"), scatter_dimension=0, tiled=True)
    kv_heads = head_cols // (2 * HD)
    projected = projected.reshape(row_count, STEPS, kv_heads, 2, HD)
    positions = (lengths[:, None] + jnp.arange(STEPS, dtype=jnp.int32)[None, :]).astype(jnp.float32)
    new_keys = rotate_keys(projected[:, :, :, 0], positions[:, :, None])
    fresh = jnp.stack([new_keys, projected[:, :, :, 1]], axis=3).astype(jnp.bfloat16)
    new_kv = fresh.reshape(row_count, STEPS, head_cols)
    span_length = cache_keys.shape[1]
    grouped = queries.reshape(row_count, STEPS, kv_heads, PER_GROUP, HD)
    cached_keys = cache_keys.reshape(row_count, span_length, kv_heads, HD)
    cached_values = cache_values.reshape(row_count, span_length, kv_heads, HD)
    new_scores = (
        jnp.einsum(
            "risgd,rjsd->risgj", grouped, fresh[:, :, :, 0], preferred_element_type=jnp.float32
        )
        * score_scale
    )
    causal = jnp.arange(STEPS)[:, None] >= jnp.arange(STEPS)[None, :]
    new_scores = jnp.where(causal[None, :, None, None, :], new_scores, masked_score)
    scores = (
        jnp.einsum("risgd,rpsd->risgp", grouped, cached_keys, preferred_element_type=jnp.float32)
        * score_scale
    )
    in_range = jnp.arange(span_length, dtype=jnp.int32)[None, :] < lengths[:, None]
    all_scores = jnp.concatenate(
        [jnp.where(in_range[:, None, None, None, :], scores, masked_score), new_scores], axis=-1
    )
    highest = jnp.max(all_scores, axis=-1, keepdims=True)
    exponent = jnp.exp(all_scores - highest)
    probs = (exponent / jnp.sum(exponent, axis=-1, keepdims=True)).astype(jnp.bfloat16)
    context = jnp.einsum(
        "risgp,rpsd->risgd",
        probs[..., :span_length],
        cached_values,
        preferred_element_type=jnp.float32,
    )
    context = context + jnp.einsum(
        "risgj,rjsd->risgd",
        probs[..., span_length:],
        fresh[:, :, :, 1],
        preferred_element_type=jnp.float32,
    )
    context = context.reshape(row_count, STEPS, kv_heads * PER_GROUP * HD).astype(jnp.bfloat16)
    return (new_weights, new_moment1, new_moment2, new_kv, context)


def power_of_two(n):
    return n > 1 and n & (n - 1) == 0


def solution(mesh):
    in_specs = (
        P(("group", "fsdp"), None, None),
        P(("group", "fsdp"), None, "tp"),
        P(("group", "fsdp"), None, "tp"),
        P(("group", "fsdp"), None, "tp"),
        P(("group", "fsdp")),
        P(("fsdp", "tp"), None),
        P(("fsdp", "tp"), None),
        P(("fsdp", "tp"), None),
        P("group", ("fsdp", "tp"), None),
    )
    out_specs = (
        P(("fsdp", "tp"), None),
        P(("fsdp", "tp"), None),
        P(("fsdp", "tp"), None),
        P(("group", "fsdp"), None, "tp"),
        P(("group", "fsdp"), None, "tp"),
    )
    sizes = mesh.shape
    pairwise = power_of_two(sizes["group"]) and power_of_two(sizes["fsdp"]) and sizes["tp"] == 2
    shards = butterfly_shards if pairwise else plain_shards
    return jax.shard_map(shards, mesh=mesh, in_specs=in_specs, out_specs=out_specs, check_vma=False)
```

```python
import functools
import math

import jax
import jax.numpy as jnp
from jax import lax
from jax.experimental import pallas as pl
from jax.experimental.pallas import tpu as pltpu
from jax.sharding import PartitionSpec as P

QH = 40
KVH = 8
HD = 128
STEPS = 4
PER_GROUP = QH // KVH
HEAD_COLS = 2 * HD


beta_one = 0.9
beta_two = 0.95
learning_rate = 0.004
decay_rate = 0.1
epsilon = 1e-08
correct_one = 1.0 - 0.9**10
correct_two = 1.0 - 0.95**10
masked_score = -1e30
score_scale = 1.0 / math.sqrt(HD)
VMEM_LIMIT = 12 * 1024 * 1024


def adam_update(weights, moment1, moment2, gradient):
    new_moment1 = beta_one * moment1 + (1.0 - beta_one) * gradient
    new_moment2 = beta_two * moment2 + (1.0 - beta_two) * gradient * gradient
    direction = new_moment1 / correct_one / (jnp.sqrt(new_moment2 / correct_two) + epsilon)
    new_weights = weights - learning_rate * (direction + decay_rate * weights)
    return (new_weights, new_moment1, new_moment2)


def rotation_tables(lengths):
    half_width = HD // 2
    frequency = jnp.power(
        jnp.float32(1000000.0), -2.0 * jnp.arange(half_width, dtype=jnp.float32) / HD
    )
    positions = (lengths[:, None] + jnp.arange(STEPS, dtype=jnp.int32)[None, :]).astype(jnp.float32)
    angles = positions.reshape(-1)[:, None] * frequency
    cosine = jnp.cos(angles)
    sine = jnp.sin(angles)
    return (
        jnp.concatenate([cosine, cosine], axis=-1),
        jnp.concatenate([-sine, sine], axis=-1),
    )


def whole(a):
    return pl.BlockSpec(a.shape, lambda *_: (0,) * len(a.shape))


def after(value, *earlier):
    return lax.optimization_barrier((value, *earlier))[0] if earlier else value


def cost(busy_us):
    return pl.CostEstimate(flops=1, bytes_accessed=max(1, int(busy_us * 2.5e6)), transcendentals=0)


def in_hbm(a):
    return pltpu.with_memory_space_constraint(a, pltpu.HBM)


VMEM = pl.BlockSpec(memory_space=pltpu.VMEM)
ANYWHERE = pl.BlockSpec(memory_space=pl.ANY)


def block_columns(place, part, unit):
    half = place[0] if part == 0 else 1 - place[0]
    return pl.ds(pl.multiple_of((half * place[2] + unit) * HEAD_COLS, HEAD_COLS), HEAD_COLS)


def cast_kernel(wanted, place, source, *refs):
    outs, (buffer, sems) = refs[:-2], refs[-2:]
    blocks = [(o, k, part, unit) for o, (part, units, _) in enumerate(wanted) for k, unit in enumerate(units)]
    copies = [
        pltpu.make_async_copy(source.at[:, block_columns(place, part, unit)], buffer.at[i], sems.at[i])
        for i, (_, _, part, unit) in enumerate(blocks)
    ]
    for copy in copies:
        copy.start()
    first = [sum(w[2] for w in wanted[:o]) for o in range(len(wanted))]
    for i, (o, k, _, _) in enumerate(blocks):
        copies[i].wait()
        n_pieces = wanted[o][2]
        rows = buffer.shape[1] // n_pieces
        for p in range(n_pieces):
            piece = buffer[i, p * rows : (p + 1) * rows].astype(jnp.bfloat16)
            outs[first[o] + p][:, k * HEAD_COLS : (k + 1) * HEAD_COLS] = piece


def cast_units(place, local, wanted):
    rows = local.shape[0]
    n = sum(len(units) for _, units, _ in wanted)
    shapes = [(rows // p, len(units) * HEAD_COLS) for _, units, p in wanted for _ in range(p)]
    out = pl.pallas_call(
        functools.partial(cast_kernel, wanted),
        grid_spec=pltpu.PrefetchScalarGridSpec(
            num_scalar_prefetch=1,
            grid=(),
            in_specs=[ANYWHERE],
            out_specs=[VMEM] * len(shapes),
            scratch_shapes=[pltpu.VMEM((n, rows, HEAD_COLS), jnp.float32), pltpu.SemaphoreType.DMA((n,))],
        ),
        out_shape=[jax.ShapeDtypeStruct(shape, jnp.bfloat16) for shape in shapes],
        compiler_params=pltpu.CompilerParams(vmem_limit_bytes=VMEM_LIMIT),
        cost_estimate=cost(0),
        name="cast_units",
    )(place, in_hbm(local))
    results = []
    for _, _, p in wanted:
        results.append(out[:p])
        out = out[p:]
    return results


def sum_kernel(n_a, n_b, *refs):
    a, b, outs = refs[:n_a], refs[n_a : n_a + n_b], refs[n_a + n_b :]
    total = join(a).astype(jnp.float32) + join(b).astype(jnp.float32)
    step = total.shape[0] // len(outs)
    for p, out in enumerate(outs):
        out[...] = total[p * step : (p + 1) * step].astype(out.dtype)


def sum_pieces(a, b, n_pieces):
    rows = sum(x.shape[0] for x in a)
    return pl.pallas_call(
        functools.partial(sum_kernel, len(a), len(b)),
        in_specs=[VMEM] * (len(a) + len(b)),
        out_specs=[VMEM] * n_pieces,
        out_shape=[jax.ShapeDtypeStruct((rows // n_pieces, a[0].shape[1]), jnp.bfloat16)] * n_pieces,
        compiler_params=pltpu.CompilerParams(vmem_limit_bytes=VMEM_LIMIT),
        cost_estimate=cost(0),
        name="sum_pieces",
    )(*a, *b)


def token_kernel(n, place, source, *outs):
    rows, steps, _ = source.shape
    width = outs[0].shape[1]
    for d in range(n):
        at = pl.ds(pl.multiple_of((place[3] ^ d) * place[4] + place[5], HD), width)
        pieces = [source[r, :, at].astype(jnp.float32) for r in range(rows)]
        outs[d][...] = jnp.concatenate(pieces, axis=0).astype(jnp.bfloat16)


def token_pieces(place, tokens, n, width):
    row_count, steps, _ = tokens.shape
    return pl.pallas_call(
        functools.partial(token_kernel, n),
        grid_spec=pltpu.PrefetchScalarGridSpec(
            num_scalar_prefetch=1, grid=(), in_specs=[VMEM], out_specs=[VMEM] * n
        ),
        out_shape=[jax.ShapeDtypeStruct((row_count * steps, width), jnp.bfloat16)] * n,
        compiler_params=pltpu.CompilerParams(vmem_limit_bytes=VMEM_LIMIT),
        cost_estimate=cost(0),
        name="token_pieces",
    )(place, tokens)


def join(halves):
    return jnp.concatenate([h[...] for h in halves], axis=0)


def adam_kernel(units, n_mine, n_partner, n_tok, held, projects, updates, place, *refs):
    refs = list(refs)
    take = lambda n: [refs.pop(0) for _ in range(n)]
    mine = take(n_mine)
    partner = take(n_partner)
    state = take(1 if held else 3)
    toks = take(n_tok)
    if updates:
        take(0 if updates == 1 else 3)
        updated = take(3)
    sums = take(2) if projects else None
    in_sems = None if held else take(1)[0]
    out_sems = take(1)[0] if updates else None
    buffer = refs.pop(0) if refs else None

    n = len(units)
    columns = [block_columns(place, i // n, units[i % n]) for i in range(2 * n)]
    incoming = []
    if not held:
        for i in range(2 * n):
            incoming.append(
                [
                    pltpu.make_async_copy(state[q].at[:, columns[i]], buffer.at[q, i], in_sems.at[q, i])
                    for q in range(3)
                ]
            )
            for copy in incoming[i]:
                copy.start()
    if projects:
        tok = join(toks)
    source = state[0] if held else buffer
    totals = [join(mine), join(partner)]
    outgoing, products = [], []
    for i in range(2 * n):
        for copy in incoming[i] if incoming else ():
            copy.wait()
        at = slice((i % n) * HEAD_COLS, (i % n + 1) * HEAD_COLS)
        gradient = totals[i // n][:, at].astype(jnp.float32)
        results = adam_update(source[0, i], source[1, i], source[2, i], gradient)
        if updates:
            for q in range(3):
                buffer[q, i] = results[q]
                outgoing.append(
                    pltpu.make_async_copy(buffer.at[q, i], updated[q].at[:, columns[i]], out_sems.at[q, i])
                )
                outgoing[-1].start()
        if projects:
            products.append(
                jnp.dot(tok, results[0].astype(jnp.bfloat16), preferred_element_type=jnp.float32)
            )
    if projects:
        sent, kept = sums
        stays = place[0] == place[1]
        for k in range(n):
            at = slice(k * HEAD_COLS, (k + 1) * HEAD_COLS)
            kept[:, at] = jnp.where(stays, products[k], products[n + k])
            sent[:, at] = jnp.where(stays, products[n + k], products[k]).astype(jnp.bfloat16)
    for copy in outgoing:
        copy.wait()


def adam_units(place, total, state, toks, units, width, projects=True, updates=True, previous=None):
    mine, partner = total
    held = not isinstance(state, tuple)
    n = 2 * len(units)
    rows = sum(m.shape[0] for m in mine)
    toks = toks if projects else []
    operands = [*mine, *partner]
    in_specs = [VMEM] * len(operands)
    operands += [state] if held else [in_hbm(a) for a in state]
    in_specs += [VMEM] if held else [ANYWHERE] * 3
    operands += toks
    in_specs += [VMEM] * len(toks)
    out_specs, out_shape, scratch, aliases = [], [], [], {}
    if updates:
        if previous is not None:
            aliases = {1 + len(operands) + i: i for i in range(3)}
            operands += previous
            in_specs += [ANYWHERE] * 3
        out_specs += [ANYWHERE] * 3
        out_shape += [jax.ShapeDtypeStruct((rows, width), jnp.float32)] * 3
    if projects:
        shape = (sum(t.shape[0] for t in toks), len(units) * HEAD_COLS)
        out_specs += [VMEM] * 2
        out_shape += [jax.ShapeDtypeStruct(shape, jnp.bfloat16), jax.ShapeDtypeStruct(shape, jnp.float32)]
    scratch += [pltpu.SemaphoreType.DMA((3, n))] * (int(not held) + int(updates))
    if updates or not held:
        scratch.append(pltpu.VMEM((3, n, rows, HEAD_COLS), jnp.float32))
    out = pl.pallas_call(
        functools.partial(
            adam_kernel,
            units,
            len(mine),
            len(partner),
            len(toks),
            held,
            projects,
            0 if not updates else 1 if previous is None else 2,
        ),
        grid_spec=pltpu.PrefetchScalarGridSpec(
            num_scalar_prefetch=1, grid=(), in_specs=in_specs, out_specs=out_specs, scratch_shapes=scratch
        ),
        out_shape=out_shape,
        input_output_aliases=aliases,
        compiler_params=pltpu.CompilerParams(vmem_limit_bytes=VMEM_LIMIT),
        cost_estimate=cost(0),
        name="adam_project" if projects else "adam_update",
    )(place, *operands)
    return (out[:3] if updates else None), (out[-2:] if projects else None)


SLOT = 32


def cache_kernel(heads, lens, q, k, v, stacked, acc, stats):
    step = pl.program_id(0)
    rows = q.shape[0]
    span = k.shape[1]
    used = PER_GROUP * STEPS
    for i in range(rows):
        length = lens[step * rows + i]
        query = q[i].astype(jnp.float32)
        scores = []
        for h in range(heads):
            pieces = [
                query[:, (h * PER_GROUP + g) * HD : (h * PER_GROUP + g + 1) * HD] for g in range(PER_GROUP)
            ]
            pieces.append(jnp.zeros((SLOT - used, HD), jnp.float32))
            one = jnp.concatenate(pieces, axis=0).astype(jnp.bfloat16)
            stacked[h, i] = one
            scores.append(
                lax.dot_general(
                    one,
                    k[i, :, h * HD : (h + 1) * HD],
                    (((1,), (1,)), ((), ())),
                    preferred_element_type=jnp.float32,
                )
            )
        scores = jnp.concatenate(scores, axis=0) * score_scale
        in_range = lax.broadcasted_iota(jnp.int32, (1, span), 1) < length
        scores = jnp.where(in_range, scores, masked_score)
        highest = jnp.max(scores, axis=-1, keepdims=True)
        weight = jnp.exp(scores - highest)
        total = jnp.sum(weight, axis=-1, keepdims=True)
        weight = weight.astype(jnp.bfloat16)
        lane = lax.broadcasted_iota(jnp.int32, (heads * SLOT, HD), 1)
        stat = jnp.where(lane < HD // 2, highest, total)
        for h in range(heads):
            at = slice(h * SLOT, (h + 1) * SLOT)
            acc[h, i] = jnp.dot(
                weight[at], v[i, :, h * HD : (h + 1) * HD], preferred_element_type=jnp.float32
            )
            stats[h, i] = stat[at]


def cache_attention(queries, cache_keys, cache_values, lengths):
    row_count, span, kv_cols = cache_keys.shape
    heads = kv_cols // HD
    rows = 2 if row_count % 2 == 0 else 1
    shape = (heads, row_count, SLOT, HD)
    out_block = pl.BlockSpec((heads, rows, SLOT, HD), lambda r, lens: (0, r, 0, 0))
    in_block = lambda a: pl.BlockSpec((rows, *a.shape[1:]), lambda r, lens: (r, 0, 0))
    return pl.pallas_call(
        functools.partial(cache_kernel, heads),
        grid_spec=pltpu.PrefetchScalarGridSpec(
            num_scalar_prefetch=1,
            grid=(row_count // rows,),
            in_specs=[in_block(queries), in_block(cache_keys), in_block(cache_values)],
            out_specs=[out_block] * 3,
        ),
        out_shape=[
            jax.ShapeDtypeStruct(shape, jnp.bfloat16),
            jax.ShapeDtypeStruct(shape, jnp.float32),
            jax.ShapeDtypeStruct(shape, jnp.float32),
        ],
        compiler_params=pltpu.CompilerParams(vmem_limit_bytes=VMEM_LIMIT),
        cost_estimate=cost(0),
        name="cache_attention",
    )(lengths, in_hbm(queries), in_hbm(cache_keys), in_hbm(cache_values))


def merge_kernel(n_folds, row_count, *refs):
    folds, refs = refs[: 2 * n_folds], refs[2 * n_folds :]
    cosine, sine, stacked, acc, stats, new_kv, context = refs
    every = jnp.concatenate(
        [folds[2 * f][...].astype(jnp.float32) + folds[2 * f + 1][...] for f in range(n_folds)], axis=1
    )
    heads = stacked.shape[0]
    at = lax.broadcasted_iota(jnp.int32, (row_count * SLOT, row_count * STEPS), 0)
    to = lax.broadcasted_iota(jnp.int32, (row_count * SLOT, row_count * STEPS), 1)
    seen = (at // SLOT == to // STEPS) & (at % STEPS >= to % STEPS)
    for u in range(heads):
        total = every[:, u * HEAD_COLS : (u + 1) * HEAD_COLS]
        keys = total[:, :HD]
        keys = keys * cosine[...] + pltpu.roll(keys, HD // 2, 1) * sine[...]
        keys = keys.astype(jnp.bfloat16)
        values = total[:, HD:].astype(jnp.bfloat16)
        both = jnp.concatenate([keys, values], axis=1).astype(jnp.float32)
        for r in range(row_count):
            new_kv[r, :, u * HEAD_COLS : (u + 1) * HEAD_COLS] = both[
                r * STEPS : (r + 1) * STEPS
            ].astype(jnp.bfloat16)
        query = stacked[u].reshape(row_count * SLOT, HD)
        scores = (
            lax.dot_general(query, keys, (((1,), (1,)), ((), ())), preferred_element_type=jnp.float32)
            * score_scale
        )
        scores = jnp.where(seen, scores, masked_score)
        stat = stats[u].reshape(row_count * SLOT, HD)
        old_highest = stat[:, :1]
        old_total = stat[:, HD // 2 : HD // 2 + 1]
        highest = jnp.maximum(jnp.max(scores, axis=-1, keepdims=True), old_highest)
        weight = jnp.exp(scores - highest)
        scale = jnp.exp(old_highest - highest)
        denominator = jnp.sum(weight, axis=-1, keepdims=True) + scale * old_total
        out = jnp.dot(weight.astype(jnp.bfloat16), values, preferred_element_type=jnp.float32)
        out = (out + scale * acc[u].reshape(row_count * SLOT, HD)) / denominator
        for r in range(row_count):
            for g in range(PER_GROUP):
                at_row = r * SLOT + g * STEPS
                at_col = (u * PER_GROUP + g) * HD
                context[r, :, at_col : at_col + HD] = out[at_row : at_row + STEPS].astype(jnp.bfloat16)


def merge(folds, cosine, sine, attended):
    heads, row_count = attended[0].shape[:2]
    operands = [a for fold in folds for a in fold] + [cosine, sine, *attended]
    widths = (HEAD_COLS, PER_GROUP * HD)
    return pl.pallas_call(
        functools.partial(merge_kernel, len(folds), row_count),
        in_specs=[VMEM] * len(operands),
        out_specs=[VMEM] * 2,
        out_shape=[jax.ShapeDtypeStruct((row_count, STEPS, heads * w), jnp.bfloat16) for w in widths],
        compiler_params=pltpu.CompilerParams(vmem_limit_bytes=VMEM_LIMIT),
        cost_estimate=cost(0),
        name="merge_new",
    )(*operands)


def swap(array, axis, bit):
    size = lax.axis_size(axis)
    return lax.ppermute(array, axis, [(i, i ^ bit) for i in range(size)])


def fold_rows(arrived, kept, n):
    total = arrived.astype(jnp.float32) + kept
    half = total.shape[0] // 2
    return total[half:].astype(jnp.bfloat16), total[:half]


def butterfly_shards(
    tokens, queries, cache_keys, cache_values, lengths, weights, moment1, moment2, grad_parts
):
    group_count = lax.axis_size("group")
    fsdp_count = lax.axis_size("fsdp")
    tp_count = lax.axis_size("tp")
    core = lax.axis_index("group") % 2
    fsdp = lax.axis_index("fsdp")
    tp = lax.axis_index("tp")
    rows, width = weights.shape
    row_count = tokens.shape[0]
    n_units = width // (tp_count * HEAD_COLS)
    local = grad_parts[0]
    place = jnp.stack(
        [core, tp, jnp.full_like(core, n_units), fsdp, jnp.full_like(core, tp_count * rows), tp * rows]
    ).astype(jnp.int32)

    crossings = [[*range(n_units // 2)], [*range(n_units // 2, n_units)]]
    crossings = [c for c in crossings if c]
    cut = 1
    folds = [range(cut), range(cut, len(crossings))]
    folds = [f for f in folds if len(f)]

    pieces = [1] + [4] * (len(crossings) - 1)
    cast = cast_units(
        place, local, [(part, units, p if part else 1) for units, p in zip(crossings, pieces) for part in (1, 0)]
    )
    mine, crossed = [], []
    for away, home in zip(cast[::2], cast[1::2]):
        (one,) = sum_pieces(home, [swap(a, "group", 1) for a in away], 1)
        mine.append(one)
        crossed.append(swap(one, "group", 2))

    toks = token_pieces(place, after(tokens, *mine), fsdp_count, rows)
    cosine, sine = rotation_tables(lengths)
    attended = cache_attention(after(queries, *mine), cache_keys, cache_values, lengths)
    distance = 1
    while distance < fsdp_count:
        toks = [swap(t, "fsdp", distance) if d & distance else t for d, t in enumerate(toks)]
        if distance == 1:
            toks = list(lax.optimization_barrier((*toks, attended[1])))[:-1]
        distance *= 2

    state = (weights, moment1, moment2)
    last = crossings[-1]

    totals, sums = [], []
    updated = None
    step = (attended[1],)
    for c, units in enumerate(crossings):
        one, other = [mine[c]], after(crossed[c], *step)
        bit = 2
        while True:
            bit *= 2
            one = sum_pieces(one, [other], 4 if bit >= group_count else 1)
            if bit >= group_count:
                break
            other = swap(one[0], "group", bit)
        totals.append((one, [swap(p, "group", 1) for p in one]))
        updated, both = adam_units(place, totals[c], state, toks, units, width, previous=updated)
        sums.append(both)
        step = (sums[c][0],)

    moving = []
    for members in folds:
        sent = jnp.concatenate([sums[c][0] for c in members], axis=1)
        kept = jnp.concatenate([sums[c][1] for c in members], axis=1)
        moving.append((swap(sent, "tp", 1), kept))
    distance = fsdp_count // 2
    while distance:
        for f, (got, kept) in enumerate(moving):
            sent, kept = fold_rows(got, kept, fsdp_count)
            moving[f] = (swap(sent, "fsdp", distance), kept)
        distance //= 2

    outs = merge(moving, cosine, sine, attended)
    return (*updated, *outs)


def rotate_keys(keys, positions):
    half_width = keys.shape[-1] // 2
    frequency = jnp.power(
        jnp.float32(1000000.0), -2.0 * jnp.arange(half_width, dtype=jnp.float32) / keys.shape[-1]
    )
    angles = positions[..., None] * frequency
    leading = keys[..., :half_width]
    trailing = keys[..., half_width:]
    cosine = jnp.cos(angles)
    sine_part = jnp.sin(angles)
    return jnp.concatenate(
        [leading * cosine - trailing * sine_part, trailing * cosine + leading * sine_part], axis=-1
    )


def plain_shards(
    tokens, queries, cache_keys, cache_values, lengths, weights, moment1, moment2, grad_parts
):
    gradient = lax.psum(grad_parts[0], "group")
    new_weights, new_moment1, new_moment2 = adam_update(weights, moment1, moment2, gradient)
    weight_shard = new_weights.astype(jnp.bfloat16)
    tp_count = lax.axis_size("tp")
    fsdp_count = lax.axis_size("fsdp")
    head_cols = weight_shard.shape[1] // tp_count
    row_count = tokens.shape[0]
    block_rows = weight_shard.shape[0]
    split_tokens = tokens.reshape(row_count, STEPS, fsdp_count, tp_count, block_rows)
    own_columns = lax.dynamic_index_in_dim(split_tokens, lax.axis_index("tp"), 3, keepdims=False)
    arrived = lax.all_to_all(own_columns, "fsdp", split_axis=2, concat_axis=0, tiled=True)
    arrived = arrived.reshape(fsdp_count * row_count * STEPS, block_rows)
    partial_terms = jnp.dot(arrived, weight_shard, preferred_element_type=jnp.float32)
    partial_terms = partial_terms.reshape(fsdp_count, row_count * STEPS, tp_count, head_cols)
    partial_terms = partial_terms.transpose(0, 2, 1, 3).reshape(
        fsdp_count * tp_count * row_count * STEPS, head_cols
    )
    projected = lax.psum_scatter(partial_terms, ("fsdp", "tp"), scatter_dimension=0, tiled=True)
    kv_heads = head_cols // (2 * HD)
    projected = projected.reshape(row_count, STEPS, kv_heads, 2, HD)
    positions = (lengths[:, None] + jnp.arange(STEPS, dtype=jnp.int32)[None, :]).astype(jnp.float32)
    new_keys = rotate_keys(projected[:, :, :, 0], positions[:, :, None])
    fresh = jnp.stack([new_keys, projected[:, :, :, 1]], axis=3).astype(jnp.bfloat16)
    new_kv = fresh.reshape(row_count, STEPS, head_cols)
    span_length = cache_keys.shape[1]
    grouped = queries.reshape(row_count, STEPS, kv_heads, PER_GROUP, HD)
    cached_keys = cache_keys.reshape(row_count, span_length, kv_heads, HD)
    cached_values = cache_values.reshape(row_count, span_length, kv_heads, HD)
    new_scores = (
        jnp.einsum(
            "risgd,rjsd->risgj", grouped, fresh[:, :, :, 0], preferred_element_type=jnp.float32
        )
        * score_scale
    )
    causal = jnp.arange(STEPS)[:, None] >= jnp.arange(STEPS)[None, :]
    new_scores = jnp.where(causal[None, :, None, None, :], new_scores, masked_score)
    scores = (
        jnp.einsum("risgd,rpsd->risgp", grouped, cached_keys, preferred_element_type=jnp.float32)
        * score_scale
    )
    in_range = jnp.arange(span_length, dtype=jnp.int32)[None, :] < lengths[:, None]
    all_scores = jnp.concatenate(
        [jnp.where(in_range[:, None, None, None, :], scores, masked_score), new_scores], axis=-1
    )
    highest = jnp.max(all_scores, axis=-1, keepdims=True)
    exponent = jnp.exp(all_scores - highest)
    probs = (exponent / jnp.sum(exponent, axis=-1, keepdims=True)).astype(jnp.bfloat16)
    context = jnp.einsum(
        "risgp,rpsd->risgd",
        probs[..., :span_length],
        cached_values,
        preferred_element_type=jnp.float32,
    )
    context = context + jnp.einsum(
        "risgj,rjsd->risgd",
        probs[..., span_length:],
        fresh[:, :, :, 1],
        preferred_element_type=jnp.float32,
    )
    context = context.reshape(row_count, STEPS, kv_heads * PER_GROUP * HD).astype(jnp.bfloat16)
    return (new_weights, new_moment1, new_moment2, new_kv, context)


def power_of_two(n):
    return n > 1 and n & (n - 1) == 0


def solution(mesh):
    in_specs = (
        P(("group", "fsdp"), None, None),
        P(("group", "fsdp"), None, "tp"),
        P(("group", "fsdp"), None, "tp"),
        P(("group", "fsdp"), None, "tp"),
        P(("group", "fsdp")),
        P(("fsdp", "tp"), None),
        P(("fsdp", "tp"), None),
        P(("fsdp", "tp"), None),
        P("group", ("fsdp", "tp"), None),
    )
    out_specs = (
        P(("fsdp", "tp"), None),
        P(("fsdp", "tp"), None),
        P(("fsdp", "tp"), None),
        P(("group", "fsdp"), None, "tp"),
        P(("group", "fsdp"), None, "tp"),
    )
    sizes = mesh.shape
    pairwise = power_of_two(sizes["group"]) and power_of_two(sizes["fsdp"]) and sizes["tp"] == 2
    shards = butterfly_shards if pairwise else plain_shards
    return jax.shard_map(shards, mesh=mesh, in_specs=in_specs, out_specs=out_specs, check_vma=False)
```

```python
import functools
import math

import jax
import jax.numpy as jnp
from jax import lax
from jax.experimental import pallas as pl
from jax.experimental.pallas import tpu as pltpu
from jax.sharding import PartitionSpec as P

QH = 40
KVH = 8
HD = 128
STEPS = 4
PER_GROUP = QH // KVH
HEAD_COLS = 2 * HD


beta_one = 0.9
beta_two = 0.95
learning_rate = 0.004
decay_rate = 0.1
epsilon = 1e-08
correct_one = 1.0 - 0.9**10
correct_two = 1.0 - 0.95**10
masked_score = -1e30
score_scale = 1.0 / math.sqrt(HD)
N_PIECES = 2
MIB = 1024 * 1024


def adam_update(weights, moment1, moment2, gradient):
    new_moment1 = beta_one * moment1 + (1.0 - beta_one) * gradient
    new_moment2 = beta_two * moment2 + (1.0 - beta_two) * gradient * gradient
    direction = new_moment1 / correct_one / (jnp.sqrt(new_moment2 / correct_two) + epsilon)
    new_weights = weights - learning_rate * (direction + decay_rate * weights)
    return (new_weights, new_moment1, new_moment2)


def rotation_tables(lengths):
    half_width = HD // 2
    frequency = jnp.power(
        jnp.float32(1000000.0), -2.0 * jnp.arange(half_width, dtype=jnp.float32) / HD
    )
    positions = (lengths[:, None] + jnp.arange(STEPS, dtype=jnp.int32)[None, :]).astype(jnp.float32)
    angles = positions.reshape(-1)[:, None] * frequency
    cosine = jnp.cos(angles)
    sine = jnp.sin(angles)
    return (
        jnp.concatenate([cosine, cosine], axis=-1),
        jnp.concatenate([-sine, sine], axis=-1),
    )


def whole(a):
    return pl.BlockSpec(a.shape, lambda *_: (0,) * len(a.shape))


def after(value, *earlier):
    return lax.optimization_barrier((value, *earlier))[0] if earlier else value


def cost(busy_us):
    return pl.CostEstimate(flops=1, bytes_accessed=max(1, int(busy_us * 2.5e6)), transcendentals=0)


def in_hbm(a):
    return pltpu.with_memory_space_constraint(a, pltpu.HBM)


VMEM = pl.BlockSpec(memory_space=pltpu.VMEM)
ANYWHERE = pl.BlockSpec(memory_space=pl.ANY)


def block_columns(place, part, unit):
    half = place[0] if part == 0 else 1 - place[0]
    return pl.ds(pl.multiple_of((half * place[2] + unit) * HEAD_COLS, HEAD_COLS), HEAD_COLS)


def cast_kernel(wanted, n_units, source, *refs):
    place = (lax.axis_index("group") % 2, None, n_units)
    outs, (buffer, sems) = refs[:-2], refs[-2:]
    blocks = [(o, k, part, unit) for o, (part, units, _) in enumerate(wanted) for k, unit in enumerate(units)]
    copies = [
        pltpu.make_async_copy(source.at[:, block_columns(place, part, unit)], buffer.at[i], sems.at[i])
        for i, (_, _, part, unit) in enumerate(blocks)
    ]
    for copy in copies:
        copy.start()
    first = [sum(w[2] for w in wanted[:o]) for o in range(len(wanted))]
    for i, (o, k, _, _) in enumerate(blocks):
        copies[i].wait()
        n_pieces = wanted[o][2]
        rows = buffer.shape[1] // n_pieces
        for p in range(n_pieces):
            piece = buffer[i, p * rows : (p + 1) * rows].astype(jnp.bfloat16)
            outs[first[o] + p][:, k * HEAD_COLS : (k + 1) * HEAD_COLS] = piece


def cast_units(local, n_units, wanted):
    rows = local.shape[0]
    n = sum(len(units) for _, units, _ in wanted)
    shapes = [(rows // p, len(units) * HEAD_COLS) for _, units, p in wanted for _ in range(p)]
    out = pl.pallas_call(
        functools.partial(cast_kernel, wanted, n_units),
        in_specs=[ANYWHERE],
        out_specs=[VMEM] * len(shapes),
        scratch_shapes=[pltpu.VMEM((n, rows, HEAD_COLS), jnp.float32), pltpu.SemaphoreType.DMA((n,))],
        out_shape=[jax.ShapeDtypeStruct(shape, jnp.bfloat16) for shape in shapes],
        compiler_params=pltpu.CompilerParams(vmem_limit_bytes=6 * MIB),
        cost_estimate=cost(0),
        name="cast_units",
    )(in_hbm(local))
    results = []
    for _, _, p in wanted:
        results.append(out[:p])
        out = out[p:]
    return results


def sum_kernel(n_a, n_b, *refs):
    a, b, outs = refs[:n_a], refs[n_a : n_a + n_b], refs[n_a + n_b :]
    total = join(a).astype(jnp.float32) + join(b).astype(jnp.float32)
    step = total.shape[0] // len(outs)
    for p, out in enumerate(outs):
        out[...] = total[p * step : (p + 1) * step].astype(out.dtype)


def sum_pieces(a, b, n_pieces):
    rows = sum(x.shape[0] for x in a)
    return pl.pallas_call(
        functools.partial(sum_kernel, len(a), len(b)),
        in_specs=[VMEM] * (len(a) + len(b)),
        out_specs=[VMEM] * n_pieces,
        out_shape=[jax.ShapeDtypeStruct((rows // n_pieces, a[0].shape[1]), jnp.bfloat16)] * n_pieces,
        compiler_params=pltpu.CompilerParams(vmem_limit_bytes=6 * MIB),
        cost_estimate=cost(0),
        name="sum_pieces",
    )(*a, *b)


def token_kernel(n, place, source, *outs):
    rows, steps, _ = source.shape
    width = outs[0].shape[1]
    for d in range(n):
        at = pl.ds(pl.multiple_of((place[3] ^ d) * place[4] + place[5], HD), width)
        pieces = [source[r, :, at].astype(jnp.float32) for r in range(rows)]
        outs[d][...] = jnp.concatenate(pieces, axis=0).astype(jnp.bfloat16)


def token_pieces(place, tokens, n, width):
    row_count, steps, _ = tokens.shape
    return pl.pallas_call(
        functools.partial(token_kernel, n),
        grid_spec=pltpu.PrefetchScalarGridSpec(
            num_scalar_prefetch=1, grid=(), in_specs=[VMEM], out_specs=[VMEM] * n
        ),
        out_shape=[jax.ShapeDtypeStruct((row_count * steps, width), jnp.bfloat16)] * n,
        compiler_params=pltpu.CompilerParams(vmem_limit_bytes=4 * MIB),
        cost_estimate=cost(0),
        name="token_pieces",
    )(place, tokens)


def join(halves):
    return jnp.concatenate([h[...] for h in halves], axis=0)


def adam_kernel(units, n_mine, n_partner, n_tok, held, projects, updates, place, *refs):
    refs = list(refs)
    take = lambda n: [refs.pop(0) for _ in range(n)]
    mine = take(n_mine)
    partner = take(n_partner)
    state = take(1 if held else 3)
    toks = take(n_tok)
    if updates:
        take(0 if updates == 1 else 3)
        updated = take(3)
    sums = take(2) if projects else None
    in_sems = None if held else take(1)[0]
    out_sems = take(1)[0] if updates else None
    buffer = refs.pop(0) if refs else None

    n = len(units)
    columns = [block_columns(place, i // n, units[i % n]) for i in range(2 * n)]
    incoming = []
    if not held:
        for i in range(2 * n):
            incoming.append(
                [
                    pltpu.make_async_copy(state[q].at[:, columns[i]], buffer.at[q, i], in_sems.at[q, i])
                    for q in range(3)
                ]
            )
            for copy in incoming[i]:
                copy.start()
    if projects:
        tok = join(toks)
    source = state[0] if held else buffer
    totals = [join(mine), join(partner)]
    outgoing, products = [], []
    for i in range(2 * n):
        for copy in incoming[i] if incoming else ():
            copy.wait()
        at = slice((i % n) * HEAD_COLS, (i % n + 1) * HEAD_COLS)
        gradient = totals[i // n][:, at].astype(jnp.float32)
        results = adam_update(source[0, i], source[1, i], source[2, i], gradient)
        if updates:
            for q in range(3):
                buffer[q, i] = results[q]
                outgoing.append(
                    pltpu.make_async_copy(buffer.at[q, i], updated[q].at[:, columns[i]], out_sems.at[q, i])
                )
                outgoing[-1].start()
        if projects:
            products.append(
                jnp.dot(tok, results[0].astype(jnp.bfloat16), preferred_element_type=jnp.float32)
            )
    if projects:
        sent, kept = sums
        stays = place[0] == place[1]
        for k in range(n):
            at = slice(k * HEAD_COLS, (k + 1) * HEAD_COLS)
            kept[:, at] = jnp.where(stays, products[k], products[n + k])
            sent[:, at] = jnp.where(stays, products[n + k], products[k]).astype(jnp.bfloat16)
    for copy in outgoing:
        copy.wait()


def adam_units(place, total, state, toks, units, width, projects=True, updates=True, previous=None):
    mine, partner = total
    held = not isinstance(state, tuple)
    n = 2 * len(units)
    rows = sum(m.shape[0] for m in mine)
    toks = toks if projects else []
    operands = [*mine, *partner]
    in_specs = [VMEM] * len(operands)
    operands += [state] if held else [in_hbm(a) for a in state]
    in_specs += [VMEM] if held else [ANYWHERE] * 3
    operands += toks
    in_specs += [VMEM] * len(toks)
    out_specs, out_shape, scratch, aliases = [], [], [], {}
    if updates:
        if previous is not None:
            aliases = {1 + len(operands) + i: i for i in range(3)}
            operands += previous
            in_specs += [ANYWHERE] * 3
        out_specs += [ANYWHERE] * 3
        out_shape += [jax.ShapeDtypeStruct((rows, width), jnp.float32)] * 3
    if projects:
        shape = (sum(t.shape[0] for t in toks), len(units) * HEAD_COLS)
        out_specs += [VMEM] * 2
        out_shape += [jax.ShapeDtypeStruct(shape, jnp.bfloat16), jax.ShapeDtypeStruct(shape, jnp.float32)]
    scratch += [pltpu.SemaphoreType.DMA((3, n))] * (int(not held) + int(updates))
    if updates or not held:
        scratch.append(pltpu.VMEM((3, n, rows, HEAD_COLS), jnp.float32))
    out = pl.pallas_call(
        functools.partial(
            adam_kernel,
            units,
            len(mine),
            len(partner),
            len(toks),
            held,
            projects,
            0 if not updates else 1 if previous is None else 2,
        ),
        grid_spec=pltpu.PrefetchScalarGridSpec(
            num_scalar_prefetch=1, grid=(), in_specs=in_specs, out_specs=out_specs, scratch_shapes=scratch
        ),
        out_shape=out_shape,
        input_output_aliases=aliases,
        compiler_params=pltpu.CompilerParams(vmem_limit_bytes=12 * MIB),
        cost_estimate=cost(0),
        name="adam_project" if projects else "adam_update",
    )(place, *operands)
    return (out[:3] if updates else None), (out[-2:] if projects else None)


SLOT = 32


def cache_kernel(heads, first, lens, q, k, v, stacked, acc, stats):
    step = pl.program_id(0)
    rows = q.shape[0]
    span = k.shape[1]
    used = PER_GROUP * STEPS
    for i in range(rows):
        length = lens[first + step * rows + i]
        query = q[i].astype(jnp.float32)
        scores = []
        for h in range(heads):
            pieces = [
                query[:, (h * PER_GROUP + g) * HD : (h * PER_GROUP + g + 1) * HD] for g in range(PER_GROUP)
            ]
            pieces.append(jnp.zeros((SLOT - used, HD), jnp.float32))
            one = jnp.concatenate(pieces, axis=0).astype(jnp.bfloat16)
            stacked[h, i] = one
            scores.append(
                lax.dot_general(
                    one,
                    k[i, :, h * HD : (h + 1) * HD],
                    (((1,), (1,)), ((), ())),
                    preferred_element_type=jnp.float32,
                )
            )
        scores = jnp.concatenate(scores, axis=0) * score_scale
        in_range = lax.broadcasted_iota(jnp.int32, (1, span), 1) < length
        scores = jnp.where(in_range, scores, masked_score)
        highest = jnp.max(scores, axis=-1, keepdims=True)
        weight = jnp.exp(scores - highest)
        total = jnp.sum(weight, axis=-1, keepdims=True)
        weight = weight.astype(jnp.bfloat16)
        lane = lax.broadcasted_iota(jnp.int32, (heads * SLOT, HD), 1)
        stat = jnp.where(lane < HD // 2, highest, total)
        for h in range(heads):
            at = slice(h * SLOT, (h + 1) * SLOT)
            acc[h, i] = jnp.dot(
                weight[at], v[i, :, h * HD : (h + 1) * HD], preferred_element_type=jnp.float32
            )
            stats[h, i] = stat[at]


def cache_attention(queries, cache_keys, cache_values, lengths, first, row_count):
    _, span, kv_cols = cache_keys.shape
    heads = kv_cols // HD
    rows = 2 if row_count % 2 == 0 and first % 2 == 0 else 1
    shape = (heads, row_count, SLOT, HD)
    out_block = pl.BlockSpec((heads, rows, SLOT, HD), lambda r, lens: (0, r, 0, 0))
    in_block = lambda a: pl.BlockSpec((rows, *a.shape[1:]), lambda r, lens: (first // rows + r, 0, 0))
    return pl.pallas_call(
        functools.partial(cache_kernel, heads, first),
        grid_spec=pltpu.PrefetchScalarGridSpec(
            num_scalar_prefetch=1,
            grid=(row_count // rows,),
            in_specs=[in_block(queries), in_block(cache_keys), in_block(cache_values)],
            out_specs=[out_block] * 3,
        ),
        out_shape=[
            jax.ShapeDtypeStruct(shape, jnp.bfloat16),
            jax.ShapeDtypeStruct(shape, jnp.float32),
            jax.ShapeDtypeStruct(shape, jnp.float32),
        ],
        compiler_params=pltpu.CompilerParams(vmem_limit_bytes=10 * MIB),
        cost_estimate=cost(7),
        name="cache_attention",
    )(lengths, in_hbm(queries), in_hbm(cache_keys), in_hbm(cache_values))


def merge_kernel(n_parts, *refs):
    arrived, kept, cosine, sine = refs[:4]
    stacked, acc, stats = (refs[4 + i : 4 + 3 * n_parts : 3] for i in range(3))
    new_kv, context = refs[-2:]
    row_count = new_kv.shape[0]
    every = arrived[...].astype(jnp.float32) + kept[...]
    at = lax.broadcasted_iota(jnp.int32, (row_count * SLOT, row_count * STEPS), 0)
    to = lax.broadcasted_iota(jnp.int32, (row_count * SLOT, row_count * STEPS), 1)
    seen = (at // SLOT == to // STEPS) & (at % STEPS >= to % STEPS)
    rows_of = lambda parts, u: jnp.concatenate([p[u].reshape(-1, HD) for p in parts], axis=0)
    for u in range(stacked[0].shape[0]):
        total = every[:, u * HEAD_COLS : (u + 1) * HEAD_COLS]
        keys = total[:, :HD]
        keys = keys * cosine[...] + pltpu.roll(keys, HD // 2, 1) * sine[...]
        keys = keys.astype(jnp.bfloat16)
        values = total[:, HD:].astype(jnp.bfloat16)
        both = jnp.concatenate([keys, values], axis=1).astype(jnp.float32)
        for r in range(row_count):
            new_kv[r, :, u * HEAD_COLS : (u + 1) * HEAD_COLS] = both[
                r * STEPS : (r + 1) * STEPS
            ].astype(jnp.bfloat16)
        scores = (
            lax.dot_general(
                rows_of(stacked, u), keys, (((1,), (1,)), ((), ())), preferred_element_type=jnp.float32
            )
            * score_scale
        )
        scores = jnp.where(seen, scores, masked_score)
        stat = rows_of(stats, u)
        old_highest = stat[:, :1]
        old_total = stat[:, HD // 2 : HD // 2 + 1]
        highest = jnp.maximum(jnp.max(scores, axis=-1, keepdims=True), old_highest)
        weight = jnp.exp(scores - highest)
        scale = jnp.exp(old_highest - highest)
        denominator = jnp.sum(weight, axis=-1, keepdims=True) + scale * old_total
        out = jnp.dot(weight.astype(jnp.bfloat16), values, preferred_element_type=jnp.float32)
        out = (out + scale * rows_of(acc, u)) / denominator
        for r in range(row_count):
            for g in range(PER_GROUP):
                at_row = r * SLOT + g * STEPS
                at_col = (u * PER_GROUP + g) * HD
                context[r, :, at_col : at_col + HD] = out[at_row : at_row + STEPS].astype(jnp.bfloat16)


def merge(arrived, kept, cosine, sine, attended, row_count, first, n_units, previous):
    heads = attended[0][0].shape[0]
    block = first // n_units
    operands = [arrived, kept, cosine, sine]
    in_specs = [whole(a) for a in operands]
    for part in attended:
        operands += part
        in_specs += [pl.BlockSpec((n_units, *p.shape[1:]), lambda i: (block, 0, 0, 0)) for p in part]
    aliases = {}
    if previous is not None:
        aliases = {len(operands) + i: i for i in range(2)}
        operands += previous
        in_specs += [ANYWHERE] * 2
    widths = (HEAD_COLS, PER_GROUP * HD)
    return pl.pallas_call(
        functools.partial(merge_kernel, len(attended)),
        grid=(1,),
        in_specs=in_specs,
        out_specs=[pl.BlockSpec((row_count, STEPS, n_units * w), lambda i: (0, 0, block)) for w in widths],
        out_shape=[jax.ShapeDtypeStruct((row_count, STEPS, heads * w), jnp.bfloat16) for w in widths],
        input_output_aliases=aliases,
        compiler_params=pltpu.CompilerParams(vmem_limit_bytes=8 * MIB),
        cost_estimate=cost(0),
        name="merge_new",
    )(*operands)


def swap(array, axis, bit):
    size = lax.axis_size(axis)
    return lax.ppermute(array, axis, [(i, i ^ bit) for i in range(size)])


def reversed_bits(n):
    order = [0]
    while len(order) < n:
        order = [2 * i for i in order] + [2 * i + 1 for i in order]
    return order


def fold_rows(arrived, kept, n):
    total = arrived.astype(jnp.float32) + kept
    half = total.shape[0] // 2
    return total[half:].astype(jnp.bfloat16), total[:half]


def butterfly_shards(
    tokens, queries, cache_keys, cache_values, lengths, weights, moment1, moment2, grad_parts
):
    group_count = lax.axis_size("group")
    fsdp_count = lax.axis_size("fsdp")
    tp_count = lax.axis_size("tp")
    core = lax.axis_index("group") % 2
    fsdp = lax.axis_index("fsdp")
    tp = lax.axis_index("tp")
    rows, width = weights.shape
    row_count = tokens.shape[0]
    n_units = width // (tp_count * HEAD_COLS)
    local = grad_parts[0]
    place = jnp.stack(
        [core, tp, jnp.full_like(core, n_units), fsdp, jnp.full_like(core, tp_count * rows), tp * rows]
    ).astype(jnp.int32)

    crossings = [[*range(n_units // 2)], [*range(n_units // 2, n_units)]]
    crossings = [c for c in crossings if c]
    cut = 1
    folds = [range(cut), range(cut, len(crossings))]
    folds = [f for f in folds if len(f)]

    pieces = [1] + [N_PIECES] * (len(crossings) - 1)
    mine, crossed, toks = [], [], None
    distance = 1
    for units, p in zip(crossings, pieces):
        away, home = cast_units(after(local, *mine), n_units, [(1, units, p), (0, units, 1)])
        got = [swap(a, "group", 1) for a in away]
        if toks is None:
            toks = token_pieces(place, after(tokens, *away), fsdp_count, rows)
            home = [after(home[0], *toks)]
        (one,) = sum_pieces(home, got, 1)
        mine.append(one)
        crossed.append(swap(one, "group", 2))
        if distance == 1:
            toks = [swap(t, "fsdp", distance) if d & distance else t for d, t in enumerate(toks)]
            distance *= 2
    cosine, sine = rotation_tables(lengths)
    attended = [
        cache_attention(after(queries, *mine, *toks), cache_keys, cache_values, lengths, 0, row_count)
    ]
    while distance < fsdp_count:
        toks = [swap(t, "fsdp", distance) if d & distance else t for d, t in enumerate(toks)]
        distance *= 2
    toks = [toks[d] for d in reversed_bits(fsdp_count)]

    state = (weights, moment1, moment2)
    last = crossings[-1]

    totals, sums = [], []
    updated = None
    step = (attended[0][1], *toks)
    for c, units in enumerate(crossings):
        one, other = [mine[c]], after(crossed[c], *step)
        bit = 2
        while True:
            bit *= 2
            one = sum_pieces(one, [other], N_PIECES if bit >= group_count else 1)
            if bit >= group_count:
                break
            other = swap(one[0], "group", bit)
        totals.append((one, [swap(p, "group", 1) for p in one]))
        updated, both = adam_units(place, totals[c], state, toks, units, width, previous=updated)
        sums.append(both)
        step = (sums[c][0],)

    moving = []
    for members in folds:
        sent = jnp.concatenate([sums[c][0] for c in members], axis=1)
        kept = jnp.concatenate([sums[c][1] for c in members], axis=1)
        moving.append((swap(sent, "tp", 1), kept))
    distance = 1
    while distance < fsdp_count:
        for f, (got, kept) in enumerate(moving):
            sent, kept = fold_rows(got, kept, fsdp_count)
            moving[f] = (swap(sent, "fsdp", distance), kept)
        distance *= 2

    outs = None
    for members, (got, kept) in zip(folds, moving):
        units = [u for c in members for u in crossings[c]]
        outs = merge(got, kept, cosine, sine, attended, row_count, units[0], len(units), outs)
    return (*updated, *outs)


def rotate_keys(keys, positions):
    half_width = keys.shape[-1] // 2
    frequency = jnp.power(
        jnp.float32(1000000.0), -2.0 * jnp.arange(half_width, dtype=jnp.float32) / keys.shape[-1]
    )
    angles = positions[..., None] * frequency
    leading = keys[..., :half_width]
    trailing = keys[..., half_width:]
    cosine = jnp.cos(angles)
    sine_part = jnp.sin(angles)
    return jnp.concatenate(
        [leading * cosine - trailing * sine_part, trailing * cosine + leading * sine_part], axis=-1
    )


def plain_shards(
    tokens, queries, cache_keys, cache_values, lengths, weights, moment1, moment2, grad_parts
):
    gradient = lax.psum(grad_parts[0], "group")
    new_weights, new_moment1, new_moment2 = adam_update(weights, moment1, moment2, gradient)
    weight_shard = new_weights.astype(jnp.bfloat16)
    tp_count = lax.axis_size("tp")
    fsdp_count = lax.axis_size("fsdp")
    head_cols = weight_shard.shape[1] // tp_count
    row_count = tokens.shape[0]
    block_rows = weight_shard.shape[0]
    split_tokens = tokens.reshape(row_count, STEPS, fsdp_count, tp_count, block_rows)
    own_columns = lax.dynamic_index_in_dim(split_tokens, lax.axis_index("tp"), 3, keepdims=False)
    arrived = lax.all_to_all(own_columns, "fsdp", split_axis=2, concat_axis=0, tiled=True)
    arrived = arrived.reshape(fsdp_count * row_count * STEPS, block_rows)
    partial_terms = jnp.dot(arrived, weight_shard, preferred_element_type=jnp.float32)
    partial_terms = partial_terms.reshape(fsdp_count, row_count * STEPS, tp_count, head_cols)
    partial_terms = partial_terms.transpose(0, 2, 1, 3).reshape(
        fsdp_count * tp_count * row_count * STEPS, head_cols
    )
    projected = lax.psum_scatter(partial_terms, ("fsdp", "tp"), scatter_dimension=0, tiled=True)
    kv_heads = head_cols // (2 * HD)
    projected = projected.reshape(row_count, STEPS, kv_heads, 2, HD)
    positions = (lengths[:, None] + jnp.arange(STEPS, dtype=jnp.int32)[None, :]).astype(jnp.float32)
    new_keys = rotate_keys(projected[:, :, :, 0], positions[:, :, None])
    fresh = jnp.stack([new_keys, projected[:, :, :, 1]], axis=3).astype(jnp.bfloat16)
    new_kv = fresh.reshape(row_count, STEPS, head_cols)
    span_length = cache_keys.shape[1]
    grouped = queries.reshape(row_count, STEPS, kv_heads, PER_GROUP, HD)
    cached_keys = cache_keys.reshape(row_count, span_length, kv_heads, HD)
    cached_values = cache_values.reshape(row_count, span_length, kv_heads, HD)
    new_scores = (
        jnp.einsum(
            "risgd,rjsd->risgj", grouped, fresh[:, :, :, 0], preferred_element_type=jnp.float32
        )
        * score_scale
    )
    causal = jnp.arange(STEPS)[:, None] >= jnp.arange(STEPS)[None, :]
    new_scores = jnp.where(causal[None, :, None, None, :], new_scores, masked_score)
    scores = (
        jnp.einsum("risgd,rpsd->risgp", grouped, cached_keys, preferred_element_type=jnp.float32)
        * score_scale
    )
    in_range = jnp.arange(span_length, dtype=jnp.int32)[None, :] < lengths[:, None]
    all_scores = jnp.concatenate(
        [jnp.where(in_range[:, None, None, None, :], scores, masked_score), new_scores], axis=-1
    )
    highest = jnp.max(all_scores, axis=-1, keepdims=True)
    exponent = jnp.exp(all_scores - highest)
    probs = (exponent / jnp.sum(exponent, axis=-1, keepdims=True)).astype(jnp.bfloat16)
    context = jnp.einsum(
        "risgp,rpsd->risgd",
        probs[..., :span_length],
        cached_values,
        preferred_element_type=jnp.float32,
    )
    context = context + jnp.einsum(
        "risgj,rjsd->risgd",
        probs[..., span_length:],
        fresh[:, :, :, 1],
        preferred_element_type=jnp.float32,
    )
    context = context.reshape(row_count, STEPS, kv_heads * PER_GROUP * HD).astype(jnp.bfloat16)
    return (new_weights, new_moment1, new_moment2, new_kv, context)


def power_of_two(n):
    return n > 1 and n & (n - 1) == 0


def solution(mesh):
    in_specs = (
        P(("group", "fsdp"), None, None),
        P(("group", "fsdp"), None, "tp"),
        P(("group", "fsdp"), None, "tp"),
        P(("group", "fsdp"), None, "tp"),
        P(("group", "fsdp")),
        P(("fsdp", "tp"), None),
        P(("fsdp", "tp"), None),
        P(("fsdp", "tp"), None),
        P("group", ("fsdp", "tp"), None),
    )
    out_specs = (
        P(("fsdp", "tp"), None),
        P(("fsdp", "tp"), None),
        P(("fsdp", "tp"), None),
        P(("group", "fsdp"), None, "tp"),
        P(("group", "fsdp"), None, "tp"),
    )
    sizes = mesh.shape
    pairwise = power_of_two(sizes["group"]) and power_of_two(sizes["fsdp"]) and sizes["tp"] == 2
    shards = butterfly_shards if pairwise else plain_shards
    return jax.shard_map(shards, mesh=mesh, in_specs=in_specs, out_specs=out_specs, check_vma=False)
```

```python
import functools
import math

import jax
import jax.numpy as jnp
from jax import lax
from jax.experimental import pallas as pl
from jax.experimental.pallas import tpu as pltpu
from jax.sharding import PartitionSpec as P

QH = 40
KVH = 8
HD = 128
STEPS = 4
PER_GROUP = QH // KVH
HEAD_COLS = 2 * HD


beta_one = 0.9
beta_two = 0.95
learning_rate = 0.004
decay_rate = 0.1
epsilon = 1e-08
correct_one = 1.0 - 0.9**10
correct_two = 1.0 - 0.95**10
masked_score = -1e30
score_scale = 1.0 / math.sqrt(HD)

N_PIECES = 2
MIB = 1024 * 1024


def adam_update(weights, moment1, moment2, gradient):
    new_moment1 = beta_one * moment1 + (1.0 - beta_one) * gradient
    new_moment2 = beta_two * moment2 + (1.0 - beta_two) * gradient * gradient
    direction = new_moment1 / correct_one / (jnp.sqrt(new_moment2 / correct_two) + epsilon)
    new_weights = weights - learning_rate * (direction + decay_rate * weights)
    return (new_weights, new_moment1, new_moment2)


def rotation_tables(lengths):
    half_width = HD // 2
    frequency = jnp.power(
        jnp.float32(1000000.0), -2.0 * jnp.arange(half_width, dtype=jnp.float32) / HD
    )
    positions = (lengths[:, None] + jnp.arange(STEPS, dtype=jnp.int32)[None, :]).astype(jnp.float32)
    angles = positions.reshape(-1)[:, None] * frequency
    cosine = jnp.cos(angles)
    sine = jnp.sin(angles)
    return (
        jnp.concatenate([cosine, cosine], axis=-1),
        jnp.concatenate([-sine, sine], axis=-1),
    )


def whole(a):
    return pl.BlockSpec(a.shape, lambda *_: (0,) * len(a.shape))


def after(value, *earlier):
    return lax.optimization_barrier((value, *earlier))[0] if earlier else value


def cost(busy_us):
    return pl.CostEstimate(flops=1, bytes_accessed=max(1, int(busy_us * 2.5e6)), transcendentals=0)


def in_hbm(a):
    return pltpu.with_memory_space_constraint(a, pltpu.HBM)


VMEM = pl.BlockSpec(memory_space=pltpu.VMEM)
ANYWHERE = pl.BlockSpec(memory_space=pl.ANY)


def columns_at(place, part, first, n):
    half = place[0] if part == 0 else 1 - place[0]
    return pl.ds(pl.multiple_of((half * place[2] + first) * HD, HD), n * HD)


def slab_ends(rows):
    if rows % HD:
        return [(0, rows)]
    return [(r, min(r + 2 * HD, rows)) for r in range(0, rows, 2 * HD)]


def cast_kernel(wanted, n_units, source, *refs):
    outs, buffers, sems = refs[: -len(wanted) - 1], refs[-len(wanted) - 1 : -1], refs[-1]
    place = (lax.axis_index("group") % 2, None, n_units)
    ends = slab_ends(source.shape[0])
    copies = [
        [
            pltpu.make_async_copy(
                source.at[r:e, columns_at(place, part, first, n)], buffers[w].at[r:e], sems.at[w, i]
            )
            for i, (r, e) in enumerate(ends)
        ]
        for w, (part, first, n, _) in enumerate(wanted)
    ]
    for copy in sum(copies, []):
        copy.start()
    at = 0
    for w, (_, _, _, n_pieces) in enumerate(wanted):
        if n_pieces == 1:
            for copy, (r, e) in zip(copies[w], ends):
                copy.wait()
                outs[at][r:e] = buffers[w][r:e].astype(jnp.bfloat16)
        else:
            for copy in copies[w]:
                copy.wait()
            step = buffers[w].shape[0] // n_pieces
            for p in range(n_pieces):
                outs[at + p][...] = buffers[w][p * step : (p + 1) * step].astype(jnp.bfloat16)
        at += n_pieces


def cast_units(local, n_units, wanted):
    rows = local.shape[0]
    shapes = [(rows // p, n * HD) for _, _, n, p in wanted for _ in range(p)]
    out = pl.pallas_call(
        functools.partial(cast_kernel, wanted, n_units),
        in_specs=[ANYWHERE],
        out_specs=[VMEM] * len(shapes),
        scratch_shapes=[pltpu.VMEM((rows, n * HD), jnp.float32) for _, _, n, _ in wanted]
        + [pltpu.SemaphoreType.DMA((len(wanted), len(slab_ends(rows))))],
        out_shape=[jax.ShapeDtypeStruct(shape, jnp.bfloat16) for shape in shapes],
        compiler_params=pltpu.CompilerParams(vmem_limit_bytes=6 * MIB),
        cost_estimate=cost(0),
        name="cast_units",
    )(in_hbm(local))
    results = []
    for _, _, _, p in wanted:
        results.append(out[:p])
        out = out[p:]
    return results


def sum_kernel(axis, cuts, n_a, n_b, *refs):
    a, b, outs = refs[:n_a], refs[n_a : n_a + n_b], refs[n_a + n_b :]
    total = join(a, axis).astype(jnp.float32) + join(b, axis).astype(jnp.float32)
    at = 0
    for out, n in zip(outs, cuts):
        piece = total[at : at + n] if axis else total[:, at : at + n]
        out[...] = piece.astype(out.dtype)
        at += n


def sum_pieces(a, b, axis, cuts):
    joined = sum(x.shape[axis] for x in a)
    return pl.pallas_call(
        functools.partial(sum_kernel, axis, cuts, len(a), len(b)),
        in_specs=[VMEM] * (len(a) + len(b)),
        out_specs=[VMEM] * len(cuts),
        out_shape=[jax.ShapeDtypeStruct((n, joined) if axis else (joined, n), jnp.bfloat16) for n in cuts],
        compiler_params=pltpu.CompilerParams(vmem_limit_bytes=6 * MIB),
        cost_estimate=cost(0),
        name="sum_pieces",
    )(*a, *b)


def token_kernel(n, place, source, *outs):
    rows, steps, _ = source.shape
    width = outs[0].shape[1]
    for d in range(n):
        at = pl.ds(pl.multiple_of((place[3] ^ d) * place[4] + place[5], HD), width)
        pieces = [source[r, :, at].astype(jnp.float32) for r in range(rows)]
        outs[d][...] = jnp.concatenate(pieces, axis=0).astype(jnp.bfloat16)


def token_pieces(place, tokens, n, width):
    row_count, steps, _ = tokens.shape
    return pl.pallas_call(
        functools.partial(token_kernel, n),
        grid_spec=pltpu.PrefetchScalarGridSpec(
            num_scalar_prefetch=1, grid=(), in_specs=[VMEM], out_specs=[VMEM] * n
        ),
        out_shape=[jax.ShapeDtypeStruct((row_count * steps, width), jnp.bfloat16)] * n,
        compiler_params=pltpu.CompilerParams(vmem_limit_bytes=4 * MIB),
        cost_estimate=cost(0),
        name="token_pieces",
    )(place, tokens)


def stack_kernel(takes, *refs):
    refs[-1][...] = jnp.concatenate([r[at * n : (at + 1) * n] for r, (at, n) in zip(refs[:-1], takes)], axis=0)


def stack_blocks(blocks, rows):
    arrays = [a for a, _ in blocks]
    return pl.pallas_call(
        functools.partial(stack_kernel, [(at, rows) for _, at in blocks]),
        in_specs=[VMEM] * len(arrays),
        out_specs=VMEM,
        out_shape=jax.ShapeDtypeStruct((rows * len(arrays), arrays[0].shape[1]), arrays[0].dtype),
        compiler_params=pltpu.CompilerParams(vmem_limit_bytes=4 * MIB),
        cost_estimate=cost(0),
        name="stack_blocks",
    )(*arrays)


def join(pieces, axis=0):
    return jnp.concatenate([p[...] for p in pieces], axis=axis)


def adam_kernel(first, n, n_mine, n_partner, tok_places, previous, place, *refs):
    refs = list(refs)
    take = lambda n: [refs.pop(0) for _ in range(n)]
    pieces = take(n_mine + n_partner)
    state = take(3)
    toks = take(len(tok_places))
    take(3 * previous)
    updated = take(3)
    sent, kept, in_sems, out_sems, buffer = refs

    slabs = [(part, slice(*ends)) for part in range(2) for ends in slab_ends(buffer.shape[2])]
    columns = [columns_at(place, part, first, n) for part in range(2)]
    incoming = []
    for i, (part, at) in enumerate(slabs):
        incoming.append(
            [
                pltpu.make_async_copy(
                    state[q].at[at, columns[part]], buffer.at[q, part, at], in_sems.at[q, i]
                )
                for q in range(3)
            ]
        )
        for copy in incoming[i]:
            copy.start()
    block = sent.shape[0] // len(toks)
    tok = jnp.concatenate([t[k * block : (k + 1) * block] for t, k in zip(toks, tok_places)], axis=0)
    totals = [join(pieces[:n_mine]), join(pieces[n_mine:])]
    outgoing, products = [], [None, None]
    for i, (part, at) in enumerate(slabs):
        for copy in incoming[i]:
            copy.wait()
        gradient = totals[part][at].astype(jnp.float32)
        results = adam_update(buffer[0, part, at], buffer[1, part, at], buffer[2, part, at], gradient)
        for q in range(3):
            buffer[q, part, at] = results[q]
            outgoing.append(
                pltpu.make_async_copy(
                    buffer.at[q, part, at], updated[q].at[at, columns[part]], out_sems.at[q, i]
                )
            )
            outgoing[-1].start()
        terms = jnp.dot(tok[:, at], results[0].astype(jnp.bfloat16), preferred_element_type=jnp.float32)
        products[part] = terms if products[part] is None else products[part] + terms
    stays = place[0] == place[1]
    kept[...] = jnp.where(stays, products[0], products[1])
    sent[...] = jnp.where(stays, products[1], products[0]).astype(jnp.bfloat16)
    for copy in outgoing:
        copy.wait()


def adam_units(place, total, state, toks, first, n, previous):
    mine, partner = total
    rows, width = state[0].shape
    n_slabs = 2 * len(slab_ends(rows))
    n_tokens = min(t.shape[0] for t, _ in toks) * len(toks)
    operands = [*mine, *partner, *[in_hbm(a) for a in state], *[t for t, _ in toks]]
    in_specs = [VMEM] * (len(mine) + len(partner)) + [ANYWHERE] * 3 + [VMEM] * len(toks)
    aliases = {}
    if previous is not None:
        aliases = {1 + len(operands) + i: i for i in range(3)}
        operands += previous
        in_specs += [ANYWHERE] * 3
    shape = (n_tokens, n * HD)
    out = pl.pallas_call(
        functools.partial(
            adam_kernel, first, n, len(mine), len(partner), [at for _, at in toks], previous is not None
        ),
        grid_spec=pltpu.PrefetchScalarGridSpec(
            num_scalar_prefetch=1,
            grid=(),
            in_specs=in_specs,
            out_specs=[ANYWHERE] * 3 + [VMEM] * 2,
            scratch_shapes=[
                pltpu.SemaphoreType.DMA((3, n_slabs)),
                pltpu.SemaphoreType.DMA((3, n_slabs)),
                pltpu.VMEM((3, 2, rows, n * HD), jnp.float32),
            ],
        ),
        out_shape=[jax.ShapeDtypeStruct((rows, width), jnp.float32)] * 3
        + [jax.ShapeDtypeStruct(shape, jnp.bfloat16), jax.ShapeDtypeStruct(shape, jnp.float32)],
        input_output_aliases=aliases,
        compiler_params=pltpu.CompilerParams(vmem_limit_bytes=15 * MIB),
        cost_estimate=cost(0),
        name="adam_project",
    )(place, *operands)
    return out[:3], out[3:]


SLOT = 32


def cache_kernel(heads, first, lens, q, k, v, stacked, acc, stats):
    step = pl.program_id(0)
    rows = q.shape[0]
    span = k.shape[1]
    used = PER_GROUP * STEPS
    for i in range(rows):
        length = lens[first + step * rows + i]
        query = q[i].astype(jnp.float32)
        scores = []
        for h in range(heads):
            pieces = [
                query[:, (h * PER_GROUP + g) * HD : (h * PER_GROUP + g + 1) * HD] for g in range(PER_GROUP)
            ]
            pieces.append(jnp.zeros((SLOT - used, HD), jnp.float32))
            one = jnp.concatenate(pieces, axis=0).astype(jnp.bfloat16)
            stacked[h, i] = one
            scores.append(
                lax.dot_general(
                    one,
                    k[i, :, h * HD : (h + 1) * HD],
                    (((1,), (1,)), ((), ())),
                    preferred_element_type=jnp.float32,
                )
            )
        scores = jnp.concatenate(scores, axis=0) * score_scale
        in_range = lax.broadcasted_iota(jnp.int32, (1, span), 1) < length
        scores = jnp.where(in_range, scores, masked_score)
        highest = jnp.max(scores, axis=-1, keepdims=True)
        weight = jnp.exp(scores - highest)
        total = jnp.sum(weight, axis=-1, keepdims=True)
        weight = weight.astype(jnp.bfloat16)
        lane = lax.broadcasted_iota(jnp.int32, (heads * SLOT, HD), 1)
        stat = jnp.where(lane < HD // 2, highest, total)
        for h in range(heads):
            at = slice(h * SLOT, (h + 1) * SLOT)
            acc[h, i] = jnp.dot(
                weight[at], v[i, :, h * HD : (h + 1) * HD], preferred_element_type=jnp.float32
            )
            stats[h, i] = stat[at]


def cache_attention(queries, cache_keys, cache_values, lengths, first, row_count):
    _, span, kv_cols = cache_keys.shape
    heads = kv_cols // HD
    rows = 2 if row_count % 2 == 0 and first % 2 == 0 else 1
    shape = (heads, row_count, SLOT, HD)
    out_block = pl.BlockSpec((heads, rows, SLOT, HD), lambda r, lens: (0, r, 0, 0))
    in_block = lambda a: pl.BlockSpec((rows, *a.shape[1:]), lambda r, lens: (first // rows + r, 0, 0))
    return pl.pallas_call(
        functools.partial(cache_kernel, heads, first),
        grid_spec=pltpu.PrefetchScalarGridSpec(
            num_scalar_prefetch=1,
            grid=(row_count // rows,),
            in_specs=[in_block(queries), in_block(cache_keys), in_block(cache_values)],
            out_specs=[out_block] * 3,
        ),
        out_shape=[
            jax.ShapeDtypeStruct(shape, jnp.bfloat16),
            jax.ShapeDtypeStruct(shape, jnp.float32),
            jax.ShapeDtypeStruct(shape, jnp.float32),
        ],
        compiler_params=pltpu.CompilerParams(vmem_limit_bytes=10 * MIB),
        cost_estimate=cost(7),
        name="cache_attention",
    )(lengths, in_hbm(queries), in_hbm(cache_keys), in_hbm(cache_values))


def merge_kernel(spans, first, n_heads, *refs):
    folds, refs = refs[: 2 * len(spans)], refs[2 * len(spans) :]
    cosine, sine, stacked, acc, stats = refs[:5]
    new_kv, context = refs[-2:]
    row_count = new_kv.shape[0]
    every = jnp.concatenate(
        [
            folds[2 * f][:, span].astype(jnp.float32) + folds[2 * f + 1][:, span]
            for f, span in enumerate(spans)
        ],
        axis=1,
    )
    at = lax.broadcasted_iota(jnp.int32, (row_count * SLOT, row_count * STEPS), 0)
    to = lax.broadcasted_iota(jnp.int32, (row_count * SLOT, row_count * STEPS), 1)
    seen = (at // SLOT == to // STEPS) & (at % STEPS >= to % STEPS)
    rows_of = lambda a, u: a[first + u].reshape(-1, HD)
    for u in range(n_heads):
        total = every[:, u * HEAD_COLS : (u + 1) * HEAD_COLS]
        keys = total[:, :HD]
        keys = keys * cosine[...] + pltpu.roll(keys, HD // 2, 1) * sine[...]
        keys = keys.astype(jnp.bfloat16)
        values = total[:, HD:].astype(jnp.bfloat16)
        both = jnp.concatenate([keys, values], axis=1).astype(jnp.float32)
        for r in range(row_count):
            new_kv[r, :, u * HEAD_COLS : (u + 1) * HEAD_COLS] = both[
                r * STEPS : (r + 1) * STEPS
            ].astype(jnp.bfloat16)
        scores = (
            lax.dot_general(
                rows_of(stacked, u), keys, (((1,), (1,)), ((), ())), preferred_element_type=jnp.float32
            )
            * score_scale
        )
        scores = jnp.where(seen, scores, masked_score)
        stat = rows_of(stats, u)
        old_highest = stat[:, :1]
        old_total = stat[:, HD // 2 : HD // 2 + 1]
        highest = jnp.maximum(jnp.max(scores, axis=-1, keepdims=True), old_highest)
        weight = jnp.exp(scores - highest)
        scale = jnp.exp(old_highest - highest)
        denominator = jnp.sum(weight, axis=-1, keepdims=True) + scale * old_total
        out = jnp.dot(weight.astype(jnp.bfloat16), values, preferred_element_type=jnp.float32)
        out = (out + scale * rows_of(acc, u)) / denominator
        for r in range(row_count):
            for g in range(PER_GROUP):
                at_row = r * SLOT + g * STEPS
                at_col = (u * PER_GROUP + g) * HD
                context[r, :, at_col : at_col + HD] = out[at_row : at_row + STEPS].astype(jnp.bfloat16)


def merge(folds, cosine, sine, attended, row_count, first, n_heads, previous):
    heads = attended[0].shape[0]
    block = first // n_heads
    operands = [a for fold in folds for a in fold[:2]] + [cosine, sine, *attended]
    in_specs = [VMEM] * len(operands)
    aliases = {}
    if previous is not None:
        aliases = {len(operands) + i: i for i in range(2)}
        operands += previous
        in_specs += [ANYWHERE] * 2
    widths = (HEAD_COLS, PER_GROUP * HD)
    return pl.pallas_call(
        functools.partial(merge_kernel, [fold[2] for fold in folds], first, n_heads),
        grid=(1,),
        in_specs=in_specs,
        out_specs=[pl.BlockSpec((row_count, STEPS, n_heads * w), lambda i: (0, 0, block)) for w in widths],
        out_shape=[jax.ShapeDtypeStruct((row_count, STEPS, heads * w), jnp.bfloat16) for w in widths],
        input_output_aliases=aliases,
        compiler_params=pltpu.CompilerParams(vmem_limit_bytes=8 * MIB),
        cost_estimate=cost(0),
        name="merge_new",
    )(*operands)


def swap(array, axis, bit):
    size = lax.axis_size(axis)
    return lax.ppermute(array, axis, [(i, i ^ bit) for i in range(size)])


def reversed_bits(n):
    order = [0]
    while len(order) < n:
        order = [2 * i for i in order] + [2 * i + 1 for i in order]
    return order


def fold_rows(arrived, kept, n):
    total = arrived.astype(jnp.float32) + kept
    half = total.shape[0] // 2
    return total[half:].astype(jnp.bfloat16), total[:half]


def butterfly_shards(
    tokens, queries, cache_keys, cache_values, lengths, weights, moment1, moment2, grad_parts
):
    fsdp_count = lax.axis_size("fsdp")
    tp_count = lax.axis_size("tp")
    core = lax.axis_index("group") % 2
    fsdp = lax.axis_index("fsdp")
    tp = lax.axis_index("tp")
    rows, width = weights.shape
    row_count = tokens.shape[0]
    n_units = width // (tp_count * HD)
    local = grad_parts[0]
    place = jnp.stack(
        [core, tp, jnp.full_like(core, n_units), fsdp, jnp.full_like(core, tp_count * rows), tp * rows]
    ).astype(jnp.int32)

    n_first = n_units // 2 + n_units // 8
    n_early = n_first
    n_late = n_units - n_early

    def chip_sum(away, home, cuts):
        return sum_pieces([home], [swap(a, "group", 1) for a in away], 0, cuts)

    (away,) = cast_units(local, n_units, [(1, 0, n_first, 1)])
    ((home,),) = cast_units(after(local, *away), n_units, [(0, 0, n_first, 1)])
    (begun,) = chip_sum(away, home, [n_first * HD])
    early, crossed = [begun], [swap(begun, "group", 2)]

    n_tokens = row_count * STEPS
    blocks = [(t, 0) for t in token_pieces(place, after(tokens, begun), fsdp_count, rows)]
    source = after(local, begun, *[t for t, _ in blocks])
    n_rest = n_units - n_first
    away, (home,) = cast_units(source, n_units, [(1, n_first, n_rest, N_PIECES), (0, n_first, n_rest, 1)])
    *more, last = chip_sum(away, home, [n_late * HD])
    early += more
    crossed += [swap(m, "group", 2) for m in more]
    crossed_last = swap(last, "group", 2)

    cosine, sine = rotation_tables(lengths)
    ready = [*early, last]
    attended = cache_attention(after(queries, *ready), cache_keys, cache_values, lengths, 0, row_count)
    distance = fsdp_count // 2
    step = (attended[1],)
    while distance:
        going = [d for d in range(fsdp_count) if d & distance]
        leaving = [blocks[d] for d in going]
        if distance < fsdp_count // 2:
            leaving = [(after(t, attended[1]), at) for t, at in leaving]
        stacked = stack_blocks(leaving, n_tokens)
        got = swap(stacked, "fsdp", distance)
        for i, d in enumerate(going):
            blocks[d] = (got, i)
        distance //= 2
        step = (attended[1], got)
    toks = [blocks[d] for d in reversed_bits(fsdp_count)]

    state = (weights, moment1, moment2)

    def total(parts, arrived, n_pieces, *earlier):
        arrived = list(lax.optimization_barrier((*arrived, *earlier)))[: len(arrived)]
        one = sum_pieces(parts, arrived, 1, [rows // n_pieces] * n_pieces)
        return one, [swap(p, "group", 1) for p in one]

    both = total(early, crossed, N_PIECES, *step)
    updated, (sent, kept) = adam_units(place, both, state, toks, 0, n_early, None)
    moving = [(swap(sent, "tp", 1), kept)]
    both = total([last], [crossed_last], N_PIECES, sent)
    updated, (sent, kept) = adam_units(place, both, state, toks, n_early, n_late, updated)
    moving.append((swap(sent, "tp", 1), kept))
    distance = 1
    while distance < fsdp_count:
        for f, (got, kept) in enumerate(moving):
            sent, kept = fold_rows(got, kept, fsdp_count)
            moving[f] = (swap(sent, "fsdp", distance), kept)
        distance *= 2

    n_heads = n_units * HD // HEAD_COLS
    whole_heads = n_heads // 2
    split = whole_heads * HEAD_COLS
    outs = merge(
        [(*moving[0], slice(0, split))], cosine, sine, attended, row_count, 0, whole_heads, None
    )
    parts = [(*moving[0], slice(split, n_early * HD)), (*moving[1], slice(0, n_late * HD))]
    outs = merge(
        parts[0 if split < n_early * HD else 1 :],
        cosine,
        sine,
        attended,
        row_count,
        whole_heads,
        n_heads - whole_heads,
        outs,
    )
    return (*updated, *outs)


def rotate_keys(keys, positions):
    half_width = keys.shape[-1] // 2
    frequency = jnp.power(
        jnp.float32(1000000.0), -2.0 * jnp.arange(half_width, dtype=jnp.float32) / keys.shape[-1]
    )
    angles = positions[..., None] * frequency
    leading = keys[..., :half_width]
    trailing = keys[..., half_width:]
    cosine = jnp.cos(angles)
    sine_part = jnp.sin(angles)
    return jnp.concatenate(
        [leading * cosine - trailing * sine_part, trailing * cosine + leading * sine_part], axis=-1
    )


def plain_shards(
    tokens, queries, cache_keys, cache_values, lengths, weights, moment1, moment2, grad_parts
):
    gradient = lax.psum(grad_parts[0], "group")
    new_weights, new_moment1, new_moment2 = adam_update(weights, moment1, moment2, gradient)
    weight_shard = new_weights.astype(jnp.bfloat16)
    tp_count = lax.axis_size("tp")
    fsdp_count = lax.axis_size("fsdp")
    head_cols = weight_shard.shape[1] // tp_count
    row_count = tokens.shape[0]
    block_rows = weight_shard.shape[0]
    split_tokens = tokens.reshape(row_count, STEPS, fsdp_count, tp_count, block_rows)
    own_columns = lax.dynamic_index_in_dim(split_tokens, lax.axis_index("tp"), 3, keepdims=False)
    arrived = lax.all_to_all(own_columns, "fsdp", split_axis=2, concat_axis=0, tiled=True)
    arrived = arrived.reshape(fsdp_count * row_count * STEPS, block_rows)
    partial_terms = jnp.dot(arrived, weight_shard, preferred_element_type=jnp.float32)
    partial_terms = partial_terms.reshape(fsdp_count, row_count * STEPS, tp_count, head_cols)
    partial_terms = partial_terms.transpose(0, 2, 1, 3).reshape(
        fsdp_count * tp_count * row_count * STEPS, head_cols
    )
    projected = lax.psum_scatter(partial_terms, ("fsdp", "tp"), scatter_dimension=0, tiled=True)
    kv_heads = head_cols // (2 * HD)
    projected = projected.reshape(row_count, STEPS, kv_heads, 2, HD)
    positions = (lengths[:, None] + jnp.arange(STEPS, dtype=jnp.int32)[None, :]).astype(jnp.float32)
    new_keys = rotate_keys(projected[:, :, :, 0], positions[:, :, None])
    fresh = jnp.stack([new_keys, projected[:, :, :, 1]], axis=3).astype(jnp.bfloat16)
    new_kv = fresh.reshape(row_count, STEPS, head_cols)
    span_length = cache_keys.shape[1]
    grouped = queries.reshape(row_count, STEPS, kv_heads, PER_GROUP, HD)
    cached_keys = cache_keys.reshape(row_count, span_length, kv_heads, HD)
    cached_values = cache_values.reshape(row_count, span_length, kv_heads, HD)
    new_scores = (
        jnp.einsum(
            "risgd,rjsd->risgj", grouped, fresh[:, :, :, 0], preferred_element_type=jnp.float32
        )
        * score_scale
    )
    causal = jnp.arange(STEPS)[:, None] >= jnp.arange(STEPS)[None, :]
    new_scores = jnp.where(causal[None, :, None, None, :], new_scores, masked_score)
    scores = (
        jnp.einsum("risgd,rpsd->risgp", grouped, cached_keys, preferred_element_type=jnp.float32)
        * score_scale
    )
    in_range = jnp.arange(span_length, dtype=jnp.int32)[None, :] < lengths[:, None]
    all_scores = jnp.concatenate(
        [jnp.where(in_range[:, None, None, None, :], scores, masked_score), new_scores], axis=-1
    )
    highest = jnp.max(all_scores, axis=-1, keepdims=True)
    exponent = jnp.exp(all_scores - highest)
    probs = (exponent / jnp.sum(exponent, axis=-1, keepdims=True)).astype(jnp.bfloat16)
    context = jnp.einsum(
        "risgp,rpsd->risgd",
        probs[..., :span_length],
        cached_values,
        preferred_element_type=jnp.float32,
    )
    context = context + jnp.einsum(
        "risgj,rjsd->risgd",
        probs[..., span_length:],
        fresh[:, :, :, 1],
        preferred_element_type=jnp.float32,
    )
    context = context.reshape(row_count, STEPS, kv_heads * PER_GROUP * HD).astype(jnp.bfloat16)
    return (new_weights, new_moment1, new_moment2, new_kv, context)


def power_of_two(n):
    return n > 1 and n & (n - 1) == 0


def solution(mesh):
    in_specs = (
        P(("group", "fsdp"), None, None),
        P(("group", "fsdp"), None, "tp"),
        P(("group", "fsdp"), None, "tp"),
        P(("group", "fsdp"), None, "tp"),
        P(("group", "fsdp")),
        P(("fsdp", "tp"), None),
        P(("fsdp", "tp"), None),
        P(("fsdp", "tp"), None),
        P("group", ("fsdp", "tp"), None),
    )
    out_specs = (
        P(("fsdp", "tp"), None),
        P(("fsdp", "tp"), None),
        P(("fsdp", "tp"), None),
        P(("group", "fsdp"), None, "tp"),
        P(("group", "fsdp"), None, "tp"),
    )
    sizes = mesh.shape
    pairwise = sizes["group"] == 4 and power_of_two(sizes["fsdp"]) and sizes["tp"] == 2
    shards = butterfly_shards if pairwise else plain_shards
    return jax.shard_map(shards, mesh=mesh, in_specs=in_specs, out_specs=out_specs, check_vma=False)
```

```python
import functools
import math

import jax
import jax.numpy as jnp
from jax import lax
from jax.experimental import pallas as pl
from jax.experimental.pallas import tpu as pltpu
from jax.sharding import PartitionSpec as P

QH = 40
KVH = 8
HD = 128
STEPS = 4
PER_GROUP = QH // KVH
HEAD_COLS = 2 * HD


beta_one = 0.9
beta_two = 0.95
learning_rate = 0.004
decay_rate = 0.1
epsilon = 1e-08
correct_one = 1.0 - 0.9**10
correct_two = 1.0 - 0.95**10
masked_score = -1e30
score_scale = 1.0 / math.sqrt(HD)

N_PIECES = 2
MIB = 1024 * 1024


def adam_update(weights, moment1, moment2, gradient):
    new_moment1 = beta_one * moment1 + (1.0 - beta_one) * gradient
    new_moment2 = beta_two * moment2 + (1.0 - beta_two) * gradient * gradient
    direction = new_moment1 / correct_one / (jnp.sqrt(new_moment2 / correct_two) + epsilon)
    new_weights = weights - learning_rate * (direction + decay_rate * weights)
    return (new_weights, new_moment1, new_moment2)


def rotation_tables(lengths):
    half_width = HD // 2
    frequency = jnp.power(
        jnp.float32(1000000.0), -2.0 * jnp.arange(half_width, dtype=jnp.float32) / HD
    )
    positions = (lengths[:, None] + jnp.arange(STEPS, dtype=jnp.int32)[None, :]).astype(jnp.float32)
    angles = positions.reshape(-1)[:, None] * frequency
    cosine = jnp.cos(angles)
    sine = jnp.sin(angles)
    return (
        jnp.concatenate([cosine, cosine], axis=-1),
        jnp.concatenate([-sine, sine], axis=-1),
    )


def whole(a):
    return pl.BlockSpec(a.shape, lambda *_: (0,) * len(a.shape))


def after(value, *earlier):
    return lax.optimization_barrier((value, *earlier))[0] if earlier else value


def cost(busy_us):
    return pl.CostEstimate(flops=1, bytes_accessed=max(1, int(busy_us * 2.5e6)), transcendentals=0)


def in_hbm(a):
    return pltpu.with_memory_space_constraint(a, pltpu.HBM)


VMEM = pl.BlockSpec(memory_space=pltpu.VMEM)
ANYWHERE = pl.BlockSpec(memory_space=pl.ANY)


def columns_at(place, part, first, n):
    half = place[0] if part == 0 else 1 - place[0]
    return pl.ds(pl.multiple_of((half * place[2] + first) * HD, HD), n * HD)


def slab_ends(rows):
    if rows % HD:
        return [(0, rows)]
    return [(r, min(r + 2 * HD, rows)) for r in range(0, rows, 2 * HD)]


def cast_kernel(wanted, n_units, source, *refs):
    outs, buffers, sems = refs[: -len(wanted) - 1], refs[-len(wanted) - 1 : -1], refs[-1]
    place = (lax.axis_index("group") % 2, None, n_units)
    ends = slab_ends(source.shape[0])
    copies = [
        [
            pltpu.make_async_copy(
                source.at[r:e, columns_at(place, part, first, n)], buffers[w].at[r:e], sems.at[w, i]
            )
            for i, (r, e) in enumerate(ends)
        ]
        for w, (part, first, n, _) in enumerate(wanted)
    ]
    for copy in sum(copies, []):
        copy.start()
    at = 0
    for w, (_, _, _, n_pieces) in enumerate(wanted):
        if n_pieces == 1:
            for copy, (r, e) in zip(copies[w], ends):
                copy.wait()
                outs[at][r:e] = buffers[w][r:e].astype(jnp.bfloat16)
        else:
            for copy in copies[w]:
                copy.wait()
            step = buffers[w].shape[0] // n_pieces
            for p in range(n_pieces):
                outs[at + p][...] = buffers[w][p * step : (p + 1) * step].astype(jnp.bfloat16)
        at += n_pieces


def cast_units(local, n_units, wanted):
    rows = local.shape[0]
    shapes = [(rows // p, n * HD) for _, _, n, p in wanted for _ in range(p)]
    out = pl.pallas_call(
        functools.partial(cast_kernel, wanted, n_units),
        in_specs=[ANYWHERE],
        out_specs=[VMEM] * len(shapes),
        scratch_shapes=[pltpu.VMEM((rows, n * HD), jnp.float32) for _, _, n, _ in wanted]
        + [pltpu.SemaphoreType.DMA((len(wanted), len(slab_ends(rows))))],
        out_shape=[jax.ShapeDtypeStruct(shape, jnp.bfloat16) for shape in shapes],
        compiler_params=pltpu.CompilerParams(vmem_limit_bytes=6 * MIB),
        cost_estimate=cost(0),
        name="cast_units",
    )(in_hbm(local))
    results = []
    for _, _, _, p in wanted:
        results.append(out[:p])
        out = out[p:]
    return results


def sum_kernel(axis, cuts, n_a, n_b, *refs):
    a, b, outs = refs[:n_a], refs[n_a : n_a + n_b], refs[n_a + n_b :]
    total = join(a, axis).astype(jnp.float32) + join(b, axis).astype(jnp.float32)
    at = 0
    for out, n in zip(outs, cuts):
        piece = total[at : at + n] if axis else total[:, at : at + n]
        out[...] = piece.astype(out.dtype)
        at += n


def sum_pieces(a, b, axis, cuts):
    joined = sum(x.shape[axis] for x in a)
    return pl.pallas_call(
        functools.partial(sum_kernel, axis, cuts, len(a), len(b)),
        in_specs=[VMEM] * (len(a) + len(b)),
        out_specs=[VMEM] * len(cuts),
        out_shape=[jax.ShapeDtypeStruct((n, joined) if axis else (joined, n), jnp.bfloat16) for n in cuts],
        compiler_params=pltpu.CompilerParams(vmem_limit_bytes=6 * MIB),
        cost_estimate=cost(0),
        name="sum_pieces",
    )(*a, *b)


def token_kernel(n, place, source, *outs):
    rows, steps, _ = source.shape
    width = outs[0].shape[1]
    for d in range(n):
        at = pl.ds(pl.multiple_of((place[3] ^ d) * place[4] + place[5], HD), width)
        pieces = [source[r, :, at].astype(jnp.float32) for r in range(rows)]
        outs[d][...] = jnp.concatenate(pieces, axis=0).astype(jnp.bfloat16)


def token_pieces(place, tokens, n, width):
    row_count, steps, _ = tokens.shape
    return pl.pallas_call(
        functools.partial(token_kernel, n),
        grid_spec=pltpu.PrefetchScalarGridSpec(
            num_scalar_prefetch=1, grid=(), in_specs=[VMEM], out_specs=[VMEM] * n
        ),
        out_shape=[jax.ShapeDtypeStruct((row_count * steps, width), jnp.bfloat16)] * n,
        compiler_params=pltpu.CompilerParams(vmem_limit_bytes=4 * MIB),
        cost_estimate=cost(0),
        name="token_pieces",
    )(place, tokens)


def stack_kernel(takes, *refs):
    refs[-1][...] = jnp.concatenate([r[at * n : (at + 1) * n] for r, (at, n) in zip(refs[:-1], takes)], axis=0)


def stack_blocks(blocks, rows):
    arrays = [a for a, _ in blocks]
    return pl.pallas_call(
        functools.partial(stack_kernel, [(at, rows) for _, at in blocks]),
        in_specs=[VMEM] * len(arrays),
        out_specs=VMEM,
        out_shape=jax.ShapeDtypeStruct((rows * len(arrays), arrays[0].shape[1]), arrays[0].dtype),
        compiler_params=pltpu.CompilerParams(vmem_limit_bytes=4 * MIB),
        cost_estimate=cost(0),
        name="stack_blocks",
    )(*arrays)


def join(pieces, axis=0):
    return jnp.concatenate([p[...] for p in pieces], axis=axis)


def adam_kernel(first, n, n_mine, n_partner, tok_places, previous, place, *refs):
    refs = list(refs)
    take = lambda n: [refs.pop(0) for _ in range(n)]
    pieces = take(n_mine + n_partner)
    state = take(3)
    toks = take(len(tok_places))
    take(3 * previous)
    updated = take(3)
    sent, kept, in_sems, out_sems, buffer = refs

    slabs = [(part, slice(*ends)) for part in range(2) for ends in slab_ends(buffer.shape[2])]
    columns = [columns_at(place, part, first, n) for part in range(2)]
    incoming = []
    for i, (part, at) in enumerate(slabs):
        incoming.append(
            [
                pltpu.make_async_copy(
                    state[q].at[at, columns[part]], buffer.at[q, part, at], in_sems.at[q, i]
                )
                for q in range(3)
            ]
        )
        for copy in incoming[i]:
            copy.start()
    block = sent.shape[0] // len(toks)
    tok = jnp.concatenate([t[k * block : (k + 1) * block] for t, k in zip(toks, tok_places)], axis=0)
    totals = [join(pieces[:n_mine]), join(pieces[n_mine:])]
    outgoing, products = [], [None, None]
    for i, (part, at) in enumerate(slabs):
        for copy in incoming[i]:
            copy.wait()
        gradient = totals[part][at].astype(jnp.float32)
        results = adam_update(buffer[0, part, at], buffer[1, part, at], buffer[2, part, at], gradient)
        for q in range(3):
            buffer[q, part, at] = results[q]
            outgoing.append(
                pltpu.make_async_copy(
                    buffer.at[q, part, at], updated[q].at[at, columns[part]], out_sems.at[q, i]
                )
            )
            outgoing[-1].start()
        terms = jnp.dot(tok[:, at], results[0].astype(jnp.bfloat16), preferred_element_type=jnp.float32)
        products[part] = terms if products[part] is None else products[part] + terms
    stays = place[0] == place[1]
    kept[...] = jnp.where(stays, products[0], products[1])
    sent[...] = jnp.where(stays, products[1], products[0]).astype(jnp.bfloat16)
    for copy in outgoing:
        copy.wait()


def adam_units(place, total, state, toks, first, n, previous):
    mine, partner = total
    rows, width = state[0].shape
    n_slabs = 2 * len(slab_ends(rows))
    n_tokens = min(t.shape[0] for t, _ in toks) * len(toks)
    operands = [*mine, *partner, *[in_hbm(a) for a in state], *[t for t, _ in toks]]
    in_specs = [VMEM] * (len(mine) + len(partner)) + [ANYWHERE] * 3 + [VMEM] * len(toks)
    aliases = {}
    if previous is not None:
        aliases = {1 + len(operands) + i: i for i in range(3)}
        operands += previous
        in_specs += [ANYWHERE] * 3
    shape = (n_tokens, n * HD)
    out = pl.pallas_call(
        functools.partial(
            adam_kernel, first, n, len(mine), len(partner), [at for _, at in toks], previous is not None
        ),
        grid_spec=pltpu.PrefetchScalarGridSpec(
            num_scalar_prefetch=1,
            grid=(),
            in_specs=in_specs,
            out_specs=[ANYWHERE] * 3 + [VMEM] * 2,
            scratch_shapes=[
                pltpu.SemaphoreType.DMA((3, n_slabs)),
                pltpu.SemaphoreType.DMA((3, n_slabs)),
                pltpu.VMEM((3, 2, rows, n * HD), jnp.float32),
            ],
        ),
        out_shape=[jax.ShapeDtypeStruct((rows, width), jnp.float32)] * 3
        + [jax.ShapeDtypeStruct(shape, jnp.bfloat16), jax.ShapeDtypeStruct(shape, jnp.float32)],
        input_output_aliases=aliases,
        compiler_params=pltpu.CompilerParams(vmem_limit_bytes=15 * MIB),
        cost_estimate=cost(0),
        name="adam_project",
    )(place, *operands)
    return out[:3], out[3:]


SLOT = 32


def cache_kernel(heads, first, lens, q, k, v, stacked, acc, stats):
    step = pl.program_id(0)
    rows = q.shape[0]
    span = k.shape[1]
    used = PER_GROUP * STEPS
    for i in range(rows):
        length = lens[first + step * rows + i]
        query = q[i].astype(jnp.float32)
        scores = []
        for h in range(heads):
            pieces = [
                query[:, (h * PER_GROUP + g) * HD : (h * PER_GROUP + g + 1) * HD] for g in range(PER_GROUP)
            ]
            pieces.append(jnp.zeros((SLOT - used, HD), jnp.float32))
            one = jnp.concatenate(pieces, axis=0).astype(jnp.bfloat16)
            stacked[h, i] = one
            scores.append(
                lax.dot_general(
                    one,
                    k[i, :, h * HD : (h + 1) * HD],
                    (((1,), (1,)), ((), ())),
                    preferred_element_type=jnp.float32,
                )
            )
        scores = jnp.concatenate(scores, axis=0) * score_scale
        in_range = lax.broadcasted_iota(jnp.int32, (1, span), 1) < length
        scores = jnp.where(in_range, scores, masked_score)
        highest = jnp.max(scores, axis=-1, keepdims=True)
        weight = jnp.exp(scores - highest)
        total = jnp.sum(weight, axis=-1, keepdims=True)
        weight = weight.astype(jnp.bfloat16)
        lane = lax.broadcasted_iota(jnp.int32, (heads * SLOT, HD), 1)
        stat = jnp.where(lane < HD // 2, highest, total)
        for h in range(heads):
            at = slice(h * SLOT, (h + 1) * SLOT)
            acc[h, i] = jnp.dot(
                weight[at], v[i, :, h * HD : (h + 1) * HD], preferred_element_type=jnp.float32
            )
            stats[h, i] = stat[at]


def cache_attention(queries, cache_keys, cache_values, lengths, first, row_count):
    _, span, kv_cols = cache_keys.shape
    heads = kv_cols // HD
    rows = 2 if row_count % 2 == 0 and first % 2 == 0 else 1
    shape = (heads, row_count, SLOT, HD)
    out_block = pl.BlockSpec((heads, rows, SLOT, HD), lambda r, lens: (0, r, 0, 0))
    in_block = lambda a: pl.BlockSpec((rows, *a.shape[1:]), lambda r, lens: (first // rows + r, 0, 0))
    return pl.pallas_call(
        functools.partial(cache_kernel, heads, first),
        grid_spec=pltpu.PrefetchScalarGridSpec(
            num_scalar_prefetch=1,
            grid=(row_count // rows,),
            in_specs=[in_block(queries), in_block(cache_keys), in_block(cache_values)],
            out_specs=[out_block] * 3,
        ),
        out_shape=[
            jax.ShapeDtypeStruct(shape, jnp.bfloat16),
            jax.ShapeDtypeStruct(shape, jnp.float32),
            jax.ShapeDtypeStruct(shape, jnp.float32),
        ],
        compiler_params=pltpu.CompilerParams(vmem_limit_bytes=10 * MIB),
        cost_estimate=cost(7),
        name="cache_attention",
    )(lengths, in_hbm(queries), in_hbm(cache_keys), in_hbm(cache_values))


def merge_kernel(spans, first, n_heads, *refs):
    folds, refs = refs[: 2 * len(spans)], refs[2 * len(spans) :]
    cosine, sine, stacked, acc, stats = refs[:5]
    new_kv, context = refs[-2:]
    row_count = new_kv.shape[0]
    every = jnp.concatenate(
        [
            folds[2 * f][:, span].astype(jnp.float32) + folds[2 * f + 1][:, span]
            for f, span in enumerate(spans)
        ],
        axis=1,
    )
    at = lax.broadcasted_iota(jnp.int32, (row_count * SLOT, row_count * STEPS), 0)
    to = lax.broadcasted_iota(jnp.int32, (row_count * SLOT, row_count * STEPS), 1)
    seen = (at // SLOT == to // STEPS) & (at % STEPS >= to % STEPS)
    rows_of = lambda a, u: a[first + u].reshape(-1, HD)
    for u in range(n_heads):
        total = every[:, u * HEAD_COLS : (u + 1) * HEAD_COLS]
        keys = total[:, :HD]
        keys = keys * cosine[...] + pltpu.roll(keys, HD // 2, 1) * sine[...]
        keys = keys.astype(jnp.bfloat16)
        values = total[:, HD:].astype(jnp.bfloat16)
        both = jnp.concatenate([keys, values], axis=1).astype(jnp.float32)
        for r in range(row_count):
            new_kv[r, :, u * HEAD_COLS : (u + 1) * HEAD_COLS] = both[
                r * STEPS : (r + 1) * STEPS
            ].astype(jnp.bfloat16)
        scores = (
            lax.dot_general(
                rows_of(stacked, u), keys, (((1,), (1,)), ((), ())), preferred_element_type=jnp.float32
            )
            * score_scale
        )
        scores = jnp.where(seen, scores, masked_score)
        stat = rows_of(stats, u)
        old_highest = stat[:, :1]
        old_total = stat[:, HD // 2 : HD // 2 + 1]
        highest = jnp.maximum(jnp.max(scores, axis=-1, keepdims=True), old_highest)
        weight = jnp.exp(scores - highest)
        scale = jnp.exp(old_highest - highest)
        denominator = jnp.sum(weight, axis=-1, keepdims=True) + scale * old_total
        out = jnp.dot(weight.astype(jnp.bfloat16), values, preferred_element_type=jnp.float32)
        out = (out + scale * rows_of(acc, u)) / denominator
        for r in range(row_count):
            for g in range(PER_GROUP):
                at_row = r * SLOT + g * STEPS
                at_col = (u * PER_GROUP + g) * HD
                context[r, :, at_col : at_col + HD] = out[at_row : at_row + STEPS].astype(jnp.bfloat16)


def merge(folds, cosine, sine, attended, row_count, first, n_heads, previous):
    heads = attended[0].shape[0]
    block = first // n_heads
    operands = [a for fold in folds for a in fold[:2]] + [cosine, sine, *attended]
    in_specs = [VMEM] * len(operands)
    aliases = {}
    if previous is not None:
        aliases = {len(operands) + i: i for i in range(2)}
        operands += previous
        in_specs += [ANYWHERE] * 2
    widths = (HEAD_COLS, PER_GROUP * HD)
    return pl.pallas_call(
        functools.partial(merge_kernel, [fold[2] for fold in folds], first, n_heads),
        grid=(1,),
        in_specs=in_specs,
        out_specs=[pl.BlockSpec((row_count, STEPS, n_heads * w), lambda i: (0, 0, block)) for w in widths],
        out_shape=[jax.ShapeDtypeStruct((row_count, STEPS, heads * w), jnp.bfloat16) for w in widths],
        input_output_aliases=aliases,
        compiler_params=pltpu.CompilerParams(vmem_limit_bytes=8 * MIB),
        cost_estimate=cost(0),
        name="merge_new",
    )(*operands)


def swap(array, axis, bit):
    size = lax.axis_size(axis)
    return lax.ppermute(array, axis, [(i, i ^ bit) for i in range(size)])


def reversed_bits(n):
    order = [0]
    while len(order) < n:
        order = [2 * i for i in order] + [2 * i + 1 for i in order]
    return order


def fold_rows(arrived, kept, n):
    total = arrived.astype(jnp.float32) + kept
    half = total.shape[0] // 2
    return total[half:].astype(jnp.bfloat16), total[:half]


def butterfly_shards(
    tokens, queries, cache_keys, cache_values, lengths, weights, moment1, moment2, grad_parts
):
    fsdp_count = lax.axis_size("fsdp")
    tp_count = lax.axis_size("tp")
    core = lax.axis_index("group") % 2
    fsdp = lax.axis_index("fsdp")
    tp = lax.axis_index("tp")
    rows, width = weights.shape
    row_count = tokens.shape[0]
    n_units = width // (tp_count * HD)
    local = grad_parts[0]
    place = jnp.stack(
        [core, tp, jnp.full_like(core, n_units), fsdp, jnp.full_like(core, tp_count * rows), tp * rows]
    ).astype(jnp.int32)

    n_first = n_units // 2
    n_extra = n_units // 8
    n_early = n_first + n_extra
    n_late = n_units - n_early

    def chip_sum(away, home, cuts):
        return sum_pieces([home], [swap(a, "group", 1) for a in away], 0, cuts)

    (away,) = cast_units(local, n_units, [(1, 0, n_first, 1)])
    ((home,),) = cast_units(after(local, *away), n_units, [(0, 0, n_first, 1)])
    (begun,) = chip_sum(away, home, [n_first * HD])
    early, crossed = [begun], [swap(begun, "group", 2)]

    n_tokens = row_count * STEPS
    blocks = [(t, 0) for t in token_pieces(place, after(tokens, begun), fsdp_count, rows)]
    source = after(local, begun, *[t for t, _ in blocks])
    n_rest = n_units - n_first
    away, (home,) = cast_units(source, n_units, [(1, n_first, n_rest, N_PIECES), (0, n_first, n_rest, 1)])
    *more, last = chip_sum(away, home, [n * HD for n in (n_extra, n_late) if n])
    early += more
    crossed += [swap(m, "group", 2) for m in more]
    crossed_last = swap(last, "group", 2)

    cosine, sine = rotation_tables(lengths)
    ready = [*early, last]
    attended = cache_attention(after(queries, *ready), cache_keys, cache_values, lengths, 0, row_count)
    distance = fsdp_count // 2
    step = (attended[1],)
    while distance:
        going = [d for d in range(fsdp_count) if d & distance]
        leaving = [blocks[d] for d in going]
        if distance < fsdp_count // 2:
            leaving = [(after(t, attended[1]), at) for t, at in leaving]
        stacked = stack_blocks(leaving, n_tokens)
        got = swap(stacked, "fsdp", distance)
        for i, d in enumerate(going):
            blocks[d] = (got, i)
        distance //= 2
        step = (attended[1], got)
    toks = [blocks[d] for d in reversed_bits(fsdp_count)]

    state = (weights, moment1, moment2)

    def total(parts, arrived, n_pieces, *earlier):
        arrived = list(lax.optimization_barrier((*arrived, *earlier)))[: len(arrived)]
        one = sum_pieces(parts, arrived, 1, [rows // n_pieces] * n_pieces)
        return one, [swap(p, "group", 1) for p in one]

    both = total(early, crossed, N_PIECES, *step)
    updated, (sent, kept) = adam_units(place, both, state, toks, 0, n_early, None)
    moving = [(swap(sent, "tp", 1), kept)]
    both = total([last], [crossed_last], 1, sent)
    updated, (sent, kept) = adam_units(place, both, state, toks, n_early, n_late, updated)
    moving.append((swap(sent, "tp", 1), kept))
    distance = 1
    while distance < fsdp_count:
        for f, (got, kept) in enumerate(moving):
            sent, kept = fold_rows(got, kept, fsdp_count)
            moving[f] = (swap(sent, "fsdp", distance), kept)
        distance *= 2

    n_heads = n_units * HD // HEAD_COLS
    whole_heads = n_heads // 2
    split = whole_heads * HEAD_COLS
    outs = merge(
        [(*moving[0], slice(0, split))], cosine, sine, attended, row_count, 0, whole_heads, None
    )
    parts = [(*moving[0], slice(split, n_early * HD)), (*moving[1], slice(0, n_late * HD))]
    outs = merge(
        parts[0 if split < n_early * HD else 1 :],
        cosine,
        sine,
        attended,
        row_count,
        whole_heads,
        n_heads - whole_heads,
        outs,
    )
    return (*updated, *outs)


def rotate_keys(keys, positions):
    half_width = keys.shape[-1] // 2
    frequency = jnp.power(
        jnp.float32(1000000.0), -2.0 * jnp.arange(half_width, dtype=jnp.float32) / keys.shape[-1]
    )
    angles = positions[..., None] * frequency
    leading = keys[..., :half_width]
    trailing = keys[..., half_width:]
    cosine = jnp.cos(angles)
    sine_part = jnp.sin(angles)
    return jnp.concatenate(
        [leading * cosine - trailing * sine_part, trailing * cosine + leading * sine_part], axis=-1
    )


def plain_shards(
    tokens, queries, cache_keys, cache_values, lengths, weights, moment1, moment2, grad_parts
):
    gradient = lax.psum(grad_parts[0], "group")
    new_weights, new_moment1, new_moment2 = adam_update(weights, moment1, moment2, gradient)
    weight_shard = new_weights.astype(jnp.bfloat16)
    tp_count = lax.axis_size("tp")
    fsdp_count = lax.axis_size("fsdp")
    head_cols = weight_shard.shape[1] // tp_count
    row_count = tokens.shape[0]
    block_rows = weight_shard.shape[0]
    split_tokens = tokens.reshape(row_count, STEPS, fsdp_count, tp_count, block_rows)
    own_columns = lax.dynamic_index_in_dim(split_tokens, lax.axis_index("tp"), 3, keepdims=False)
    arrived = lax.all_to_all(own_columns, "fsdp", split_axis=2, concat_axis=0, tiled=True)
    arrived = arrived.reshape(fsdp_count * row_count * STEPS, block_rows)
    partial_terms = jnp.dot(arrived, weight_shard, preferred_element_type=jnp.float32)
    partial_terms = partial_terms.reshape(fsdp_count, row_count * STEPS, tp_count, head_cols)
    partial_terms = partial_terms.transpose(0, 2, 1, 3).reshape(
        fsdp_count * tp_count * row_count * STEPS, head_cols
    )
    projected = lax.psum_scatter(partial_terms, ("fsdp", "tp"), scatter_dimension=0, tiled=True)
    kv_heads = head_cols // (2 * HD)
    projected = projected.reshape(row_count, STEPS, kv_heads, 2, HD)
    positions = (lengths[:, None] + jnp.arange(STEPS, dtype=jnp.int32)[None, :]).astype(jnp.float32)
    new_keys = rotate_keys(projected[:, :, :, 0], positions[:, :, None])
    fresh = jnp.stack([new_keys, projected[:, :, :, 1]], axis=3).astype(jnp.bfloat16)
    new_kv = fresh.reshape(row_count, STEPS, head_cols)
    span_length = cache_keys.shape[1]
    grouped = queries.reshape(row_count, STEPS, kv_heads, PER_GROUP, HD)
    cached_keys = cache_keys.reshape(row_count, span_length, kv_heads, HD)
    cached_values = cache_values.reshape(row_count, span_length, kv_heads, HD)
    new_scores = (
        jnp.einsum(
            "risgd,rjsd->risgj", grouped, fresh[:, :, :, 0], preferred_element_type=jnp.float32
        )
        * score_scale
    )
    causal = jnp.arange(STEPS)[:, None] >= jnp.arange(STEPS)[None, :]
    new_scores = jnp.where(causal[None, :, None, None, :], new_scores, masked_score)
    scores = (
        jnp.einsum("risgd,rpsd->risgp", grouped, cached_keys, preferred_element_type=jnp.float32)
        * score_scale
    )
    in_range = jnp.arange(span_length, dtype=jnp.int32)[None, :] < lengths[:, None]
    all_scores = jnp.concatenate(
        [jnp.where(in_range[:, None, None, None, :], scores, masked_score), new_scores], axis=-1
    )
    highest = jnp.max(all_scores, axis=-1, keepdims=True)
    exponent = jnp.exp(all_scores - highest)
    probs = (exponent / jnp.sum(exponent, axis=-1, keepdims=True)).astype(jnp.bfloat16)
    context = jnp.einsum(
        "risgp,rpsd->risgd",
        probs[..., :span_length],
        cached_values,
        preferred_element_type=jnp.float32,
    )
    context = context + jnp.einsum(
        "risgj,rjsd->risgd",
        probs[..., span_length:],
        fresh[:, :, :, 1],
        preferred_element_type=jnp.float32,
    )
    context = context.reshape(row_count, STEPS, kv_heads * PER_GROUP * HD).astype(jnp.bfloat16)
    return (new_weights, new_moment1, new_moment2, new_kv, context)


def power_of_two(n):
    return n > 1 and n & (n - 1) == 0


def solution(mesh):
    in_specs = (
        P(("group", "fsdp"), None, None),
        P(("group", "fsdp"), None, "tp"),
        P(("group", "fsdp"), None, "tp"),
        P(("group", "fsdp"), None, "tp"),
        P(("group", "fsdp")),
        P(("fsdp", "tp"), None),
        P(("fsdp", "tp"), None),
        P(("fsdp", "tp"), None),
        P("group", ("fsdp", "tp"), None),
    )
    out_specs = (
        P(("fsdp", "tp"), None),
        P(("fsdp", "tp"), None),
        P(("fsdp", "tp"), None),
        P(("group", "fsdp"), None, "tp"),
        P(("group", "fsdp"), None, "tp"),
    )
    sizes = mesh.shape
    pairwise = sizes["group"] == 4 and power_of_two(sizes["fsdp"]) and sizes["tp"] == 2
    shards = butterfly_shards if pairwise else plain_shards
    return jax.shard_map(shards, mesh=mesh, in_specs=in_specs, out_specs=out_specs, check_vma=False)
```

```python
import functools
import math

import jax
import jax.numpy as jnp
from jax import lax
from jax.experimental import pallas as pl
from jax.experimental.pallas import tpu as pltpu
from jax.sharding import PartitionSpec as P

QH = 40
KVH = 8
HD = 128
STEPS = 4
PER_GROUP = QH // KVH
HEAD_COLS = 2 * HD


beta_one = 0.9
beta_two = 0.95
learning_rate = 0.004
decay_rate = 0.1
epsilon = 1e-08
correct_one = 1.0 - 0.9**10
correct_two = 1.0 - 0.95**10
masked_score = -1e30
score_scale = 1.0 / math.sqrt(HD)

N_PIECES = 2
MIB = 1024 * 1024


def adam_update(weights, moment1, moment2, gradient):
    new_moment1 = beta_one * moment1 + (1.0 - beta_one) * gradient
    new_moment2 = beta_two * moment2 + (1.0 - beta_two) * gradient * gradient
    direction = new_moment1 / correct_one / (jnp.sqrt(new_moment2 / correct_two) + epsilon)
    new_weights = weights - learning_rate * (direction + decay_rate * weights)
    return (new_weights, new_moment1, new_moment2)


def rotation_tables(lengths):
    half_width = HD // 2
    frequency = jnp.power(
        jnp.float32(1000000.0), -2.0 * jnp.arange(half_width, dtype=jnp.float32) / HD
    )
    positions = (lengths[:, None] + jnp.arange(STEPS, dtype=jnp.int32)[None, :]).astype(jnp.float32)
    angles = positions.reshape(-1)[:, None] * frequency
    cosine = jnp.cos(angles)
    sine = jnp.sin(angles)
    return (
        jnp.concatenate([cosine, cosine], axis=-1),
        jnp.concatenate([-sine, sine], axis=-1),
    )


def whole(a):
    return pl.BlockSpec(a.shape, lambda *_: (0,) * len(a.shape))


def after(value, *earlier):
    return lax.optimization_barrier((value, *earlier))[0] if earlier else value


def cost(busy_us):
    return pl.CostEstimate(flops=1, bytes_accessed=max(1, int(busy_us * 2.5e6)), transcendentals=0)


def in_hbm(a):
    return pltpu.with_memory_space_constraint(a, pltpu.HBM)


VMEM = pl.BlockSpec(memory_space=pltpu.VMEM)
ANYWHERE = pl.BlockSpec(memory_space=pl.ANY)


def columns_at(place, part, first, n):
    half = place[0] if part == 0 else 1 - place[0]
    return pl.ds(pl.multiple_of((half * place[2] + first) * HD, HD), n * HD)


def slab_ends(rows):
    if rows % HD:
        return [(0, rows)]
    return [(r, min(r + 2 * HD, rows)) for r in range(0, rows, 2 * HD)]


def held_from(rows):
    return slab_ends(rows)[-2:][0][0]


def cast_kernel(wanted, n_units, source, *refs):
    outs, buffers, sems = refs[: -len(wanted) - 1], refs[-len(wanted) - 1 : -1], refs[-1]
    place = (lax.axis_index("group") % 2, None, n_units)
    ends = slab_ends(source.shape[0])
    copies = [
        [
            pltpu.make_async_copy(
                source.at[r:e, columns_at(place, part, first, n)], buffers[w].at[r:e], sems.at[w, i]
            )
            for i, (r, e) in enumerate(ends)
        ]
        for w, (part, first, n, _) in enumerate(wanted)
    ]
    for copy in sum(copies, []):
        copy.start()
    at = 0
    for w, (_, _, _, n_pieces) in enumerate(wanted):
        if n_pieces == 1:
            for copy, (r, e) in zip(copies[w], ends):
                copy.wait()
                outs[at][r:e] = buffers[w][r:e].astype(jnp.bfloat16)
        else:
            for copy in copies[w]:
                copy.wait()
            step = buffers[w].shape[0] // n_pieces
            for p in range(n_pieces):
                outs[at + p][...] = buffers[w][p * step : (p + 1) * step].astype(jnp.bfloat16)
        at += n_pieces


def cast_units(local, n_units, wanted):
    rows = local.shape[0]
    shapes = [(rows // p, n * HD) for _, _, n, p in wanted for _ in range(p)]
    out = pl.pallas_call(
        functools.partial(cast_kernel, wanted, n_units),
        in_specs=[ANYWHERE],
        out_specs=[VMEM] * len(shapes),
        scratch_shapes=[pltpu.VMEM((rows, n * HD), jnp.float32) for _, _, n, _ in wanted]
        + [pltpu.SemaphoreType.DMA((len(wanted), len(slab_ends(rows))))],
        out_shape=[jax.ShapeDtypeStruct(shape, jnp.bfloat16) for shape in shapes],
        compiler_params=pltpu.CompilerParams(vmem_limit_bytes=6 * MIB),
        cost_estimate=cost(0),
        name="cast_units",
    )(in_hbm(local))
    results = []
    for _, _, _, p in wanted:
        results.append(out[:p])
        out = out[p:]
    return results


def sum_kernel(axis, cuts, n_a, n_b, *refs):
    a, b, outs = refs[:n_a], refs[n_a : n_a + n_b], refs[n_a + n_b :]
    total = join(a, axis).astype(jnp.float32) + join(b, axis).astype(jnp.float32)
    at = 0
    for out, n in zip(outs, cuts):
        piece = total[at : at + n] if axis else total[:, at : at + n]
        out[...] = piece.astype(out.dtype)
        at += n


def sum_pieces(a, b, axis, cuts):
    joined = sum(x.shape[axis] for x in a)
    return pl.pallas_call(
        functools.partial(sum_kernel, axis, cuts, len(a), len(b)),
        in_specs=[VMEM] * (len(a) + len(b)),
        out_specs=[VMEM] * len(cuts),
        out_shape=[jax.ShapeDtypeStruct((n, joined) if axis else (joined, n), jnp.bfloat16) for n in cuts],
        compiler_params=pltpu.CompilerParams(vmem_limit_bytes=6 * MIB),
        cost_estimate=cost(0),
        name="sum_pieces",
    )(*a, *b)


def token_kernel(n, place, source, *outs):
    rows, steps, _ = source.shape
    width = outs[0].shape[1]
    for d in range(n):
        at = pl.ds(pl.multiple_of((place[3] ^ d) * place[4] + place[5], HD), width)
        pieces = [source[r, :, at].astype(jnp.float32) for r in range(rows)]
        outs[d][...] = jnp.concatenate(pieces, axis=0).astype(jnp.bfloat16)


def token_pieces(place, tokens, n, width):
    row_count, steps, _ = tokens.shape
    return pl.pallas_call(
        functools.partial(token_kernel, n),
        grid_spec=pltpu.PrefetchScalarGridSpec(
            num_scalar_prefetch=1, grid=(), in_specs=[VMEM], out_specs=[VMEM] * n
        ),
        out_shape=[jax.ShapeDtypeStruct((row_count * steps, width), jnp.bfloat16)] * n,
        compiler_params=pltpu.CompilerParams(vmem_limit_bytes=4 * MIB),
        cost_estimate=cost(0),
        name="token_pieces",
    )(place, tokens)


def stack_kernel(takes, *refs):
    refs[-1][...] = jnp.concatenate([r[at * n : (at + 1) * n] for r, (at, n) in zip(refs[:-1], takes)], axis=0)


def stack_blocks(blocks, rows):
    arrays = [a for a, _ in blocks]
    return pl.pallas_call(
        functools.partial(stack_kernel, [(at, rows) for _, at in blocks]),
        in_specs=[VMEM] * len(arrays),
        out_specs=VMEM,
        out_shape=jax.ShapeDtypeStruct((rows * len(arrays), arrays[0].shape[1]), arrays[0].dtype),
        compiler_params=pltpu.CompilerParams(vmem_limit_bytes=4 * MIB),
        cost_estimate=cost(0),
        name="stack_blocks",
    )(*arrays)


def join(pieces, axis=0):
    return jnp.concatenate([p[...] for p in pieces], axis=axis)


def adam_kernel(first, n, n_mine, n_partner, tok_places, previous, hold, place, *refs):
    refs = list(refs)
    take = lambda n: [refs.pop(0) for _ in range(n)]
    pieces = take(n_mine + n_partner)
    state = take(3)
    toks = take(len(tok_places))
    take(3 * previous)
    updated = take(3)
    sent, kept = take(2)
    held = take(3 * hold)
    in_sems, out_sems, buffer = refs

    rows = buffer.shape[2]
    slabs = [(part, slice(*ends)) for part in range(2) for ends in slab_ends(rows)]
    columns = [columns_at(place, part, first, n) for part in range(2)]
    incoming = []
    for i, (part, at) in enumerate(slabs):
        incoming.append(
            [
                pltpu.make_async_copy(
                    state[q].at[at, columns[part]], buffer.at[q, part, at], in_sems.at[q, i]
                )
                for q in range(3)
            ]
        )
        for copy in incoming[i]:
            copy.start()
    block = sent.shape[0] // len(toks)
    tok = jnp.concatenate([t[k * block : (k + 1) * block] for t, k in zip(toks, tok_places)], axis=0)
    totals = [join(pieces[:n_mine]), join(pieces[n_mine:])]
    outgoing, products = [], [None, None]
    for i, (part, at) in enumerate(slabs):
        for copy in incoming[i]:
            copy.wait()
        gradient = totals[part][at].astype(jnp.float32)
        results = adam_update(buffer[0, part, at], buffer[1, part, at], buffer[2, part, at], gradient)
        for q in range(3):
            if hold and part == 1 and at.start >= held_from(rows):
                held[q][at.start - held_from(rows) : at.stop - held_from(rows)] = results[q]
                continue
            buffer[q, part, at] = results[q]
            outgoing.append(
                pltpu.make_async_copy(
                    buffer.at[q, part, at], updated[q].at[at, columns[part]], out_sems.at[q, i]
                )
            )
            outgoing[-1].start()
        terms = jnp.dot(tok[:, at], results[0].astype(jnp.bfloat16), preferred_element_type=jnp.float32)
        products[part] = terms if products[part] is None else products[part] + terms
    stays = place[0] == place[1]
    kept[...] = jnp.where(stays, products[0], products[1])
    sent[...] = jnp.where(stays, products[1], products[0]).astype(jnp.bfloat16)
    for copy in outgoing:
        copy.wait()


def adam_units(place, total, state, toks, first, n, previous, hold):
    mine, partner = total
    rows, width = state[0].shape
    n_slabs = 2 * len(slab_ends(rows))
    n_tokens = min(t.shape[0] for t, _ in toks) * len(toks)
    operands = [*mine, *partner, *[in_hbm(a) for a in state], *[t for t, _ in toks]]
    in_specs = [VMEM] * (len(mine) + len(partner)) + [ANYWHERE] * 3 + [VMEM] * len(toks)
    aliases = {}
    if previous is not None:
        aliases = {1 + len(operands) + i: i for i in range(3)}
        operands += previous
        in_specs += [ANYWHERE] * 3
    shape = (n_tokens, n * HD)
    out = pl.pallas_call(
        functools.partial(
            adam_kernel, first, n, len(mine), len(partner), [at for _, at in toks], previous is not None, hold
        ),
        grid_spec=pltpu.PrefetchScalarGridSpec(
            num_scalar_prefetch=1,
            grid=(),
            in_specs=in_specs,
            out_specs=[ANYWHERE] * 3 + [VMEM] * (2 + 3 * hold),
            scratch_shapes=[
                pltpu.SemaphoreType.DMA((3, n_slabs)),
                pltpu.SemaphoreType.DMA((3, n_slabs)),
                pltpu.VMEM((3, 2, rows, n * HD), jnp.float32),
            ],
        ),
        out_shape=[jax.ShapeDtypeStruct((rows, width), jnp.float32)] * 3
        + [jax.ShapeDtypeStruct(shape, jnp.bfloat16), jax.ShapeDtypeStruct(shape, jnp.float32)]
        + [jax.ShapeDtypeStruct((rows - held_from(rows), n * HD), jnp.float32)] * (3 * hold),
        input_output_aliases=aliases,
        compiler_params=pltpu.CompilerParams(vmem_limit_bytes=15 * MIB),
        cost_estimate=cost(0),
        name="adam_project",
    )(place, *operands)
    return out[:3], out[3:5], out[5:]


def write_kernel(first, n, place, *refs):
    held, outs, sems = refs[:3], refs[6:9], refs[9]
    copies = [
        pltpu.make_async_copy(
            held[q],
            outs[q].at[outs[q].shape[0] - held[q].shape[0] :, columns_at(place, 1, first, n)],
            sems.at[q],
        )
        for q in range(3)
    ]
    for copy in copies:
        copy.start()
    for copy in copies:
        copy.wait()


def write_held(place, held, previous, first, n):
    return pl.pallas_call(
        functools.partial(write_kernel, first, n),
        grid_spec=pltpu.PrefetchScalarGridSpec(
            num_scalar_prefetch=1,
            grid=(),
            in_specs=[VMEM] * 3 + [ANYWHERE] * 3,
            out_specs=[ANYWHERE] * 3,
            scratch_shapes=[pltpu.SemaphoreType.DMA((3,))],
        ),
        out_shape=[jax.ShapeDtypeStruct(p.shape, p.dtype) for p in previous],
        input_output_aliases={4: 0, 5: 1, 6: 2},
        compiler_params=pltpu.CompilerParams(vmem_limit_bytes=6 * MIB),
        cost_estimate=cost(2),
        name="write_held",
    )(place, *held, *previous)


SLOT = 32


def cache_kernel(heads, first, lens, q, k, v, stacked, acc, stats):
    step = pl.program_id(0)
    rows = q.shape[0]
    span = k.shape[1]
    used = PER_GROUP * STEPS
    for i in range(rows):
        length = lens[first + step * rows + i]
        query = q[i].astype(jnp.float32)
        scores = []
        for h in range(heads):
            pieces = [
                query[:, (h * PER_GROUP + g) * HD : (h * PER_GROUP + g + 1) * HD] for g in range(PER_GROUP)
            ]
            pieces.append(jnp.zeros((SLOT - used, HD), jnp.float32))
            one = jnp.concatenate(pieces, axis=0).astype(jnp.bfloat16)
            stacked[h, i] = one
            scores.append(
                lax.dot_general(
                    one,
                    k[i, :, h * HD : (h + 1) * HD],
                    (((1,), (1,)), ((), ())),
                    preferred_element_type=jnp.float32,
                )
            )
        scores = jnp.concatenate(scores, axis=0) * score_scale
        in_range = lax.broadcasted_iota(jnp.int32, (1, span), 1) < length
        scores = jnp.where(in_range, scores, masked_score)
        highest = jnp.max(scores, axis=-1, keepdims=True)
        weight = jnp.exp(scores - highest)
        total = jnp.sum(weight, axis=-1, keepdims=True)
        weight = weight.astype(jnp.bfloat16)
        lane = lax.broadcasted_iota(jnp.int32, (heads * SLOT, HD), 1)
        stat = jnp.where(lane < HD // 2, highest, total)
        for h in range(heads):
            at = slice(h * SLOT, (h + 1) * SLOT)
            acc[h, i] = jnp.dot(
                weight[at], v[i, :, h * HD : (h + 1) * HD], preferred_element_type=jnp.float32
            )
            stats[h, i] = stat[at]


def cache_attention(queries, cache_keys, cache_values, lengths, first, row_count):
    _, span, kv_cols = cache_keys.shape
    heads = kv_cols // HD
    rows = 2 if row_count % 2 == 0 and first % 2 == 0 else 1
    shape = (heads, row_count, SLOT, HD)
    out_block = pl.BlockSpec((heads, rows, SLOT, HD), lambda r, lens: (0, r, 0, 0))
    in_block = lambda a: pl.BlockSpec((rows, *a.shape[1:]), lambda r, lens: (first // rows + r, 0, 0))
    return pl.pallas_call(
        functools.partial(cache_kernel, heads, first),
        grid_spec=pltpu.PrefetchScalarGridSpec(
            num_scalar_prefetch=1,
            grid=(row_count // rows,),
            in_specs=[in_block(queries), in_block(cache_keys), in_block(cache_values)],
            out_specs=[out_block] * 3,
        ),
        out_shape=[
            jax.ShapeDtypeStruct(shape, jnp.bfloat16),
            jax.ShapeDtypeStruct(shape, jnp.float32),
            jax.ShapeDtypeStruct(shape, jnp.float32),
        ],
        compiler_params=pltpu.CompilerParams(vmem_limit_bytes=10 * MIB),
        cost_estimate=cost(7),
        name="cache_attention",
    )(lengths, in_hbm(queries), in_hbm(cache_keys), in_hbm(cache_values))


def merge_kernel(spans, first, n_heads, *refs):
    folds, refs = refs[: 2 * len(spans)], refs[2 * len(spans) :]
    cosine, sine, stacked, acc, stats = refs[:5]
    new_kv, context = refs[-2:]
    row_count = new_kv.shape[0]
    every = jnp.concatenate(
        [
            folds[2 * f][:, span].astype(jnp.float32) + folds[2 * f + 1][:, span]
            for f, span in enumerate(spans)
        ],
        axis=1,
    )
    at = lax.broadcasted_iota(jnp.int32, (row_count * SLOT, row_count * STEPS), 0)
    to = lax.broadcasted_iota(jnp.int32, (row_count * SLOT, row_count * STEPS), 1)
    seen = (at // SLOT == to // STEPS) & (at % STEPS >= to % STEPS)
    rows_of = lambda a, u: a[first + u].reshape(-1, HD)
    for u in range(n_heads):
        total = every[:, u * HEAD_COLS : (u + 1) * HEAD_COLS]
        keys = total[:, :HD]
        keys = keys * cosine[...] + pltpu.roll(keys, HD // 2, 1) * sine[...]
        keys = keys.astype(jnp.bfloat16)
        values = total[:, HD:].astype(jnp.bfloat16)
        both = jnp.concatenate([keys, values], axis=1).astype(jnp.float32)
        for r in range(row_count):
            new_kv[r, :, u * HEAD_COLS : (u + 1) * HEAD_COLS] = both[
                r * STEPS : (r + 1) * STEPS
            ].astype(jnp.bfloat16)
        scores = (
            lax.dot_general(
                rows_of(stacked, u), keys, (((1,), (1,)), ((), ())), preferred_element_type=jnp.float32
            )
            * score_scale
        )
        scores = jnp.where(seen, scores, masked_score)
        stat = rows_of(stats, u)
        old_highest = stat[:, :1]
        old_total = stat[:, HD // 2 : HD // 2 + 1]
        highest = jnp.maximum(jnp.max(scores, axis=-1, keepdims=True), old_highest)
        weight = jnp.exp(scores - highest)
        scale = jnp.exp(old_highest - highest)
        denominator = jnp.sum(weight, axis=-1, keepdims=True) + scale * old_total
        out = jnp.dot(weight.astype(jnp.bfloat16), values, preferred_element_type=jnp.float32)
        out = (out + scale * rows_of(acc, u)) / denominator
        for r in range(row_count):
            for g in range(PER_GROUP):
                at_row = r * SLOT + g * STEPS
                at_col = (u * PER_GROUP + g) * HD
                context[r, :, at_col : at_col + HD] = out[at_row : at_row + STEPS].astype(jnp.bfloat16)


def merge(folds, cosine, sine, attended, row_count, first, n_heads, previous):
    heads = attended[0].shape[0]
    block = first // n_heads
    operands = [a for fold in folds for a in fold[:2]] + [cosine, sine, *attended]
    in_specs = [VMEM] * len(operands)
    aliases = {}
    if previous is not None:
        aliases = {len(operands) + i: i for i in range(2)}
        operands += previous
        in_specs += [ANYWHERE] * 2
    widths = (HEAD_COLS, PER_GROUP * HD)
    return pl.pallas_call(
        functools.partial(merge_kernel, [fold[2] for fold in folds], first, n_heads),
        grid=(1,),
        in_specs=in_specs,
        out_specs=[pl.BlockSpec((row_count, STEPS, n_heads * w), lambda i: (0, 0, block)) for w in widths],
        out_shape=[jax.ShapeDtypeStruct((row_count, STEPS, heads * w), jnp.bfloat16) for w in widths],
        input_output_aliases=aliases,
        compiler_params=pltpu.CompilerParams(vmem_limit_bytes=8 * MIB),
        cost_estimate=cost(0),
        name="merge_new",
    )(*operands)


def swap(array, axis, bit):
    size = lax.axis_size(axis)
    return lax.ppermute(array, axis, [(i, i ^ bit) for i in range(size)])


def reversed_bits(n):
    order = [0]
    while len(order) < n:
        order = [2 * i for i in order] + [2 * i + 1 for i in order]
    return order


def fold_rows(arrived, kept, n):
    total = arrived.astype(jnp.float32) + kept
    half = total.shape[0] // 2
    return total[half:].astype(jnp.bfloat16), total[:half]


def butterfly_shards(
    tokens, queries, cache_keys, cache_values, lengths, weights, moment1, moment2, grad_parts
):
    fsdp_count = lax.axis_size("fsdp")
    tp_count = lax.axis_size("tp")
    core = lax.axis_index("group") % 2
    fsdp = lax.axis_index("fsdp")
    tp = lax.axis_index("tp")
    rows, width = weights.shape
    row_count = tokens.shape[0]
    n_units = width // (tp_count * HD)
    local = grad_parts[0]
    place = jnp.stack(
        [core, tp, jnp.full_like(core, n_units), fsdp, jnp.full_like(core, tp_count * rows), tp * rows]
    ).astype(jnp.int32)

    n_first = n_units // 2
    n_extra = n_units // 8
    n_early = n_first + n_extra
    n_late = n_units - n_early

    def chip_sum(away, home, cuts):
        return sum_pieces([home], [swap(a, "group", 1) for a in away], 0, cuts)

    (away,) = cast_units(local, n_units, [(1, 0, n_first, 1)])
    ((home,),) = cast_units(after(local, *away), n_units, [(0, 0, n_first, 1)])
    (begun,) = chip_sum(away, home, [n_first * HD])
    early, crossed = [begun], [swap(begun, "group", 2)]

    n_tokens = row_count * STEPS
    blocks = [(t, 0) for t in token_pieces(place, after(tokens, begun), fsdp_count, rows)]
    source = after(local, begun, *[t for t, _ in blocks])
    n_rest = n_units - n_first
    away, (home,) = cast_units(source, n_units, [(1, n_first, n_rest, N_PIECES), (0, n_first, n_rest, 1)])
    *more, last = chip_sum(away, home, [n * HD for n in (n_extra, n_late) if n])
    early += more
    crossed += [swap(m, "group", 2) for m in more]
    crossed_last = swap(last, "group", 2)

    cosine, sine = rotation_tables(lengths)
    ready = [*early, last]
    attended = cache_attention(after(queries, *ready), cache_keys, cache_values, lengths, 0, row_count)
    distance = fsdp_count // 2
    step = (attended[1],)
    while distance:
        going = [d for d in range(fsdp_count) if d & distance]
        leaving = [blocks[d] for d in going]
        if distance < fsdp_count // 2:
            leaving = [(after(t, attended[1]), at) for t, at in leaving]
        stacked = stack_blocks(leaving, n_tokens)
        got = swap(stacked, "fsdp", distance)
        for i, d in enumerate(going):
            blocks[d] = (got, i)
        distance //= 2
        step = (attended[1], got)
    toks = [blocks[d] for d in reversed_bits(fsdp_count)]

    state = (weights, moment1, moment2)

    def total(parts, arrived, n_pieces, *earlier):
        arrived = list(lax.optimization_barrier((*arrived, *earlier)))[: len(arrived)]
        one = sum_pieces(parts, arrived, 1, [rows // n_pieces] * n_pieces)
        return one, [swap(p, "group", 1) for p in one]

    both = total(early, crossed, N_PIECES, *step)
    updated, (sent, kept), _ = adam_units(place, both, state, toks, 0, n_early, None, False)
    moving = [(swap(sent, "tp", 1), kept)]
    both = total([last], [crossed_last], 1, sent)
    updated, (sent, kept), held = adam_units(place, both, state, toks, n_early, n_late, updated, True)
    updated = write_held(after(place, sent), held, updated, n_early, n_late)
    moving.append((after(swap(sent, "tp", 1), updated[0]), kept))
    distance = 1
    while distance < fsdp_count:
        for f, (got, kept) in enumerate(moving):
            sent, kept = fold_rows(got, kept, fsdp_count)
            moving[f] = (swap(sent, "fsdp", distance), kept)
        distance *= 2

    n_heads = n_units * HD // HEAD_COLS
    whole_heads = n_heads // 2
    split = whole_heads * HEAD_COLS
    outs = merge(
        [(*moving[0], slice(0, split))], cosine, sine, attended, row_count, 0, whole_heads, None
    )
    parts = [(*moving[0], slice(split, n_early * HD)), (*moving[1], slice(0, n_late * HD))]
    outs = merge(
        parts[0 if split < n_early * HD else 1 :],
        cosine,
        sine,
        attended,
        row_count,
        whole_heads,
        n_heads - whole_heads,
        outs,
    )
    return (*updated, *outs)


def rotate_keys(keys, positions):
    half_width = keys.shape[-1] // 2
    frequency = jnp.power(
        jnp.float32(1000000.0), -2.0 * jnp.arange(half_width, dtype=jnp.float32) / keys.shape[-1]
    )
    angles = positions[..., None] * frequency
    leading = keys[..., :half_width]
    trailing = keys[..., half_width:]
    cosine = jnp.cos(angles)
    sine_part = jnp.sin(angles)
    return jnp.concatenate(
        [leading * cosine - trailing * sine_part, trailing * cosine + leading * sine_part], axis=-1
    )


def plain_shards(
    tokens, queries, cache_keys, cache_values, lengths, weights, moment1, moment2, grad_parts
):
    gradient = lax.psum(grad_parts[0], "group")
    new_weights, new_moment1, new_moment2 = adam_update(weights, moment1, moment2, gradient)
    weight_shard = new_weights.astype(jnp.bfloat16)
    tp_count = lax.axis_size("tp")
    fsdp_count = lax.axis_size("fsdp")
    head_cols = weight_shard.shape[1] // tp_count
    row_count = tokens.shape[0]
    block_rows = weight_shard.shape[0]
    split_tokens = tokens.reshape(row_count, STEPS, fsdp_count, tp_count, block_rows)
    own_columns = lax.dynamic_index_in_dim(split_tokens, lax.axis_index("tp"), 3, keepdims=False)
    arrived = lax.all_to_all(own_columns, "fsdp", split_axis=2, concat_axis=0, tiled=True)
    arrived = arrived.reshape(fsdp_count * row_count * STEPS, block_rows)
    partial_terms = jnp.dot(arrived, weight_shard, preferred_element_type=jnp.float32)
    partial_terms = partial_terms.reshape(fsdp_count, row_count * STEPS, tp_count, head_cols)
    partial_terms = partial_terms.transpose(0, 2, 1, 3).reshape(
        fsdp_count * tp_count * row_count * STEPS, head_cols
    )
    projected = lax.psum_scatter(partial_terms, ("fsdp", "tp"), scatter_dimension=0, tiled=True)
    kv_heads = head_cols // (2 * HD)
    projected = projected.reshape(row_count, STEPS, kv_heads, 2, HD)
    positions = (lengths[:, None] + jnp.arange(STEPS, dtype=jnp.int32)[None, :]).astype(jnp.float32)
    new_keys = rotate_keys(projected[:, :, :, 0], positions[:, :, None])
    fresh = jnp.stack([new_keys, projected[:, :, :, 1]], axis=3).astype(jnp.bfloat16)
    new_kv = fresh.reshape(row_count, STEPS, head_cols)
    span_length = cache_keys.shape[1]
    grouped = queries.reshape(row_count, STEPS, kv_heads, PER_GROUP, HD)
    cached_keys = cache_keys.reshape(row_count, span_length, kv_heads, HD)
    cached_values = cache_values.reshape(row_count, span_length, kv_heads, HD)
    new_scores = (
        jnp.einsum(
            "risgd,rjsd->risgj", grouped, fresh[:, :, :, 0], preferred_element_type=jnp.float32
        )
        * score_scale
    )
    causal = jnp.arange(STEPS)[:, None] >= jnp.arange(STEPS)[None, :]
    new_scores = jnp.where(causal[None, :, None, None, :], new_scores, masked_score)
    scores = (
        jnp.einsum("risgd,rpsd->risgp", grouped, cached_keys, preferred_element_type=jnp.float32)
        * score_scale
    )
    in_range = jnp.arange(span_length, dtype=jnp.int32)[None, :] < lengths[:, None]
    all_scores = jnp.concatenate(
        [jnp.where(in_range[:, None, None, None, :], scores, masked_score), new_scores], axis=-1
    )
    highest = jnp.max(all_scores, axis=-1, keepdims=True)
    exponent = jnp.exp(all_scores - highest)
    probs = (exponent / jnp.sum(exponent, axis=-1, keepdims=True)).astype(jnp.bfloat16)
    context = jnp.einsum(
        "risgp,rpsd->risgd",
        probs[..., :span_length],
        cached_values,
        preferred_element_type=jnp.float32,
    )
    context = context + jnp.einsum(
        "risgj,rjsd->risgd",
        probs[..., span_length:],
        fresh[:, :, :, 1],
        preferred_element_type=jnp.float32,
    )
    context = context.reshape(row_count, STEPS, kv_heads * PER_GROUP * HD).astype(jnp.bfloat16)
    return (new_weights, new_moment1, new_moment2, new_kv, context)


def power_of_two(n):
    return n > 1 and n & (n - 1) == 0


def solution(mesh):
    in_specs = (
        P(("group", "fsdp"), None, None),
        P(("group", "fsdp"), None, "tp"),
        P(("group", "fsdp"), None, "tp"),
        P(("group", "fsdp"), None, "tp"),
        P(("group", "fsdp")),
        P(("fsdp", "tp"), None),
        P(("fsdp", "tp"), None),
        P(("fsdp", "tp"), None),
        P("group", ("fsdp", "tp"), None),
    )
    out_specs = (
        P(("fsdp", "tp"), None),
        P(("fsdp", "tp"), None),
        P(("fsdp", "tp"), None),
        P(("group", "fsdp"), None, "tp"),
        P(("group", "fsdp"), None, "tp"),
    )
    sizes = mesh.shape
    pairwise = sizes["group"] == 4 and power_of_two(sizes["fsdp"]) and sizes["tp"] == 2
    shards = butterfly_shards if pairwise else plain_shards
    return jax.shard_map(shards, mesh=mesh, in_specs=in_specs, out_specs=out_specs, check_vma=False)
```

```python
import functools
import math

import jax
import jax.numpy as jnp
from jax import lax
from jax.experimental import pallas as pl
from jax.experimental.pallas import tpu as pltpu
from jax.sharding import PartitionSpec as P

QH = 40
KVH = 8
HD = 128
STEPS = 4
PER_GROUP = QH // KVH
HEAD_COLS = 2 * HD


beta_one = 0.9
beta_two = 0.95
learning_rate = 0.004
decay_rate = 0.1
epsilon = 1e-08
correct_one = 1.0 - 0.9**10
correct_two = 1.0 - 0.95**10
masked_score = -1e30
score_scale = 1.0 / math.sqrt(HD)

N_PIECES = 2
MIB = 1024 * 1024


def adam_update(weights, moment1, moment2, gradient):
    new_moment1 = beta_one * moment1 + (1.0 - beta_one) * gradient
    new_moment2 = beta_two * moment2 + (1.0 - beta_two) * gradient * gradient
    direction = new_moment1 / correct_one / (jnp.sqrt(new_moment2 / correct_two) + epsilon)
    new_weights = weights - learning_rate * (direction + decay_rate * weights)
    return (new_weights, new_moment1, new_moment2)


def rotation_tables(lengths):
    half_width = HD // 2
    frequency = jnp.power(
        jnp.float32(1000000.0), -2.0 * jnp.arange(half_width, dtype=jnp.float32) / HD
    )
    positions = (lengths[:, None] + jnp.arange(STEPS, dtype=jnp.int32)[None, :]).astype(jnp.float32)
    angles = positions.reshape(-1)[:, None] * frequency
    cosine = jnp.cos(angles)
    sine = jnp.sin(angles)
    return (
        jnp.concatenate([cosine, cosine], axis=-1),
        jnp.concatenate([-sine, sine], axis=-1),
    )


def whole(a):
    return pl.BlockSpec(a.shape, lambda *_: (0,) * len(a.shape))


def after(value, *earlier):
    return lax.optimization_barrier((value, *earlier))[0] if earlier else value


def cost(busy_us):
    return pl.CostEstimate(flops=1, bytes_accessed=max(1, int(busy_us * 2.5e6)), transcendentals=0)


def in_hbm(a):
    return pltpu.with_memory_space_constraint(a, pltpu.HBM)


VMEM = pl.BlockSpec(memory_space=pltpu.VMEM)
ANYWHERE = pl.BlockSpec(memory_space=pl.ANY)


def columns_at(place, part, first, n):
    half = place[0] if part == 0 else 1 - place[0]
    return pl.ds(pl.multiple_of((half * place[2] + first) * HD, HD), n * HD)


def slab_ends(rows):
    if rows % HD:
        return [(0, rows)]
    return [(r, min(r + 2 * HD, rows)) for r in range(0, rows, 2 * HD)]


def held_from(rows):
    return slab_ends(rows)[-2:][0][0]


def cast_kernel(wanted, n_units, source, *refs):
    outs, buffers, sems = refs[: -len(wanted) - 1], refs[-len(wanted) - 1 : -1], refs[-1]
    place = (lax.axis_index("group") % 2, None, n_units)
    ends = slab_ends(source.shape[0])
    copies = [
        [
            pltpu.make_async_copy(
                source.at[r:e, columns_at(place, part, first, n)], buffers[w].at[r:e], sems.at[w, i]
            )
            for i, (r, e) in enumerate(ends)
        ]
        for w, (part, first, n, _) in enumerate(wanted)
    ]
    for copy in sum(copies, []):
        copy.start()
    at = 0
    for w, (_, _, _, n_pieces) in enumerate(wanted):
        if n_pieces == 1:
            for copy, (r, e) in zip(copies[w], ends):
                copy.wait()
                outs[at][r:e] = buffers[w][r:e].astype(jnp.bfloat16)
        else:
            for copy in copies[w]:
                copy.wait()
            step = buffers[w].shape[0] // n_pieces
            for p in range(n_pieces):
                outs[at + p][...] = buffers[w][p * step : (p + 1) * step].astype(jnp.bfloat16)
        at += n_pieces


def cast_units(local, n_units, wanted):
    rows = local.shape[0]
    shapes = [(rows // p, n * HD) for _, _, n, p in wanted for _ in range(p)]
    out = pl.pallas_call(
        functools.partial(cast_kernel, wanted, n_units),
        in_specs=[ANYWHERE],
        out_specs=[VMEM] * len(shapes),
        scratch_shapes=[pltpu.VMEM((rows, n * HD), jnp.float32) for _, _, n, _ in wanted]
        + [pltpu.SemaphoreType.DMA((len(wanted), len(slab_ends(rows))))],
        out_shape=[jax.ShapeDtypeStruct(shape, jnp.bfloat16) for shape in shapes],
        compiler_params=pltpu.CompilerParams(vmem_limit_bytes=6 * MIB),
        cost_estimate=cost(0),
        name="cast_units",
    )(in_hbm(local))
    results = []
    for _, _, _, p in wanted:
        results.append(out[:p])
        out = out[p:]
    return results


def sum_kernel(axis, cuts, n_a, n_b, *refs):
    a, b, outs = refs[:n_a], refs[n_a : n_a + n_b], refs[n_a + n_b :]
    total = join(a, axis).astype(jnp.float32) + join(b, axis).astype(jnp.float32)
    at = 0
    for out, n in zip(outs, cuts):
        piece = total[at : at + n] if axis else total[:, at : at + n]
        out[...] = piece.astype(out.dtype)
        at += n


def sum_pieces(a, b, axis, cuts):
    joined = sum(x.shape[axis] for x in a)
    return pl.pallas_call(
        functools.partial(sum_kernel, axis, cuts, len(a), len(b)),
        in_specs=[VMEM] * (len(a) + len(b)),
        out_specs=[VMEM] * len(cuts),
        out_shape=[jax.ShapeDtypeStruct((n, joined) if axis else (joined, n), jnp.bfloat16) for n in cuts],
        compiler_params=pltpu.CompilerParams(vmem_limit_bytes=6 * MIB),
        cost_estimate=cost(0),
        name="sum_pieces",
    )(*a, *b)


def token_kernel(n, place, source, *outs):
    rows, steps, _ = source.shape
    width = outs[0].shape[1]
    for d in range(n):
        at = pl.ds(pl.multiple_of((place[3] ^ d) * place[4] + place[5], HD), width)
        pieces = [source[r, :, at].astype(jnp.float32) for r in range(rows)]
        outs[d][...] = jnp.concatenate(pieces, axis=0).astype(jnp.bfloat16)


def token_pieces(place, tokens, n, width):
    row_count, steps, _ = tokens.shape
    return pl.pallas_call(
        functools.partial(token_kernel, n),
        grid_spec=pltpu.PrefetchScalarGridSpec(
            num_scalar_prefetch=1, grid=(), in_specs=[VMEM], out_specs=[VMEM] * n
        ),
        out_shape=[jax.ShapeDtypeStruct((row_count * steps, width), jnp.bfloat16)] * n,
        compiler_params=pltpu.CompilerParams(vmem_limit_bytes=4 * MIB),
        cost_estimate=cost(0),
        name="token_pieces",
    )(place, tokens)


def stack_kernel(takes, *refs):
    refs[-1][...] = jnp.concatenate([r[at * n : (at + 1) * n] for r, (at, n) in zip(refs[:-1], takes)], axis=0)


def stack_blocks(blocks, rows):
    arrays = [a for a, _ in blocks]
    return pl.pallas_call(
        functools.partial(stack_kernel, [(at, rows) for _, at in blocks]),
        in_specs=[VMEM] * len(arrays),
        out_specs=VMEM,
        out_shape=jax.ShapeDtypeStruct((rows * len(arrays), arrays[0].shape[1]), arrays[0].dtype),
        compiler_params=pltpu.CompilerParams(vmem_limit_bytes=4 * MIB),
        cost_estimate=cost(0),
        name="stack_blocks",
    )(*arrays)


def join(pieces, axis=0):
    return jnp.concatenate([p[...] for p in pieces], axis=axis)


def adam_kernel(first, n, n_mine, n_partner, tok_places, previous, hold, place, *refs):
    refs = list(refs)
    take = lambda n: [refs.pop(0) for _ in range(n)]
    pieces = take(n_mine + n_partner)
    state = take(3)
    toks = take(len(tok_places))
    take(3 * previous)
    updated = take(3)
    sent, kept = take(2)
    held = take(3 * hold)
    in_sems, out_sems, buffer = refs

    rows = buffer.shape[2]
    slabs = [(part, slice(*ends)) for part in range(2) for ends in slab_ends(rows)]
    columns = [columns_at(place, part, first, n) for part in range(2)]
    incoming = []
    for i, (part, at) in enumerate(slabs):
        incoming.append(
            [
                pltpu.make_async_copy(
                    state[q].at[at, columns[part]], buffer.at[q, part, at], in_sems.at[q, i]
                )
                for q in range(3)
            ]
        )
        for copy in incoming[i]:
            copy.start()
    block = sent.shape[0] // len(toks)
    tok = jnp.concatenate([t[k * block : (k + 1) * block] for t, k in zip(toks, tok_places)], axis=0)
    totals = [join(pieces[:n_mine]), join(pieces[n_mine:])]
    outgoing, products = [], [None, None]
    for i, (part, at) in enumerate(slabs):
        for copy in incoming[i]:
            copy.wait()
        gradient = totals[part][at].astype(jnp.float32)
        results = adam_update(buffer[0, part, at], buffer[1, part, at], buffer[2, part, at], gradient)
        for q in range(3):
            if hold and part == 1 and at.start >= held_from(rows):
                held[q][at.start - held_from(rows) : at.stop - held_from(rows)] = results[q]
                continue
            buffer[q, part, at] = results[q]
            outgoing.append(
                pltpu.make_async_copy(
                    buffer.at[q, part, at], updated[q].at[at, columns[part]], out_sems.at[q, i]
                )
            )
            outgoing[-1].start(priority=1)
        terms = jnp.dot(tok[:, at], results[0].astype(jnp.bfloat16), preferred_element_type=jnp.float32)
        products[part] = terms if products[part] is None else products[part] + terms
    stays = place[0] == place[1]
    kept[...] = jnp.where(stays, products[0], products[1])
    sent[...] = jnp.where(stays, products[1], products[0]).astype(jnp.bfloat16)
    for copy in outgoing:
        copy.wait()


def adam_units(place, total, state, toks, first, n, previous, hold):
    mine, partner = total
    rows, width = state[0].shape
    n_slabs = 2 * len(slab_ends(rows))
    n_tokens = min(t.shape[0] for t, _ in toks) * len(toks)
    operands = [*mine, *partner, *[in_hbm(a) for a in state], *[t for t, _ in toks]]
    in_specs = [VMEM] * (len(mine) + len(partner)) + [ANYWHERE] * 3 + [VMEM] * len(toks)
    aliases = {}
    if previous is not None:
        aliases = {1 + len(operands) + i: i for i in range(3)}
        operands += previous
        in_specs += [ANYWHERE] * 3
    shape = (n_tokens, n * HD)
    out = pl.pallas_call(
        functools.partial(
            adam_kernel, first, n, len(mine), len(partner), [at for _, at in toks], previous is not None, hold
        ),
        grid_spec=pltpu.PrefetchScalarGridSpec(
            num_scalar_prefetch=1,
            grid=(),
            in_specs=in_specs,
            out_specs=[ANYWHERE] * 3 + [VMEM] * (2 + 3 * hold),
            scratch_shapes=[
                pltpu.SemaphoreType.DMA((3, n_slabs)),
                pltpu.SemaphoreType.DMA((3, n_slabs)),
                pltpu.VMEM((3, 2, rows, n * HD), jnp.float32),
            ],
        ),
        out_shape=[jax.ShapeDtypeStruct((rows, width), jnp.float32)] * 3
        + [jax.ShapeDtypeStruct(shape, jnp.bfloat16), jax.ShapeDtypeStruct(shape, jnp.float32)]
        + [jax.ShapeDtypeStruct((rows - held_from(rows), n * HD), jnp.float32)] * (3 * hold),
        input_output_aliases=aliases,
        compiler_params=pltpu.CompilerParams(vmem_limit_bytes=15 * MIB),
        cost_estimate=cost(0),
        name="adam_project",
    )(place, *operands)
    return out[:3], out[3:5], out[5:]


def write_kernel(first, n, place, *refs):
    held, outs, sems = refs[:3], refs[6:9], refs[9]
    copies = [
        pltpu.make_async_copy(
            held[q],
            outs[q].at[outs[q].shape[0] - held[q].shape[0] :, columns_at(place, 1, first, n)],
            sems.at[q],
        )
        for q in range(3)
    ]
    for copy in copies:
        copy.start()
    for copy in copies:
        copy.wait()


def write_held(place, held, previous, first, n):
    return pl.pallas_call(
        functools.partial(write_kernel, first, n),
        grid_spec=pltpu.PrefetchScalarGridSpec(
            num_scalar_prefetch=1,
            grid=(),
            in_specs=[VMEM] * 3 + [ANYWHERE] * 3,
            out_specs=[ANYWHERE] * 3,
            scratch_shapes=[pltpu.SemaphoreType.DMA((3,))],
        ),
        out_shape=[jax.ShapeDtypeStruct(p.shape, p.dtype) for p in previous],
        input_output_aliases={4: 0, 5: 1, 6: 2},
        compiler_params=pltpu.CompilerParams(vmem_limit_bytes=6 * MIB),
        cost_estimate=cost(2),
        name="write_held",
    )(place, *held, *previous)


SLOT = 32


def cache_kernel(heads, first, lens, q, k, v, stacked, acc, stats):
    step = pl.program_id(0)
    rows = q.shape[0]
    span = k.shape[1]
    used = PER_GROUP * STEPS
    for i in range(rows):
        length = lens[first + step * rows + i]
        query = q[i].astype(jnp.float32)
        scores = []
        for h in range(heads):
            pieces = [
                query[:, (h * PER_GROUP + g) * HD : (h * PER_GROUP + g + 1) * HD] for g in range(PER_GROUP)
            ]
            pieces.append(jnp.zeros((SLOT - used, HD), jnp.float32))
            one = jnp.concatenate(pieces, axis=0).astype(jnp.bfloat16)
            stacked[h, i] = one
            scores.append(
                lax.dot_general(
                    one,
                    k[i, :, h * HD : (h + 1) * HD],
                    (((1,), (1,)), ((), ())),
                    preferred_element_type=jnp.float32,
                )
            )
        scores = jnp.concatenate(scores, axis=0) * score_scale
        in_range = lax.broadcasted_iota(jnp.int32, (1, span), 1) < length
        scores = jnp.where(in_range, scores, masked_score)
        highest = jnp.max(scores, axis=-1, keepdims=True)
        weight = jnp.exp(scores - highest)
        total = jnp.sum(weight, axis=-1, keepdims=True)
        weight = weight.astype(jnp.bfloat16)
        lane = lax.broadcasted_iota(jnp.int32, (heads * SLOT, HD), 1)
        stat = jnp.where(lane < HD // 2, highest, total)
        for h in range(heads):
            at = slice(h * SLOT, (h + 1) * SLOT)
            acc[h, i] = jnp.dot(
                weight[at], v[i, :, h * HD : (h + 1) * HD], preferred_element_type=jnp.float32
            )
            stats[h, i] = stat[at]


def cache_attention(queries, cache_keys, cache_values, lengths, first, row_count):
    _, span, kv_cols = cache_keys.shape
    heads = kv_cols // HD
    rows = 2 if row_count % 2 == 0 and first % 2 == 0 else 1
    shape = (heads, row_count, SLOT, HD)
    out_block = pl.BlockSpec((heads, rows, SLOT, HD), lambda r, lens: (0, r, 0, 0))
    in_block = lambda a: pl.BlockSpec((rows, *a.shape[1:]), lambda r, lens: (first // rows + r, 0, 0))
    return pl.pallas_call(
        functools.partial(cache_kernel, heads, first),
        grid_spec=pltpu.PrefetchScalarGridSpec(
            num_scalar_prefetch=1,
            grid=(row_count // rows,),
            in_specs=[in_block(queries), in_block(cache_keys), in_block(cache_values)],
            out_specs=[out_block] * 3,
        ),
        out_shape=[
            jax.ShapeDtypeStruct(shape, jnp.bfloat16),
            jax.ShapeDtypeStruct(shape, jnp.float32),
            jax.ShapeDtypeStruct(shape, jnp.float32),
        ],
        compiler_params=pltpu.CompilerParams(vmem_limit_bytes=10 * MIB),
        cost_estimate=cost(7),
        name="cache_attention",
    )(lengths, in_hbm(queries), in_hbm(cache_keys), in_hbm(cache_values))


def merge_kernel(spans, first, n_heads, *refs):
    folds, refs = refs[: 2 * len(spans)], refs[2 * len(spans) :]
    cosine, sine, stacked, acc, stats = refs[:5]
    new_kv, context = refs[-2:]
    row_count = new_kv.shape[0]
    every = jnp.concatenate(
        [
            folds[2 * f][:, span].astype(jnp.float32) + folds[2 * f + 1][:, span]
            for f, span in enumerate(spans)
        ],
        axis=1,
    )
    at = lax.broadcasted_iota(jnp.int32, (row_count * SLOT, row_count * STEPS), 0)
    to = lax.broadcasted_iota(jnp.int32, (row_count * SLOT, row_count * STEPS), 1)
    seen = (at // SLOT == to // STEPS) & (at % STEPS >= to % STEPS)
    rows_of = lambda a, u: a[first + u].reshape(-1, HD)
    for u in range(n_heads):
        total = every[:, u * HEAD_COLS : (u + 1) * HEAD_COLS]
        keys = total[:, :HD]
        keys = keys * cosine[...] + pltpu.roll(keys, HD // 2, 1) * sine[...]
        keys = keys.astype(jnp.bfloat16)
        values = total[:, HD:].astype(jnp.bfloat16)
        both = jnp.concatenate([keys, values], axis=1).astype(jnp.float32)
        for r in range(row_count):
            new_kv[r, :, u * HEAD_COLS : (u + 1) * HEAD_COLS] = both[
                r * STEPS : (r + 1) * STEPS
            ].astype(jnp.bfloat16)
        scores = (
            lax.dot_general(
                rows_of(stacked, u), keys, (((1,), (1,)), ((), ())), preferred_element_type=jnp.float32
            )
            * score_scale
        )
        scores = jnp.where(seen, scores, masked_score)
        stat = rows_of(stats, u)
        old_highest = stat[:, :1]
        old_total = stat[:, HD // 2 : HD // 2 + 1]
        highest = jnp.maximum(jnp.max(scores, axis=-1, keepdims=True), old_highest)
        weight = jnp.exp(scores - highest)
        scale = jnp.exp(old_highest - highest)
        denominator = jnp.sum(weight, axis=-1, keepdims=True) + scale * old_total
        out = jnp.dot(weight.astype(jnp.bfloat16), values, preferred_element_type=jnp.float32)
        out = (out + scale * rows_of(acc, u)) / denominator
        for r in range(row_count):
            for g in range(PER_GROUP):
                at_row = r * SLOT + g * STEPS
                at_col = (u * PER_GROUP + g) * HD
                context[r, :, at_col : at_col + HD] = out[at_row : at_row + STEPS].astype(jnp.bfloat16)


def merge(folds, cosine, sine, attended, row_count, first, n_heads, previous):
    heads = attended[0].shape[0]
    block = first // n_heads
    operands = [a for fold in folds for a in fold[:2]] + [cosine, sine, *attended]
    in_specs = [VMEM] * len(operands)
    aliases = {}
    if previous is not None:
        aliases = {len(operands) + i: i for i in range(2)}
        operands += previous
        in_specs += [ANYWHERE] * 2
    widths = (HEAD_COLS, PER_GROUP * HD)
    return pl.pallas_call(
        functools.partial(merge_kernel, [fold[2] for fold in folds], first, n_heads),
        grid=(1,),
        in_specs=in_specs,
        out_specs=[pl.BlockSpec((row_count, STEPS, n_heads * w), lambda i: (0, 0, block)) for w in widths],
        out_shape=[jax.ShapeDtypeStruct((row_count, STEPS, heads * w), jnp.bfloat16) for w in widths],
        input_output_aliases=aliases,
        compiler_params=pltpu.CompilerParams(vmem_limit_bytes=8 * MIB),
        cost_estimate=cost(0),
        name="merge_new",
    )(*operands)


def swap(array, axis, bit):
    size = lax.axis_size(axis)
    return lax.ppermute(array, axis, [(i, i ^ bit) for i in range(size)])


def reversed_bits(n):
    order = [0]
    while len(order) < n:
        order = [2 * i for i in order] + [2 * i + 1 for i in order]
    return order


def fold_rows(arrived, kept, n):
    total = arrived.astype(jnp.float32) + kept
    half = total.shape[0] // 2
    return total[half:].astype(jnp.bfloat16), total[:half]


def butterfly_shards(
    tokens, queries, cache_keys, cache_values, lengths, weights, moment1, moment2, grad_parts
):
    fsdp_count = lax.axis_size("fsdp")
    tp_count = lax.axis_size("tp")
    core = lax.axis_index("group") % 2
    fsdp = lax.axis_index("fsdp")
    tp = lax.axis_index("tp")
    rows, width = weights.shape
    row_count = tokens.shape[0]
    n_units = width // (tp_count * HD)
    local = grad_parts[0]
    place = jnp.stack(
        [core, tp, jnp.full_like(core, n_units), fsdp, jnp.full_like(core, tp_count * rows), tp * rows]
    ).astype(jnp.int32)

    n_first = n_units // 2
    n_extra = n_units // 8
    n_early = n_first + n_extra
    n_late = n_units - n_early

    def chip_sum(away, home, cuts):
        return sum_pieces([home], [swap(a, "group", 1) for a in away], 0, cuts)

    (away,) = cast_units(local, n_units, [(1, 0, n_first, 1)])
    ((home,),) = cast_units(after(local, *away), n_units, [(0, 0, n_first, 1)])
    (begun,) = chip_sum(away, home, [n_first * HD])
    early, crossed = [begun], [swap(begun, "group", 2)]

    n_tokens = row_count * STEPS
    blocks = [(t, 0) for t in token_pieces(place, after(tokens, begun), fsdp_count, rows)]
    source = after(local, begun, *[t for t, _ in blocks])
    n_rest = n_units - n_first
    away, (home,) = cast_units(source, n_units, [(1, n_first, n_rest, N_PIECES), (0, n_first, n_rest, 1)])
    *more, last = chip_sum(away, home, [n * HD for n in (n_extra, n_late) if n])
    early += more
    crossed += [swap(m, "group", 2) for m in more]
    crossed_last = swap(last, "group", 2)

    cosine, sine = rotation_tables(lengths)
    ready = [*early, last]
    attended = cache_attention(after(queries, *ready, cosine, sine), cache_keys, cache_values, lengths, 0, row_count)
    distance = fsdp_count // 2
    step = (attended[1],)
    while distance:
        going = [d for d in range(fsdp_count) if d & distance]
        leaving = [blocks[d] for d in going]
        if distance < fsdp_count // 2:
            leaving = [(after(t, attended[1]), at) for t, at in leaving]
        stacked = stack_blocks(leaving, n_tokens)
        got = swap(stacked, "fsdp", distance)
        for i, d in enumerate(going):
            blocks[d] = (got, i)
        distance //= 2
        step = (attended[1], got)
    toks = [blocks[d] for d in reversed_bits(fsdp_count)]

    state = (weights, moment1, moment2)

    def total(parts, arrived, n_pieces, *earlier):
        arrived = list(lax.optimization_barrier((*arrived, *earlier)))[: len(arrived)]
        one = sum_pieces(parts, arrived, 1, [rows // n_pieces] * n_pieces)
        return one, [swap(p, "group", 1) for p in one]

    both = total(early, crossed, N_PIECES, *step)
    updated, (sent, kept), _ = adam_units(place, both, state, toks, 0, n_early, None, False)
    moving = [(swap(sent, "tp", 1), kept)]
    both = total([last], [crossed_last], 1, sent)
    updated, (sent, kept), held = adam_units(place, both, state, toks, n_early, n_late, updated, True)
    updated = write_held(after(place, sent), held, updated, n_early, n_late)
    moving.append((after(swap(sent, "tp", 1), updated[0]), kept))
    distance = 1
    while distance < fsdp_count:
        for f, (got, kept) in enumerate(moving):
            sent, kept = fold_rows(got, kept, fsdp_count)
            moving[f] = (swap(sent, "fsdp", distance), kept)
        distance *= 2

    n_heads = n_units * HD // HEAD_COLS
    whole_heads = n_heads // 2
    split = whole_heads * HEAD_COLS
    outs = merge(
        [(*moving[0], slice(0, split))], cosine, sine, attended, row_count, 0, whole_heads, None
    )
    parts = [(*moving[0], slice(split, n_early * HD)), (*moving[1], slice(0, n_late * HD))]
    outs = merge(
        parts[0 if split < n_early * HD else 1 :],
        cosine,
        sine,
        attended,
        row_count,
        whole_heads,
        n_heads - whole_heads,
        outs,
    )
    return (*updated, *outs)


def rotate_keys(keys, positions):
    half_width = keys.shape[-1] // 2
    frequency = jnp.power(
        jnp.float32(1000000.0), -2.0 * jnp.arange(half_width, dtype=jnp.float32) / keys.shape[-1]
    )
    angles = positions[..., None] * frequency
    leading = keys[..., :half_width]
    trailing = keys[..., half_width:]
    cosine = jnp.cos(angles)
    sine_part = jnp.sin(angles)
    return jnp.concatenate(
        [leading * cosine - trailing * sine_part, trailing * cosine + leading * sine_part], axis=-1
    )


def plain_shards(
    tokens, queries, cache_keys, cache_values, lengths, weights, moment1, moment2, grad_parts
):
    gradient = lax.psum(grad_parts[0], "group")
    new_weights, new_moment1, new_moment2 = adam_update(weights, moment1, moment2, gradient)
    weight_shard = new_weights.astype(jnp.bfloat16)
    tp_count = lax.axis_size("tp")
    fsdp_count = lax.axis_size("fsdp")
    head_cols = weight_shard.shape[1] // tp_count
    row_count = tokens.shape[0]
    block_rows = weight_shard.shape[0]
    split_tokens = tokens.reshape(row_count, STEPS, fsdp_count, tp_count, block_rows)
    own_columns = lax.dynamic_index_in_dim(split_tokens, lax.axis_index("tp"), 3, keepdims=False)
    arrived = lax.all_to_all(own_columns, "fsdp", split_axis=2, concat_axis=0, tiled=True)
    arrived = arrived.reshape(fsdp_count * row_count * STEPS, block_rows)
    partial_terms = jnp.dot(arrived, weight_shard, preferred_element_type=jnp.float32)
    partial_terms = partial_terms.reshape(fsdp_count, row_count * STEPS, tp_count, head_cols)
    partial_terms = partial_terms.transpose(0, 2, 1, 3).reshape(
        fsdp_count * tp_count * row_count * STEPS, head_cols
    )
    projected = lax.psum_scatter(partial_terms, ("fsdp", "tp"), scatter_dimension=0, tiled=True)
    kv_heads = head_cols // (2 * HD)
    projected = projected.reshape(row_count, STEPS, kv_heads, 2, HD)
    positions = (lengths[:, None] + jnp.arange(STEPS, dtype=jnp.int32)[None, :]).astype(jnp.float32)
    new_keys = rotate_keys(projected[:, :, :, 0], positions[:, :, None])
    fresh = jnp.stack([new_keys, projected[:, :, :, 1]], axis=3).astype(jnp.bfloat16)
    new_kv = fresh.reshape(row_count, STEPS, head_cols)
    span_length = cache_keys.shape[1]
    grouped = queries.reshape(row_count, STEPS, kv_heads, PER_GROUP, HD)
    cached_keys = cache_keys.reshape(row_count, span_length, kv_heads, HD)
    cached_values = cache_values.reshape(row_count, span_length, kv_heads, HD)
    new_scores = (
        jnp.einsum(
            "risgd,rjsd->risgj", grouped, fresh[:, :, :, 0], preferred_element_type=jnp.float32
        )
        * score_scale
    )
    causal = jnp.arange(STEPS)[:, None] >= jnp.arange(STEPS)[None, :]
    new_scores = jnp.where(causal[None, :, None, None, :], new_scores, masked_score)
    scores = (
        jnp.einsum("risgd,rpsd->risgp", grouped, cached_keys, preferred_element_type=jnp.float32)
        * score_scale
    )
    in_range = jnp.arange(span_length, dtype=jnp.int32)[None, :] < lengths[:, None]
    all_scores = jnp.concatenate(
        [jnp.where(in_range[:, None, None, None, :], scores, masked_score), new_scores], axis=-1
    )
    highest = jnp.max(all_scores, axis=-1, keepdims=True)
    exponent = jnp.exp(all_scores - highest)
    probs = (exponent / jnp.sum(exponent, axis=-1, keepdims=True)).astype(jnp.bfloat16)
    context = jnp.einsum(
        "risgp,rpsd->risgd",
        probs[..., :span_length],
        cached_values,
        preferred_element_type=jnp.float32,
    )
    context = context + jnp.einsum(
        "risgj,rjsd->risgd",
        probs[..., span_length:],
        fresh[:, :, :, 1],
        preferred_element_type=jnp.float32,
    )
    context = context.reshape(row_count, STEPS, kv_heads * PER_GROUP * HD).astype(jnp.bfloat16)
    return (new_weights, new_moment1, new_moment2, new_kv, context)


def power_of_two(n):
    return n > 1 and n & (n - 1) == 0


def solution(mesh):
    in_specs = (
        P(("group", "fsdp"), None, None),
        P(("group", "fsdp"), None, "tp"),
        P(("group", "fsdp"), None, "tp"),
        P(("group", "fsdp"), None, "tp"),
        P(("group", "fsdp")),
        P(("fsdp", "tp"), None),
        P(("fsdp", "tp"), None),
        P(("fsdp", "tp"), None),
        P("group", ("fsdp", "tp"), None),
    )
    out_specs = (
        P(("fsdp", "tp"), None),
        P(("fsdp", "tp"), None),
        P(("fsdp", "tp"), None),
        P(("group", "fsdp"), None, "tp"),
        P(("group", "fsdp"), None, "tp"),
    )
    sizes = mesh.shape
    pairwise = sizes["group"] == 4 and power_of_two(sizes["fsdp"]) and sizes["tp"] == 2
    shards = butterfly_shards if pairwise else plain_shards
    return jax.shard_map(shards, mesh=mesh, in_specs=in_specs, out_specs=out_specs, check_vma=False)
```

```python
import functools
import math

import jax
import jax.numpy as jnp
from jax import lax
from jax.experimental import pallas as pl
from jax.experimental.pallas import tpu as pltpu
from jax.sharding import PartitionSpec as P

QH = 40
KVH = 8
HD = 128
STEPS = 4
PER_GROUP = QH // KVH
HEAD_COLS = 2 * HD


beta_one = 0.9
beta_two = 0.95
learning_rate = 0.004
decay_rate = 0.1
epsilon = 1e-08
correct_one = 1.0 - 0.9**10
correct_two = 1.0 - 0.95**10
masked_score = -1e30
score_scale = 1.0 / math.sqrt(HD)

N_PIECES = 2
MIB = 1024 * 1024


def adam_update(weights, moment1, moment2, gradient):
    new_moment1 = beta_one * moment1 + (1.0 - beta_one) * gradient
    new_moment2 = beta_two * moment2 + (1.0 - beta_two) * gradient * gradient
    direction = new_moment1 / correct_one / (jnp.sqrt(new_moment2 / correct_two) + epsilon)
    new_weights = weights - learning_rate * (direction + decay_rate * weights)
    return (new_weights, new_moment1, new_moment2)


def rotation_tables(lengths):
    half_width = HD // 2
    frequency = jnp.power(
        jnp.float32(1000000.0), -2.0 * jnp.arange(half_width, dtype=jnp.float32) / HD
    )
    positions = (lengths[:, None] + jnp.arange(STEPS, dtype=jnp.int32)[None, :]).astype(jnp.float32)
    angles = positions.reshape(-1)[:, None] * frequency
    cosine = jnp.cos(angles)
    sine = jnp.sin(angles)
    return (
        jnp.concatenate([cosine, cosine], axis=-1),
        jnp.concatenate([-sine, sine], axis=-1),
    )


def whole(a):
    return pl.BlockSpec(a.shape, lambda *_: (0,) * len(a.shape))


def after(value, *earlier):
    return lax.optimization_barrier((value, *earlier))[0] if earlier else value


def cost(busy_us):
    return pl.CostEstimate(flops=1, bytes_accessed=max(1, int(busy_us * 2.5e6)), transcendentals=0)


def in_hbm(a):
    return pltpu.with_memory_space_constraint(a, pltpu.HBM)


VMEM = pl.BlockSpec(memory_space=pltpu.VMEM)
ANYWHERE = pl.BlockSpec(memory_space=pl.ANY)


def columns_at(place, part, first, n):
    half = place[0] if part == 0 else 1 - place[0]
    return pl.ds(pl.multiple_of((half * place[2] + first) * HD, HD), n * HD)


def slab_ends(rows):
    if rows % HD:
        return [(0, rows)]
    return [(r, min(r + 2 * HD, rows)) for r in range(0, rows, 2 * HD)]


def held_from(rows):
    return slab_ends(rows)[-2:][0][0]


def cast_kernel(wanted, n_units, source, *refs):
    outs, buffers, sems = refs[: -len(wanted) - 1], refs[-len(wanted) - 1 : -1], refs[-1]
    place = (lax.axis_index("group") % 2, None, n_units)
    ends = slab_ends(source.shape[0])
    copies = [
        [
            pltpu.make_async_copy(
                source.at[r:e, columns_at(place, part, first, n)], buffers[w].at[r:e], sems.at[w, i]
            )
            for i, (r, e) in enumerate(ends)
        ]
        for w, (part, first, n, _) in enumerate(wanted)
    ]
    for copy in sum(copies, []):
        copy.start()
    at = 0
    for w, (_, _, _, n_pieces) in enumerate(wanted):
        if n_pieces == 1:
            for copy, (r, e) in zip(copies[w], ends):
                copy.wait()
                outs[at][r:e] = buffers[w][r:e].astype(jnp.bfloat16)
        else:
            for copy in copies[w]:
                copy.wait()
            step = buffers[w].shape[0] // n_pieces
            for p in range(n_pieces):
                outs[at + p][...] = buffers[w][p * step : (p + 1) * step].astype(jnp.bfloat16)
        at += n_pieces


def cast_units(local, n_units, wanted):
    rows = local.shape[0]
    shapes = [(rows // p, n * HD) for _, _, n, p in wanted for _ in range(p)]
    out = pl.pallas_call(
        functools.partial(cast_kernel, wanted, n_units),
        in_specs=[ANYWHERE],
        out_specs=[VMEM] * len(shapes),
        scratch_shapes=[pltpu.VMEM((rows, n * HD), jnp.float32) for _, _, n, _ in wanted]
        + [pltpu.SemaphoreType.DMA((len(wanted), len(slab_ends(rows))))],
        out_shape=[jax.ShapeDtypeStruct(shape, jnp.bfloat16) for shape in shapes],
        compiler_params=pltpu.CompilerParams(vmem_limit_bytes=6 * MIB),
        cost_estimate=cost(0),
        name="cast_units",
    )(in_hbm(local))
    results = []
    for _, _, _, p in wanted:
        results.append(out[:p])
        out = out[p:]
    return results


def sum_kernel(axis, cuts, n_a, n_b, *refs):
    a, b, outs = refs[:n_a], refs[n_a : n_a + n_b], refs[n_a + n_b :]
    total = join(a, axis).astype(jnp.float32) + join(b, axis).astype(jnp.float32)
    at = 0
    for out, n in zip(outs, cuts):
        piece = total[at : at + n] if axis else total[:, at : at + n]
        out[...] = piece.astype(out.dtype)
        at += n


def sum_pieces(a, b, axis, cuts):
    joined = sum(x.shape[axis] for x in a)
    return pl.pallas_call(
        functools.partial(sum_kernel, axis, cuts, len(a), len(b)),
        in_specs=[VMEM] * (len(a) + len(b)),
        out_specs=[VMEM] * len(cuts),
        out_shape=[jax.ShapeDtypeStruct((n, joined) if axis else (joined, n), jnp.bfloat16) for n in cuts],
        compiler_params=pltpu.CompilerParams(vmem_limit_bytes=6 * MIB),
        cost_estimate=cost(0),
        name="sum_pieces",
    )(*a, *b)


def token_kernel(n, place, source, *outs):
    rows, steps, _ = source.shape
    width = outs[0].shape[1]
    for d in range(n):
        at = pl.ds(pl.multiple_of((place[3] ^ d) * place[4] + place[5], HD), width)
        pieces = [source[r, :, at].astype(jnp.float32) for r in range(rows)]
        outs[d][...] = jnp.concatenate(pieces, axis=0).astype(jnp.bfloat16)


def token_pieces(place, tokens, n, width):
    row_count, steps, _ = tokens.shape
    return pl.pallas_call(
        functools.partial(token_kernel, n),
        grid_spec=pltpu.PrefetchScalarGridSpec(
            num_scalar_prefetch=1, grid=(), in_specs=[VMEM], out_specs=[VMEM] * n
        ),
        out_shape=[jax.ShapeDtypeStruct((row_count * steps, width), jnp.bfloat16)] * n,
        compiler_params=pltpu.CompilerParams(vmem_limit_bytes=4 * MIB),
        cost_estimate=cost(0),
        name="token_pieces",
    )(place, tokens)


def stack_kernel(takes, *refs):
    refs[-1][...] = jnp.concatenate([r[at * n : (at + 1) * n] for r, (at, n) in zip(refs[:-1], takes)], axis=0)


def stack_blocks(blocks, rows):
    arrays = [a for a, _ in blocks]
    return pl.pallas_call(
        functools.partial(stack_kernel, [(at, rows) for _, at in blocks]),
        in_specs=[VMEM] * len(arrays),
        out_specs=VMEM,
        out_shape=jax.ShapeDtypeStruct((rows * len(arrays), arrays[0].shape[1]), arrays[0].dtype),
        compiler_params=pltpu.CompilerParams(vmem_limit_bytes=4 * MIB),
        cost_estimate=cost(0),
        name="stack_blocks",
    )(*arrays)


def join(pieces, axis=0):
    return jnp.concatenate([p[...] for p in pieces], axis=axis)


def adam_kernel(first, n, n_mine, n_partner, tok_places, previous, hold, place, *refs):
    refs = list(refs)
    take = lambda n: [refs.pop(0) for _ in range(n)]
    pieces = take(n_mine + n_partner)
    state = take(3)
    toks = take(len(tok_places))
    take(3 * previous)
    updated = take(3)
    sent, kept = take(2)
    held = take(3 * hold)
    in_sems, out_sems, buffer = refs

    rows = buffer.shape[2]
    slabs = [(part, slice(*ends)) for part in range(2) for ends in slab_ends(rows)]
    columns = [columns_at(place, part, first, n) for part in range(2)]
    incoming = []
    for i, (part, at) in enumerate(slabs):
        incoming.append(
            [
                pltpu.make_async_copy(
                    state[q].at[at, columns[part]], buffer.at[q, part, at], in_sems.at[q, i]
                )
                for q in range(3)
            ]
        )
        for copy in incoming[i]:
            copy.start()
    block = sent.shape[0] // len(toks)
    tok = jnp.concatenate([t[k * block : (k + 1) * block] for t, k in zip(toks, tok_places)], axis=0)
    totals = [join(pieces[:n_mine]), join(pieces[n_mine:])]
    outgoing, products = [], [None, None]
    for i, (part, at) in enumerate(slabs):
        for copy in incoming[i]:
            copy.wait()
        gradient = totals[part][at].astype(jnp.float32)
        results = adam_update(buffer[0, part, at], buffer[1, part, at], buffer[2, part, at], gradient)
        for q in range(3):
            if hold and part == 1 and at.start >= held_from(rows):
                held[q][at.start - held_from(rows) : at.stop - held_from(rows)] = results[q]
                continue
            buffer[q, part, at] = results[q]
            outgoing.append(
                pltpu.make_async_copy(
                    buffer.at[q, part, at], updated[q].at[at, columns[part]], out_sems.at[q, i]
                )
            )
            outgoing[-1].start(priority=1)
        terms = jnp.dot(tok[:, at], results[0].astype(jnp.bfloat16), preferred_element_type=jnp.float32)
        products[part] = terms if products[part] is None else products[part] + terms
    stays = place[0] == place[1]
    kept[...] = jnp.where(stays, products[0], products[1])
    sent[...] = jnp.where(stays, products[1], products[0]).astype(jnp.bfloat16)
    for copy in outgoing:
        copy.wait()


def adam_units(place, total, state, toks, first, n, previous, hold):
    mine, partner = total
    rows, width = state[0].shape
    n_slabs = 2 * len(slab_ends(rows))
    n_tokens = min(t.shape[0] for t, _ in toks) * len(toks)
    operands = [*mine, *partner, *[in_hbm(a) for a in state], *[t for t, _ in toks]]
    in_specs = [VMEM] * (len(mine) + len(partner)) + [ANYWHERE] * 3 + [VMEM] * len(toks)
    aliases = {}
    if previous is not None:
        aliases = {1 + len(operands) + i: i for i in range(3)}
        operands += previous
        in_specs += [ANYWHERE] * 3
    shape = (n_tokens, n * HD)
    out = pl.pallas_call(
        functools.partial(
            adam_kernel, first, n, len(mine), len(partner), [at for _, at in toks], previous is not None, hold
        ),
        grid_spec=pltpu.PrefetchScalarGridSpec(
            num_scalar_prefetch=1,
            grid=(),
            in_specs=in_specs,
            out_specs=[ANYWHERE] * 3 + [VMEM] * (2 + 3 * hold),
            scratch_shapes=[
                pltpu.SemaphoreType.DMA((3, n_slabs)),
                pltpu.SemaphoreType.DMA((3, n_slabs)),
                pltpu.VMEM((3, 2, rows, n * HD), jnp.float32),
            ],
        ),
        out_shape=[jax.ShapeDtypeStruct((rows, width), jnp.float32)] * 3
        + [jax.ShapeDtypeStruct(shape, jnp.bfloat16), jax.ShapeDtypeStruct(shape, jnp.float32)]
        + [jax.ShapeDtypeStruct((rows - held_from(rows), n * HD), jnp.float32)] * (3 * hold),
        input_output_aliases=aliases,
        compiler_params=pltpu.CompilerParams(vmem_limit_bytes=15 * MIB),
        cost_estimate=cost(0),
        name="adam_project",
    )(place, *operands)
    return out[:3], out[3:5], out[5:]


def write_kernel(first, n, place, *refs):
    held, outs, sems = refs[:3], refs[6:9], refs[9]
    copies = [
        pltpu.make_async_copy(
            held[q],
            outs[q].at[outs[q].shape[0] - held[q].shape[0] :, columns_at(place, 1, first, n)],
            sems.at[q],
        )
        for q in range(3)
    ]
    for copy in copies:
        copy.start()
    for copy in copies:
        copy.wait()


def write_held(place, held, previous, first, n):
    return pl.pallas_call(
        functools.partial(write_kernel, first, n),
        grid_spec=pltpu.PrefetchScalarGridSpec(
            num_scalar_prefetch=1,
            grid=(),
            in_specs=[VMEM] * 3 + [ANYWHERE] * 3,
            out_specs=[ANYWHERE] * 3,
            scratch_shapes=[pltpu.SemaphoreType.DMA((3,))],
        ),
        out_shape=[jax.ShapeDtypeStruct(p.shape, p.dtype) for p in previous],
        input_output_aliases={4: 0, 5: 1, 6: 2},
        compiler_params=pltpu.CompilerParams(vmem_limit_bytes=6 * MIB),
        cost_estimate=cost(2),
        name="write_held",
    )(place, *held, *previous)


SLOT = 32


def cache_kernel(heads, first, lens, q, k, v, stacked, acc, stats):
    step = pl.program_id(0)
    rows = q.shape[0]
    span = k.shape[1]
    used = PER_GROUP * STEPS
    for i in range(rows):
        length = lens[first + step * rows + i]
        query = q[i].astype(jnp.float32)
        scores = []
        for h in range(heads):
            pieces = [
                query[:, (h * PER_GROUP + g) * HD : (h * PER_GROUP + g + 1) * HD] for g in range(PER_GROUP)
            ]
            pieces.append(jnp.zeros((SLOT - used, HD), jnp.float32))
            one = jnp.concatenate(pieces, axis=0).astype(jnp.bfloat16)
            stacked[h, i] = one
            scores.append(
                lax.dot_general(
                    one,
                    k[i, :, h * HD : (h + 1) * HD],
                    (((1,), (1,)), ((), ())),
                    preferred_element_type=jnp.float32,
                )
            )
        scores = jnp.concatenate(scores, axis=0) * score_scale
        in_range = lax.broadcasted_iota(jnp.int32, (1, span), 1) < length
        scores = jnp.where(in_range, scores, masked_score)
        highest = jnp.max(scores, axis=-1, keepdims=True)
        weight = jnp.exp(scores - highest)
        total = jnp.sum(weight, axis=-1, keepdims=True)
        weight = weight.astype(jnp.bfloat16)
        lane = lax.broadcasted_iota(jnp.int32, (heads * SLOT, HD), 1)
        stat = jnp.where(lane < HD // 2, highest, total)
        for h in range(heads):
            at = slice(h * SLOT, (h + 1) * SLOT)
            acc[h, i] = jnp.dot(
                weight[at], v[i, :, h * HD : (h + 1) * HD], preferred_element_type=jnp.float32
            )
            stats[h, i] = stat[at]


def cache_attention(queries, cache_keys, cache_values, lengths, first, row_count):
    _, span, kv_cols = cache_keys.shape
    heads = kv_cols // HD
    rows = 2 if row_count % 2 == 0 and first % 2 == 0 else 1
    shape = (heads, row_count, SLOT, HD)
    out_block = pl.BlockSpec((heads, rows, SLOT, HD), lambda r, lens: (0, r, 0, 0))
    in_block = lambda a: pl.BlockSpec((rows, *a.shape[1:]), lambda r, lens: (first // rows + r, 0, 0))
    return pl.pallas_call(
        functools.partial(cache_kernel, heads, first),
        grid_spec=pltpu.PrefetchScalarGridSpec(
            num_scalar_prefetch=1,
            grid=(row_count // rows,),
            in_specs=[in_block(queries), in_block(cache_keys), in_block(cache_values)],
            out_specs=[out_block] * 3,
        ),
        out_shape=[
            jax.ShapeDtypeStruct(shape, jnp.bfloat16),
            jax.ShapeDtypeStruct(shape, jnp.float32),
            jax.ShapeDtypeStruct(shape, jnp.float32),
        ],
        compiler_params=pltpu.CompilerParams(vmem_limit_bytes=10 * MIB),
        cost_estimate=cost(7),
        name="cache_attention",
    )(lengths, in_hbm(queries), in_hbm(cache_keys), in_hbm(cache_values))


def merge_kernel(spans, first, n_heads, *refs):
    folds, refs = refs[: 2 * len(spans)], refs[2 * len(spans) :]
    cosine, sine, stacked, acc, stats = refs[:5]
    new_kv, context = refs[-2:]
    row_count = new_kv.shape[0]
    every = jnp.concatenate(
        [
            folds[2 * f][:, span].astype(jnp.float32) + folds[2 * f + 1][:, span]
            for f, span in enumerate(spans)
        ],
        axis=1,
    )
    at = lax.broadcasted_iota(jnp.int32, (row_count * SLOT, row_count * STEPS), 0)
    to = lax.broadcasted_iota(jnp.int32, (row_count * SLOT, row_count * STEPS), 1)
    seen = (at // SLOT == to // STEPS) & (at % STEPS >= to % STEPS)
    rows_of = lambda a, u: a[first + u].reshape(-1, HD)
    for u in range(n_heads):
        total = every[:, u * HEAD_COLS : (u + 1) * HEAD_COLS]
        keys = total[:, :HD]
        keys = keys * cosine[...] + pltpu.roll(keys, HD // 2, 1) * sine[...]
        keys = keys.astype(jnp.bfloat16)
        values = total[:, HD:].astype(jnp.bfloat16)
        both = jnp.concatenate([keys, values], axis=1).astype(jnp.float32)
        for r in range(row_count):
            new_kv[r, :, u * HEAD_COLS : (u + 1) * HEAD_COLS] = both[
                r * STEPS : (r + 1) * STEPS
            ].astype(jnp.bfloat16)
        scores = (
            lax.dot_general(
                rows_of(stacked, u), keys, (((1,), (1,)), ((), ())), preferred_element_type=jnp.float32
            )
            * score_scale
        )
        scores = jnp.where(seen, scores, masked_score)
        stat = rows_of(stats, u)
        old_highest = stat[:, :1]
        old_total = stat[:, HD // 2 : HD // 2 + 1]
        highest = jnp.maximum(jnp.max(scores, axis=-1, keepdims=True), old_highest)
        weight = jnp.exp(scores - highest)
        scale = jnp.exp(old_highest - highest)
        denominator = jnp.sum(weight, axis=-1, keepdims=True) + scale * old_total
        out = jnp.dot(weight.astype(jnp.bfloat16), values, preferred_element_type=jnp.float32)
        out = (out + scale * rows_of(acc, u)) * (1.0 / denominator)
        for r in range(row_count):
            pieces = [
                out[r * SLOT + g * STEPS : r * SLOT + (g + 1) * STEPS] for g in range(PER_GROUP)
            ]
            at_col = u * PER_GROUP * HD
            context[r, :, at_col : at_col + PER_GROUP * HD] = jnp.concatenate(pieces, axis=1).astype(
                jnp.bfloat16
            )


def merge(folds, cosine, sine, attended, row_count, first, n_heads, previous):
    heads = attended[0].shape[0]
    block = first // n_heads
    operands = [a for fold in folds for a in fold[:2]] + [cosine, sine, *attended]
    in_specs = [VMEM] * len(operands)
    aliases = {}
    if previous is not None:
        aliases = {len(operands) + i: i for i in range(2)}
        operands += previous
        in_specs += [ANYWHERE] * 2
    widths = (HEAD_COLS, PER_GROUP * HD)
    return pl.pallas_call(
        functools.partial(merge_kernel, [fold[2] for fold in folds], first, n_heads),
        grid=(1,),
        in_specs=in_specs,
        out_specs=[pl.BlockSpec((row_count, STEPS, n_heads * w), lambda i: (0, 0, block)) for w in widths],
        out_shape=[jax.ShapeDtypeStruct((row_count, STEPS, heads * w), jnp.bfloat16) for w in widths],
        input_output_aliases=aliases,
        compiler_params=pltpu.CompilerParams(vmem_limit_bytes=8 * MIB),
        cost_estimate=cost(0),
        name="merge_new",
    )(*operands)


def swap(array, axis, bit):
    size = lax.axis_size(axis)
    return lax.ppermute(array, axis, [(i, i ^ bit) for i in range(size)])


def reversed_bits(n):
    order = [0]
    while len(order) < n:
        order = [2 * i for i in order] + [2 * i + 1 for i in order]
    return order


def fold_rows(arrived, kept, n):
    total = arrived.astype(jnp.float32) + kept
    half = total.shape[0] // 2
    return total[half:].astype(jnp.bfloat16), total[:half]


def butterfly_shards(
    tokens, queries, cache_keys, cache_values, lengths, weights, moment1, moment2, grad_parts
):
    fsdp_count = lax.axis_size("fsdp")
    tp_count = lax.axis_size("tp")
    core = lax.axis_index("group") % 2
    fsdp = lax.axis_index("fsdp")
    tp = lax.axis_index("tp")
    rows, width = weights.shape
    row_count = tokens.shape[0]
    n_units = width // (tp_count * HD)
    local = grad_parts[0]
    place = jnp.stack(
        [core, tp, jnp.full_like(core, n_units), fsdp, jnp.full_like(core, tp_count * rows), tp * rows]
    ).astype(jnp.int32)

    n_first = n_units // 2
    n_extra = n_units // 8
    n_early = n_first + n_extra
    n_late = n_units - n_early

    def chip_sum(away, home, cuts):
        return sum_pieces([home], [swap(a, "group", 1) for a in away], 0, cuts)

    (away,) = cast_units(local, n_units, [(1, 0, n_first, 1)])
    ((home,),) = cast_units(after(local, *away), n_units, [(0, 0, n_first, 1)])
    (begun,) = chip_sum(away, home, [n_first * HD])
    early, crossed = [begun], [swap(begun, "group", 2)]

    n_tokens = row_count * STEPS
    blocks = [(t, 0) for t in token_pieces(place, after(tokens, begun), fsdp_count, rows)]
    source = after(local, begun, *[t for t, _ in blocks])
    n_rest = n_units - n_first
    away, (home,) = cast_units(source, n_units, [(1, n_first, n_rest, N_PIECES), (0, n_first, n_rest, 1)])
    *more, last = chip_sum(away, home, [n * HD for n in (n_extra, n_late) if n])
    early += more
    crossed += [swap(m, "group", 2) for m in more]
    crossed_last = swap(last, "group", 2)

    cosine, sine = rotation_tables(lengths)
    ready = [*early, last]
    attended = cache_attention(after(queries, *ready, cosine, sine), cache_keys, cache_values, lengths, 0, row_count)
    distance = fsdp_count // 2
    step = (attended[1],)
    while distance:
        going = [d for d in range(fsdp_count) if d & distance]
        leaving = [blocks[d] for d in going]
        if distance < fsdp_count // 2:
            leaving = [(after(t, attended[1]), at) for t, at in leaving]
        stacked = stack_blocks(leaving, n_tokens)
        got = swap(stacked, "fsdp", distance)
        for i, d in enumerate(going):
            blocks[d] = (got, i)
        distance //= 2
        step = (attended[1], got)
    toks = [blocks[d] for d in reversed_bits(fsdp_count)]

    state = (weights, moment1, moment2)

    def total(parts, arrived, n_pieces, *earlier):
        arrived = list(lax.optimization_barrier((*arrived, *earlier)))[: len(arrived)]
        one = sum_pieces(parts, arrived, 1, [rows // n_pieces] * n_pieces)
        return one, [swap(p, "group", 1) for p in one]

    both = total(early, crossed, N_PIECES, *step)
    updated, (sent, kept), _ = adam_units(place, both, state, toks, 0, n_early, None, False)
    moving = [(swap(sent, "tp", 1), kept)]
    both = total([last], [crossed_last], 1, sent)
    updated, (sent, kept), held = adam_units(place, both, state, toks, n_early, n_late, updated, True)
    updated = write_held(after(place, sent), held, updated, n_early, n_late)
    moving.append((after(swap(sent, "tp", 1), updated[0]), kept))
    distance = 1
    while distance < fsdp_count:
        for f, (got, kept) in enumerate(moving):
            sent, kept = fold_rows(got, kept, fsdp_count)
            moving[f] = (swap(sent, "fsdp", distance), kept)
        distance *= 2

    n_heads = n_units * HD // HEAD_COLS
    whole_heads = n_heads // 2
    split = whole_heads * HEAD_COLS
    outs = merge(
        [(*moving[0], slice(0, split))], cosine, sine, attended, row_count, 0, whole_heads, None
    )
    parts = [(*moving[0], slice(split, n_early * HD)), (*moving[1], slice(0, n_late * HD))]
    outs = merge(
        parts[0 if split < n_early * HD else 1 :],
        cosine,
        sine,
        attended,
        row_count,
        whole_heads,
        n_heads - whole_heads,
        outs,
    )
    return (*updated, *outs)


def rotate_keys(keys, positions):
    half_width = keys.shape[-1] // 2
    frequency = jnp.power(
        jnp.float32(1000000.0), -2.0 * jnp.arange(half_width, dtype=jnp.float32) / keys.shape[-1]
    )
    angles = positions[..., None] * frequency
    leading = keys[..., :half_width]
    trailing = keys[..., half_width:]
    cosine = jnp.cos(angles)
    sine_part = jnp.sin(angles)
    return jnp.concatenate(
        [leading * cosine - trailing * sine_part, trailing * cosine + leading * sine_part], axis=-1
    )


def plain_shards(
    tokens, queries, cache_keys, cache_values, lengths, weights, moment1, moment2, grad_parts
):
    gradient = lax.psum(grad_parts[0], "group")
    new_weights, new_moment1, new_moment2 = adam_update(weights, moment1, moment2, gradient)
    weight_shard = new_weights.astype(jnp.bfloat16)
    tp_count = lax.axis_size("tp")
    fsdp_count = lax.axis_size("fsdp")
    head_cols = weight_shard.shape[1] // tp_count
    row_count = tokens.shape[0]
    block_rows = weight_shard.shape[0]
    split_tokens = tokens.reshape(row_count, STEPS, fsdp_count, tp_count, block_rows)
    own_columns = lax.dynamic_index_in_dim(split_tokens, lax.axis_index("tp"), 3, keepdims=False)
    arrived = lax.all_to_all(own_columns, "fsdp", split_axis=2, concat_axis=0, tiled=True)
    arrived = arrived.reshape(fsdp_count * row_count * STEPS, block_rows)
    partial_terms = jnp.dot(arrived, weight_shard, preferred_element_type=jnp.float32)
    partial_terms = partial_terms.reshape(fsdp_count, row_count * STEPS, tp_count, head_cols)
    partial_terms = partial_terms.transpose(0, 2, 1, 3).reshape(
        fsdp_count * tp_count * row_count * STEPS, head_cols
    )
    projected = lax.psum_scatter(partial_terms, ("fsdp", "tp"), scatter_dimension=0, tiled=True)
    kv_heads = head_cols // (2 * HD)
    projected = projected.reshape(row_count, STEPS, kv_heads, 2, HD)
    positions = (lengths[:, None] + jnp.arange(STEPS, dtype=jnp.int32)[None, :]).astype(jnp.float32)
    new_keys = rotate_keys(projected[:, :, :, 0], positions[:, :, None])
    fresh = jnp.stack([new_keys, projected[:, :, :, 1]], axis=3).astype(jnp.bfloat16)
    new_kv = fresh.reshape(row_count, STEPS, head_cols)
    span_length = cache_keys.shape[1]
    grouped = queries.reshape(row_count, STEPS, kv_heads, PER_GROUP, HD)
    cached_keys = cache_keys.reshape(row_count, span_length, kv_heads, HD)
    cached_values = cache_values.reshape(row_count, span_length, kv_heads, HD)
    new_scores = (
        jnp.einsum(
            "risgd,rjsd->risgj", grouped, fresh[:, :, :, 0], preferred_element_type=jnp.float32
        )
        * score_scale
    )
    causal = jnp.arange(STEPS)[:, None] >= jnp.arange(STEPS)[None, :]
    new_scores = jnp.where(causal[None, :, None, None, :], new_scores, masked_score)
    scores = (
        jnp.einsum("risgd,rpsd->risgp", grouped, cached_keys, preferred_element_type=jnp.float32)
        * score_scale
    )
    in_range = jnp.arange(span_length, dtype=jnp.int32)[None, :] < lengths[:, None]
    all_scores = jnp.concatenate(
        [jnp.where(in_range[:, None, None, None, :], scores, masked_score), new_scores], axis=-1
    )
    highest = jnp.max(all_scores, axis=-1, keepdims=True)
    exponent = jnp.exp(all_scores - highest)
    probs = (exponent / jnp.sum(exponent, axis=-1, keepdims=True)).astype(jnp.bfloat16)
    context = jnp.einsum(
        "risgp,rpsd->risgd",
        probs[..., :span_length],
        cached_values,
        preferred_element_type=jnp.float32,
    )
    context = context + jnp.einsum(
        "risgj,rjsd->risgd",
        probs[..., span_length:],
        fresh[:, :, :, 1],
        preferred_element_type=jnp.float32,
    )
    context = context.reshape(row_count, STEPS, kv_heads * PER_GROUP * HD).astype(jnp.bfloat16)
    return (new_weights, new_moment1, new_moment2, new_kv, context)


def power_of_two(n):
    return n > 1 and n & (n - 1) == 0


def solution(mesh):
    in_specs = (
        P(("group", "fsdp"), None, None),
        P(("group", "fsdp"), None, "tp"),
        P(("group", "fsdp"), None, "tp"),
        P(("group", "fsdp"), None, "tp"),
        P(("group", "fsdp")),
        P(("fsdp", "tp"), None),
        P(("fsdp", "tp"), None),
        P(("fsdp", "tp"), None),
        P("group", ("fsdp", "tp"), None),
    )
    out_specs = (
        P(("fsdp", "tp"), None),
        P(("fsdp", "tp"), None),
        P(("fsdp", "tp"), None),
        P(("group", "fsdp"), None, "tp"),
        P(("group", "fsdp"), None, "tp"),
    )
    sizes = mesh.shape
    pairwise = sizes["group"] == 4 and power_of_two(sizes["fsdp"]) and sizes["tp"] == 2
    shards = butterfly_shards if pairwise else plain_shards
    return jax.shard_map(shards, mesh=mesh, in_specs=in_specs, out_specs=out_specs, check_vma=False)
```
